32 devices in a mesh: dp: 8 (over y, x, core), mp: 4 (over z).
Axes of the slice: x: 2, y: 2, z: 4, core: 2. Of those that a mesh axis runs over, the one named last changes fastest.
Arguments:
- patches: bfloat16 [32, 128, 1536], P(('dp', 'mp')), may hold values from -6 to 6
- keep_index: int32 [32, 128], P(('dp', 'mp')), may hold values from 0 to 127, each once within a row
- visible: int32 [32], P(('dp', 'mp')), may hold values from 16 to 80, as said below
- targets: bfloat16 [32, 12288], P(('dp', 'mp')), may hold values from -6 to 6
- w_up: bfloat16 [1536, 6144], P(None, 'mp'), may hold values from -0.15625 to 0.15625
- w_down: bfloat16 [6144, 1536], P('mp'), may hold values from -0.078125 to 0.078125
- dec_embed: bfloat16 [1536, 512], P('mp'), may hold values from -0.15625 to 0.15625
- dec_qkv: bfloat16 [512, 1536], P('mp'), may hold values from -1.45840774 to 1.45840774
- dec_out: bfloat16 [512, 512], P('mp'), may hold values from -0.25 to 0.25
- dec_pred: bfloat16 [512, 96], P('mp'), may hold values from -0.25 to 0.25
- mask_token: bfloat16 [512], replicated, may hold values from -4 to 4
- position: bfloat16 [128, 512], replicated, may hold values from -4.5 to 4.5
Outputs:
- recon: bfloat16 [32, 12288], P(('dp', 'mp'))
- patch_loss: float32 [32, 128], P(('dp', 'mp'))
The draws below stay inside these ranges and needn't reach their ends.
Inputs may be any that keep to these rules, and one draw needn't show every extreme that they name: For c < 16, visible[c] + visible[c + 16] = 96; some crop has exactly 80 visible patches.
All inputs are finite; a program needn't handle non-finite values.
Results may differ from the reference program's by a relative error of at most 0.04.
Values may be sent and summed in bfloat16 or wider, within the bound.
No kernel may reach another device: no remote copies, remote signals or barrier semaphores. Data moves between devices by JAX's collectives and lax.ppermute only.
A program may use at most 64 MiB of HBM per device.

```python
import math
import jax
import jax.numpy as jnp
from jax import lax

D = 1536
FF = 6144
DD = 512
HSIZE = 64
P_SIZE = 128
PIX = 96
VMAX = 80
VMEAN = 48
CROPS = 32
N_MP = 4


def draw_visible(key, part):
    half = CROPS // 2
    first = jax.random.randint(key, (half,), 2 * VMEAN - VMAX, VMAX + 1, dtype=jnp.int32)
    first = first.at[0].set(VMAX)
    return jnp.concatenate([first, 2 * VMEAN - first]).astype(jnp.int32)


def draw_dec_qkv(key, part):
    limit = 32.0 / math.sqrt(DD)
    base = jnp.clip(jax.random.normal(key, (DD, 3 * DD), jnp.float32), -4.0, 4.0) * (1.0 / math.sqrt(DD))
    return jnp.clip(base, -limit, limit).astype(jnp.bfloat16)


def draw_position(key, part):
    base = jnp.clip(jax.random.normal(key, (P_SIZE, DD), jnp.float32), -4.0, 4.0)
    return base.astype(jnp.bfloat16)


def shard_levels(own_key, shape, split, smallest, largest):
    factor_of = 1.0
    for dim, blocks in split:
        draws = jax.random.uniform(jax.random.fold_in(jax.random.fold_in(own_key, 6), dim), (blocks,), jnp.float32, smallest / len(split), largest / len(split))
        factor_of = factor_of * jnp.repeat(jnp.exp(draws), shape[dim] // blocks).reshape((-1,) + (1,) * (len(shape) - 1 - dim))
    return factor_of


def bell_draw(stream_key, dims, scale, reach, pieces=(), kind=jnp.bfloat16):
    gain = shard_levels(stream_key, dims, pieces, -0.22, 0.18) if pieces else 1.0
    entries = jax.random.normal(stream_key, dims, jnp.float32) * scale * gain
    return jnp.minimum(jnp.maximum(entries, -reach), reach).astype(kind)


def setup_inputs(seed: int = 0) -> dict:
    key_of = jax.random.split(jax.random.key(seed), 13)
    patches = bell_draw(key_of[0], (CROPS, P_SIZE, D), 1.0, 6.0, ((0, 32),))
    keep_index = jax.vmap(lambda own: jax.random.permutation(own, P_SIZE))(jax.random.split(key_of[1], CROPS)).reshape((CROPS, P_SIZE)).astype(jnp.int32)
    visible = draw_visible(jax.random.fold_in(key_of[12], 71), 0)
    targets = bell_draw(key_of[3], (CROPS, P_SIZE * PIX), 1.0, 6.0, ((0, 32),))
    w_up = bell_draw(key_of[4], (D, FF), D ** -0.5, 0.15625, ((1, 4),))
    w_down = bell_draw(key_of[5], (FF, D), FF ** -0.5, 0.078125, ((0, 4),))
    dec_embed = bell_draw(key_of[6], (D, DD), D ** -0.5, 0.15625, ((0, 4),))
    dec_qkv = draw_dec_qkv(jax.random.fold_in(key_of[12], 71), 0)
    dec_out = bell_draw(key_of[8], (DD, DD), DD ** -0.5, 0.25, ((0, 4),))
    dec_pred = bell_draw(key_of[9], (DD, PIX), DD ** -0.5, 0.25, ((0, 4),))
    mask_token = bell_draw(key_of[10], (DD,), 1.0, 4.0)
    position = draw_position(jax.random.fold_in(key_of[12], 71), 0)
    return {"patches": patches, "keep_index": keep_index, "visible": visible, "targets": targets, "w_up": w_up, "w_down": w_down, "dec_embed": dec_embed, "dec_qkv": dec_qkv, "dec_out": dec_out, "dec_pred": dec_pred, "mask_token": mask_token, "position": position}


EPSILON = 1e-06

def layer_norm(values):
    center = values - lax.optimization_barrier(jnp.mean(values, axis=-1, keepdims=True))
    spread = lax.optimization_barrier(jnp.mean(center * center, axis=-1, keepdims=True))
    return center * lax.rsqrt(spread + EPSILON)

def multiply(left, right):
    return jnp.dot(left.astype(jnp.float32), right.astype(jnp.float32), precision=lax.Precision.HIGHEST)

def reference(patches, keep_index, visible, targets, w_up, w_down, dec_embed, dec_qkv, dec_out, dec_pred, mask_token, position):
    share = FF // N_MP
    heads = DD // HSIZE
    scale = 1.0 / math.sqrt(HSIZE)

    def one_crop(item):
        patch_rows, keep, count, target = item
        row_block = jnp.take(patch_rows, keep[:VMAX], axis=0)
        normed = layer_norm(row_block.astype(jnp.float32)).astype(jnp.bfloat16)
        hidden = jax.nn.gelu(multiply(normed, w_up), approximate=True).astype(jnp.bfloat16)
        summed = jnp.zeros((VMAX, D), jnp.float32)
        for shard in range(N_MP):
            partial_term = multiply(hidden[:, shard * share:(shard + 1) * share], w_down[shard * share:(shard + 1) * share]).astype(jnp.bfloat16)
            summed = summed + lax.optimization_barrier(partial_term).astype(jnp.float32)
        encoded = (row_block.astype(jnp.float32) + summed).astype(jnp.bfloat16)
        embedded = multiply(encoded, dec_embed).astype(jnp.bfloat16)
        slots = jnp.arange(P_SIZE, dtype=jnp.int32)
        inverse = jnp.zeros((P_SIZE,), jnp.int32).at[keep].set(slots)
        seen = inverse < count
        picked = jnp.take(embedded, jnp.minimum(inverse, VMAX - 1), axis=0).astype(jnp.float32)
        start = jnp.where(seen[:, None], picked, mask_token.astype(jnp.float32)[None, :]) + position.astype(jnp.float32)
        dec_normed = layer_norm(start).astype(jnp.bfloat16)
        projections = multiply(dec_normed, dec_qkv).astype(jnp.bfloat16)
        query = projections[:, :DD].reshape(P_SIZE, heads, HSIZE).astype(jnp.float32)
        keys = projections[:, DD:2 * DD].reshape(P_SIZE, heads, HSIZE).astype(jnp.float32)
        values = projections[:, 2 * DD:].reshape(P_SIZE, heads, HSIZE).astype(jnp.float32)
        scores = jnp.einsum('qhe,khe->hqk', query, keys, precision=lax.Precision.HIGHEST) * scale
        scores = scores - lax.optimization_barrier(jnp.max(scores, axis=-1, keepdims=True))
        weights = jnp.exp(scores)
        probs = (weights / lax.optimization_barrier(jnp.sum(weights, axis=-1, keepdims=True))).astype(jnp.bfloat16)
        mixed = jnp.einsum('hqk,khe->qhe', probs.astype(jnp.float32), values, precision=lax.Precision.HIGHEST)
        mixed = mixed.astype(jnp.bfloat16).reshape(P_SIZE, DD)
        after = start + multiply(mixed, dec_out)
        final = layer_norm(after).astype(jnp.bfloat16)
        prediction = multiply(final, dec_pred)
        error = prediction - target.reshape(P_SIZE, PIX).astype(jnp.float32)
        loss = jnp.where(seen, jnp.zeros((P_SIZE,), jnp.float32), lax.optimization_barrier(jnp.mean(error * error, axis=-1)))
        return (prediction.astype(jnp.bfloat16).reshape(P_SIZE * PIX), loss)
    recon, patch_loss = lax.map(one_crop, (patches, keep_index, visible, targets))
    return (recon, patch_loss)
```

```python
import functools
import math

import jax
import jax.numpy as jnp
from jax import lax
from jax.experimental import pallas as pl
from jax.experimental.pallas import tpu as pltpu
from jax.sharding import PartitionSpec as P

DD = 512
HSIZE = 64
PIX = 96
VMAX = 80
LANES = 128
EPSILON = 1e-06
MIB = 1 << 20

f32 = jnp.float32
bf16 = jnp.bfloat16
VMEM = pl.BlockSpec(memory_space=pltpu.VMEM)
SMEM = pl.BlockSpec(memory_space=pltpu.SMEM)


def dot(left, right):
    return jnp.dot(left, right, preferred_element_type=f32)


def layer_norm(values):
    center = values - jnp.mean(values, axis=-1, keepdims=True)
    spread = jnp.mean(center * center, axis=-1, keepdims=True)
    return center * lax.rsqrt(spread + EPSILON)


def cost(flops, size, transcendentals=0):
    return pl.CostEstimate(flops=flops, bytes_accessed=size, transcendentals=transcendentals)


def xor_permute(values, axis, size, bit):
    return lax.ppermute(values, axis, [(i, i ^ bit) for i in range(size)])


def rows_kernel(keep_ref, patches_ref, rows_ref, normed_ref):
    patch_count = patches_ref.shape[1]
    patch = lax.broadcasted_iota(jnp.int32, (patch_count, patch_count), 0)
    chosen = (keep_ref[...] == patch).astype(f32).astype(bf16)[:, :VMAX]
    rows = lax.dot_general(
        chosen, patches_ref[0], (((0,), (0,)), ((), ())), preferred_element_type=f32
    )
    rows_ref[...] = rows.astype(bf16)
    normed_ref[...] = layer_norm(rows).astype(bf16)


def select_rows(keep_index, patches):
    _, patch_count, width = patches.shape
    out = jax.ShapeDtypeStruct((VMAX, width), bf16)
    return pl.pallas_call(
        rows_kernel,
        out_shape=(out, out),
        in_specs=[VMEM, VMEM],
        out_specs=(VMEM, VMEM),
        cost_estimate=cost(2 * VMAX * patch_count * width, 2 * width * (patch_count + 2 * VMAX)),
        name="select_rows",
    )(keep_index, patches)


def place_pieces(store, own_rows, mp, plane, piece):
    m = lax.axis_index("mp")
    j = lax.axis_index("dp")
    store(pl.multiple_of(m * own_rows, 16), own_rows, 0, 0)
    count = 0
    for source, near in enumerate(plane, 1):
        for k in range(1, mp):
            row = (m ^ k) * own_rows + (j ^ near) * piece
            store(pl.multiple_of(row, 16), piece, source, (k - 1) * piece)
            count += 1


def gather_pieces(part, dp, mp):
    across = jnp.concatenate([xor_permute(part, "mp", mp, k) for k in range(1, mp)], axis=0)
    near = [across] + [xor_permute(across, "dp", dp, bit) for bit in (2, 4, 6)]
    far = xor_permute(jnp.concatenate(near, axis=0), "dp", dp, 1)
    return near + [far]


PLANE = (0, 2, 4, 6)


def assemble(refs, own_refs, mp, piece, write):
    near_refs, far_ref = refs[:4], refs[4]
    m = lax.axis_index("mp")
    j = lax.axis_index("dp")
    own_rows = own_refs[0].shape[0]
    write(pl.multiple_of(m * own_rows, 16), own_rows, None, 0)
    block = (mp - 1) * piece
    for place, near in enumerate(PLANE):
        for core in (0, 1):
            source = far_ref if core else near_refs[place]
            base = place * block if core else 0
            for k in range(1, mp):
                row = (m ^ k) * own_rows + (j ^ near ^ core) * piece
                write(pl.multiple_of(row, 16), piece, source, base + (k - 1) * piece)


def fuse_kernel(mp, piece, rows_ref, down_ref, own_ref, *rest):
    refs, (fused_ref, residual_ref, embed) = rest[:-3], rest[-3:]

    @pl.when(pl.program_id(0) == 0)
    def _():
        def write(row, count, source, base):
            if source is None:
                embed[pl.ds(row, count), :] = own_ref[...]
            else:
                embed[pl.ds(row, count), :] = source[base : base + count, :]

        if refs:
            assemble(refs, [own_ref], mp, piece, write)
        else:
            embed[...] = own_ref[...]
        residual_ref[...] = dot(rows_ref[...], embed[...])

    fused_ref[...] = dot(down_ref[...], embed[...]).astype(bf16)


def fuse_weights(rows, w_down, own, pieces, mp, piece):
    hidden, width = w_down.shape
    columns = own.shape[1]
    tile = 256 if hidden % 256 == 0 else hidden
    whole = lambda a: pl.BlockSpec(a.shape, lambda i: (0, 0))
    return pl.pallas_call(
        functools.partial(fuse_kernel, mp, piece),
        grid=(hidden // tile,),
        out_shape=(
            jax.ShapeDtypeStruct((hidden, columns), bf16),
            jax.ShapeDtypeStruct((VMAX, columns), f32),
        ),
        in_specs=[whole(rows), pl.BlockSpec((tile, width), lambda i: (i, 0)), whole(own)]
        + [whole(p) for p in pieces],
        out_specs=(
            pl.BlockSpec((tile, columns), lambda i: (i, 0)),
            pl.BlockSpec((VMAX, columns), lambda i: (0, 0)),
        ),
        scratch_shapes=[pltpu.VMEM((width, columns), bf16)],
        compiler_params=pltpu.CompilerParams(vmem_limit_bytes=24 * MIB),
        cost_estimate=cost(2 * hidden * width * columns, 2 * hidden * (width + columns)),
        name="fuse_weights",
    )(rows, w_down, own, *pieces)


def decoder_weights_kernel(mp, piece, qkv_ref, out_ref, pred_ref, *rest):
    refs, (full_qkv, full_out, full_pred) = rest[:-3], rest[-3:]
    wide = full_qkv.shape[1]

    def write(row, count, source, base):
        place = pl.ds(row, count)
        if source is None:
            full_qkv[place, :] = qkv_ref[...]
            full_out[place, :] = out_ref[...]
            full_pred[place, :PIX] = pred_ref[...]
        else:
            part = pl.ds(base, count)
            full_qkv[place, :] = source[part, :wide]
            full_out[place, :] = source[part, wide : wide + DD]
            full_pred[place, :PIX] = source[part, wide + DD : wide + DD + PIX]

    assemble(refs, [qkv_ref], mp, piece, write)


def decoder_weights(own, pieces, mp, piece):
    shapes = [(mp * w.shape[0], w.shape[1]) for w in own]
    return pl.pallas_call(
        functools.partial(decoder_weights_kernel, mp, piece),
        out_shape=[jax.ShapeDtypeStruct(s, bf16) for s in shapes],
        in_specs=[VMEM] * (3 + len(pieces)),
        out_specs=[VMEM] * 3,
        compiler_params=pltpu.CompilerParams(vmem_limit_bytes=24 * MIB),
        cost_estimate=cost(0, 2 * 2 * sum(a * b for a, b in shapes)),
        name="decoder_weights",
    )(*own, *pieces)


def encode_kernel(count, up_ref, fused_ref, *rest):
    normed, outs, acc = rest[:count], rest[count : 2 * count], rest[2 * count]
    step = pl.program_id(0)
    rows = jnp.concatenate([r[...] for r in normed], axis=0)
    hidden = jax.nn.gelu(dot(rows, up_ref[...]), approximate=True).astype(bf16)
    term = dot(hidden, fused_ref[...])

    @pl.when(step == 0)
    def _():
        acc[...] = term

    @pl.when(step > 0)
    def _():
        acc[...] += term

    @pl.when(step == pl.num_programs(0) - 1)
    def _():
        for i, out in enumerate(outs):
            out[...] = acc[i * VMAX : (i + 1) * VMAX, :].astype(bf16)


def encode(normed, w_up, fused):
    width, hidden = w_up.shape
    columns = fused.shape[1]
    count = len(normed)
    tile = 256 if hidden % 256 == 0 else hidden
    return pl.pallas_call(
        functools.partial(encode_kernel, count),
        grid=(hidden // tile,),
        out_shape=[jax.ShapeDtypeStruct((VMAX, columns), bf16)] * count,
        in_specs=[
            pl.BlockSpec((width, tile), lambda i: (0, i)),
            pl.BlockSpec((tile, columns), lambda i: (i, 0)),
        ]
        + [pl.BlockSpec((VMAX, width), lambda i: (0, 0))] * count,
        out_specs=[pl.BlockSpec((VMAX, columns), lambda i: (0, 0))] * count,
        scratch_shapes=[pltpu.VMEM((count * VMAX, columns), f32)],
        compiler_params=pltpu.CompilerParams(vmem_limit_bytes=32 * MIB),
        cost_estimate=cost(
            2 * count * VMAX * hidden * (width + columns),
            2 * hidden * (width + columns),
            count * VMAX * hidden,
        ),
        name="encode",
    )(w_up, fused, *normed)


def decode_kernel(
    visible_ref,
    keep_ref,
    targets_ref,
    mask_ref,
    position_ref,
    qkv_ref,
    out_ref,
    pred_ref,
    residual_ref,
    *rest,
):
    parts, (recon_ref, loss_ref, flat, errors) = rest[:-4], rest[-4:]
    patch_count = position_ref.shape[0]
    patch = lax.broadcasted_iota(jnp.int32, (patch_count, patch_count), 0)
    slot = lax.broadcasted_iota(jnp.int32, (patch_count, patch_count), 1)
    chosen = ((keep_ref[...] == patch) & (slot < visible_ref[0])).astype(f32)
    seen = jnp.max(chosen, axis=1, keepdims=True)
    embedded = residual_ref[...]
    for part in parts:
        embedded += part[...].astype(f32)
    picked = dot(chosen.astype(bf16)[:, :VMAX], embedded.astype(bf16))
    start = jnp.where(seen > 0, picked, mask_ref[...].astype(f32)) + position_ref[...].astype(f32)
    projections = dot(layer_norm(start).astype(bf16), qkv_ref[...]).astype(bf16)
    scale = 1.0 / math.sqrt(HSIZE)
    mixed = []
    for head in range(DD // HSIZE):
        columns = slice(head * HSIZE, (head + 1) * HSIZE)
        query = projections[:, :DD][:, columns]
        key = projections[:, DD : 2 * DD][:, columns]
        value = projections[:, 2 * DD :][:, columns]
        scores = lax.dot_general(
            query, key, (((1,), (1,)), ((), ())), preferred_element_type=f32
        ) * scale
        weights = jnp.exp(scores - jnp.max(scores, axis=-1, keepdims=True))
        probs = (weights / jnp.sum(weights, axis=-1, keepdims=True)).astype(bf16)
        mixed.append(dot(probs, value).astype(bf16))
    after = start + dot(jnp.concatenate(mixed, axis=1), out_ref[...])
    prediction = dot(layer_norm(after).astype(bf16), pred_ref[...])
    group = 4
    wide = group * PIX
    flat[:, :PIX] = prediction[:, :PIX]
    lines = patch_count // group
    together = jnp.concatenate(
        [flat[pl.ds(i, lines, stride=group), :][:, :PIX] for i in range(group)], axis=1
    )
    for line in range(lines):
        place = slice(line * wide, (line + 1) * wide)
        recon_ref[:, place] = together[line : line + 1, :].astype(bf16)
        errors[line : line + 1, :] = together[line : line + 1, :] - targets_ref[:, place].astype(f32)
    squares = errors[...] * errors[...]
    for i in range(group):
        flat[pl.ds(i, lines, stride=group), :PIX] = squares[:, i * PIX : (i + 1) * PIX]
    loss = jnp.sum(flat[:, :PIX], axis=1, keepdims=True) * (1.0 / PIX)
    loss = jnp.where(seen > 0, 0.0, loss)
    loss_ref[...] = jnp.sum(jnp.where(patch == slot, loss, 0.0), axis=0, keepdims=True)


def decode(visible, keep_index, targets, mask_token, position, weights, residual, parts):
    patch_count = position.shape[0]
    rest = (keep_index, targets, mask_token[None], position, *weights, residual, *parts)
    return pl.pallas_call(
        decode_kernel,
        out_shape=(
            jax.ShapeDtypeStruct(targets.shape, bf16),
            jax.ShapeDtypeStruct((1, patch_count), f32),
        ),
        in_specs=[SMEM] + [VMEM] * len(rest),
        out_specs=(VMEM, VMEM),
        scratch_shapes=[
            pltpu.VMEM((patch_count, LANES), f32),
            pltpu.VMEM((patch_count // 4, 4 * PIX), f32),
        ],
        compiler_params=pltpu.CompilerParams(vmem_limit_bytes=24 * MIB),
        cost_estimate=cost(2 * patch_count * DD * (5 * DD), 2 * 6 * DD * DD, 8 * patch_count**2),
        name="decode",
    )(visible, *rest)


def body(
    dp,
    mp,
    patches,
    keep_index,
    visible,
    targets,
    w_up,
    w_down,
    dec_embed,
    dec_qkv,
    dec_out,
    dec_pred,
    mask_token,
    position,
):
    embed_piece = dec_embed.shape[0] // dp
    piece = dec_qkv.shape[0] // dp
    in_pieces = dp == 8 and embed_piece % 16 == 0 and piece % 16 == 0
    j = lax.axis_index("dp")
    if in_pieces:
        cut = lambda a, n: lax.dynamic_slice_in_dim(a, j * n, n, 0)
        own_embed = dec_embed
        embed_pieces = gather_pieces(cut(dec_embed, embed_piece), dp, mp)
    else:
        own_embed = lax.all_gather(dec_embed, "mp", axis=0, tiled=True)
        embed_pieces = []
    rows, normed = select_rows(keep_index, patches)
    others = [xor_permute(normed, "mp", mp, k) for k in range(mp - 1, 0, -1)]
    if in_pieces:
        pad = jnp.zeros((piece, LANES - PIX), bf16)
        part = jnp.concatenate([cut(dec_qkv, piece), cut(dec_out, piece), cut(dec_pred, piece), pad], 1)
        pieces = gather_pieces(part, dp, mp)
        weights = decoder_weights((dec_qkv, dec_out, dec_pred), pieces, mp, piece)
    else:
        weights = [lax.all_gather(w, "mp", axis=0, tiled=True) for w in (dec_qkv, dec_out, dec_pred)]
    fused, residual = fuse_weights(rows, w_down, own_embed, embed_pieces, mp, embed_piece)
    sums = encode([normed] + others, w_up, fused)
    parts = [sums[0]] + [
        xor_permute(s, "mp", mp, k) for k, s in zip(range(mp - 1, 0, -1), sums[1:])
    ]
    return decode(visible, keep_index, targets, mask_token, position, weights, residual, parts)


def solution(mesh):
    return jax.shard_map(
        functools.partial(body, mesh.shape["dp"], mesh.shape["mp"]),
        mesh=mesh,
        in_specs=(
            P(("dp", "mp"), None, None),
            P(("dp", "mp"), None),
            P(("dp", "mp")),
            P(("dp", "mp"), None),
            P(None, "mp"),
            P("mp", None),
            P("mp", None),
            P("mp", None),
            P("mp", None),
            P("mp", None),
            P(),
            P(),
        ),
        out_specs=(P(("dp", "mp"), None), P(("dp", "mp"), None)),
        check_vma=False,
    )
```

```python
import functools
import math

import jax
import jax.numpy as jnp
from jax import lax
from jax.experimental import pallas as pl
from jax.experimental.pallas import tpu as pltpu
from jax.sharding import PartitionSpec as P

DD = 512
HSIZE = 64
PIX = 96
VMAX = 80
SHARE = 48
SMALLEST = 2 * SHARE - VMAX
LANES = 128
EPSILON = 1e-06
MIB = 1 << 20

f32 = jnp.float32
bf16 = jnp.bfloat16
VMEM = pl.BlockSpec(memory_space=pltpu.VMEM)
SMEM = pl.BlockSpec(memory_space=pltpu.SMEM)


def dot(left, right):
    return jnp.dot(left, right, preferred_element_type=f32)


def layer_norm(values):
    center = values - jnp.mean(values, axis=-1, keepdims=True)
    spread = jnp.mean(center * center, axis=-1, keepdims=True)
    return center * lax.rsqrt(spread + EPSILON)


def cost(flops, size, transcendentals=0):
    return pl.CostEstimate(flops=flops, bytes_accessed=size, transcendentals=transcendentals)


def xor_permute(values, axis, size, bit):
    return lax.ppermute(values, axis, [(i, i ^ bit) for i in range(size)])


def first_kernel(keep_ref, patches_ref, embed_ref, qkv_ref, out_ref, pred_ref, tail_ref, embed_part_ref, part_ref):
    patch_count = patches_ref.shape[1]
    patch = lax.broadcasted_iota(jnp.int32, (patch_count, patch_count), 0)
    chosen = (keep_ref[...] == patch).astype(f32).astype(bf16)[:, SHARE:VMAX]
    tail_ref[...] = pick(chosen, patches_ref[0]).astype(bf16)
    if embed_ref is None:
        return
    j = lax.axis_index("dp")
    cut = lambda ref, n: ref[pl.ds(pl.multiple_of(j * n, 16), n), :]
    embed_part_ref[...] = cut(embed_ref, embed_part_ref.shape[0])
    count, wide = part_ref.shape[0], qkv_ref.shape[1]
    part_ref[:, :wide] = cut(qkv_ref, count)
    part_ref[:, wide : wide + DD] = cut(out_ref, count)
    part_ref[:, wide + DD :] = jnp.zeros((count, LANES), bf16)
    part_ref[:, wide + DD : wide + DD + PIX] = cut(pred_ref, count)


def pick(chosen, values):
    return lax.dot_general(chosen, values, (((0,), (0,)), ((), ())), preferred_element_type=f32)


def first_parts(keep_index, patches, weights, dp):
    _, patch_count, width = patches.shape
    shapes = [(VMAX - SHARE, width)]
    kernel = first_kernel
    if weights:
        embed, qkv, out, pred = weights
        shapes.append((embed.shape[0] // dp, embed.shape[1]))
        shapes.append((qkv.shape[0] // dp, qkv.shape[1] + DD + LANES))
    else:
        kernel = lambda keep, patches, tail: first_kernel(keep, patches, *[None] * 4, tail, None, None)
    return pl.pallas_call(
        kernel,
        out_shape=[jax.ShapeDtypeStruct(shape, bf16) for shape in shapes],
        in_specs=[VMEM] * (2 + len(weights)),
        out_specs=[VMEM] * len(shapes),
        cost_estimate=cost(2 * patch_count * width * 32, 2 * width * patch_count),
        name="first_parts",
    )(keep_index, patches, *weights)


def rows_kernel(visible_ref, keep_ref, patches_ref, tail_ref, rows_ref, normed_ref):
    patch_count = patches_ref.shape[1]
    visible = visible_ref[0]
    square = (patch_count, patch_count)
    patch = lax.broadcasted_iota(jnp.int32, square, 0)
    slot = lax.broadcasted_iota(jnp.int32, square, 1)
    own = ((keep_ref[...] == patch) & (slot < visible)).astype(f32).astype(bf16)[:, :SHARE]
    other = (slot - visible == patch).astype(f32).astype(bf16)[: VMAX - SHARE, :SHARE]
    rows = pick(own, patches_ref[0]) + pick(other, tail_ref[...])
    rows_ref[...] = rows.astype(bf16)
    normed_ref[...] = layer_norm(rows).astype(bf16)


def select_rows(visible, keep_index, patches, tail):
    _, patch_count, width = patches.shape
    out = jax.ShapeDtypeStruct((SHARE, width), bf16)
    return pl.pallas_call(
        rows_kernel,
        out_shape=(out, out),
        in_specs=[SMEM, VMEM, VMEM, VMEM],
        out_specs=(VMEM, VMEM),
        cost_estimate=cost(2 * VMAX * patch_count * width, 2 * width * (patch_count + 2 * VMAX)),
        name="select_rows",
    )(visible, keep_index, patches, tail)


def gather_pieces(part, dp, mp):
    across = jnp.concatenate([xor_permute(part, "mp", mp, k) for k in range(1, mp)], axis=0)
    near = [across] + [xor_permute(across, "dp", dp, bit) for bit in (2, 4, 6)]
    far = xor_permute(jnp.concatenate(near, axis=0), "dp", dp, 1)
    return near + [far]


PLANE = (0, 2, 4, 6)


def assemble(refs, own_refs, mp, piece, write):
    near_refs, far_ref = refs[:4], refs[4]
    m = lax.axis_index("mp")
    j = lax.axis_index("dp")
    own_rows = own_refs[0].shape[0]
    write(pl.multiple_of(m * own_rows, 16), own_rows, None, 0)
    block = (mp - 1) * piece
    for place, near in enumerate(PLANE):
        for core in (0, 1):
            source = far_ref if core else near_refs[place]
            base = place * block if core else 0
            for k in range(1, mp):
                row = (m ^ k) * own_rows + (j ^ near ^ core) * piece
                write(pl.multiple_of(row, 16), piece, source, base + (k - 1) * piece)


def fuse_kernel(mp, piece, rows_ref, down_ref, own_ref, *rest):
    refs, (fused_ref, residual_ref, embed) = rest[:-3], rest[-3:]

    @pl.when(pl.program_id(0) == 0)
    def _():
        def write(row, count, source, base):
            if source is None:
                embed[pl.ds(row, count), :] = own_ref[...]
            else:
                embed[pl.ds(row, count), :] = source[base : base + count, :]

        if refs:
            assemble(refs, [own_ref], mp, piece, write)
        else:
            embed[...] = own_ref[...]
        residual_ref[...] = dot(rows_ref[...], embed[...])

    fused_ref[...] = dot(down_ref[...], embed[...]).astype(bf16)


def fuse_weights(rows, w_down, own, pieces, mp, piece):
    hidden, width = w_down.shape
    columns = own.shape[1]
    tile = 256 if hidden % 256 == 0 else hidden
    whole = lambda a: pl.BlockSpec(a.shape, lambda i: (0, 0))
    return pl.pallas_call(
        functools.partial(fuse_kernel, mp, piece),
        grid=(hidden // tile,),
        out_shape=(
            jax.ShapeDtypeStruct((hidden, columns), bf16),
            jax.ShapeDtypeStruct((SHARE, columns), f32),
        ),
        in_specs=[whole(rows), pl.BlockSpec((tile, width), lambda i: (i, 0)), whole(own)]
        + [whole(p) for p in pieces],
        out_specs=(
            pl.BlockSpec((tile, columns), lambda i: (i, 0)),
            pl.BlockSpec((SHARE, columns), lambda i: (0, 0)),
        ),
        scratch_shapes=[pltpu.VMEM((width, columns), bf16)],
        compiler_params=pltpu.CompilerParams(vmem_limit_bytes=24 * MIB),
        cost_estimate=cost(2 * hidden * width * columns, 2 * hidden * (width + columns)),
        name="fuse_weights",
    )(rows, w_down, own, *pieces)


def decoder_weights_kernel(mp, piece, qkv_ref, out_ref, pred_ref, *rest):
    refs, (full_qkv, full_out, full_pred) = rest[:-3], rest[-3:]
    wide = full_qkv.shape[1]

    def write(row, count, source, base):
        place = pl.ds(row, count)
        if source is None:
            full_qkv[place, :] = qkv_ref[...]
            full_out[place, :] = out_ref[...]
            full_pred[place, :PIX] = pred_ref[...]
        else:
            part = pl.ds(base, count)
            full_qkv[place, :] = source[part, :wide]
            full_out[place, :] = source[part, wide : wide + DD]
            full_pred[place, :PIX] = source[part, wide + DD : wide + DD + PIX]

    assemble(refs, [qkv_ref], mp, piece, write)


def decoder_weights(own, pieces, mp, piece):
    shapes = [(mp * w.shape[0], w.shape[1]) for w in own]
    return pl.pallas_call(
        functools.partial(decoder_weights_kernel, mp, piece),
        out_shape=[jax.ShapeDtypeStruct(s, bf16) for s in shapes],
        in_specs=[VMEM] * (3 + len(pieces)),
        out_specs=[VMEM] * 3,
        compiler_params=pltpu.CompilerParams(vmem_limit_bytes=24 * MIB),
        cost_estimate=cost(0, 2 * 2 * sum(a * b for a, b in shapes)),
        name="decoder_weights",
    )(*own, *pieces)


def encode_kernel(count, up_ref, fused_ref, *rest):
    normed, outs, acc = rest[:count], rest[count : 2 * count], rest[2 * count]
    step = pl.program_id(0)
    rows = jnp.concatenate([r[...] for r in normed], axis=0)
    hidden = jax.nn.gelu(dot(rows, up_ref[...]), approximate=True).astype(bf16)
    term = dot(hidden, fused_ref[...])

    @pl.when(step == 0)
    def _():
        acc[...] = term

    @pl.when(step > 0)
    def _():
        acc[...] += term

    @pl.when(step == pl.num_programs(0) - 1)
    def _():
        for i, out in enumerate(outs):
            out[...] = acc[i * SHARE : (i + 1) * SHARE, :].astype(bf16)


def encode(normed, w_up, fused):
    width, hidden = w_up.shape
    columns = fused.shape[1]
    count = len(normed)
    tile = 256 if hidden % 256 == 0 else hidden
    return pl.pallas_call(
        functools.partial(encode_kernel, count),
        grid=(hidden // tile,),
        out_shape=[jax.ShapeDtypeStruct((SHARE, columns), bf16)] * count,
        in_specs=[
            pl.BlockSpec((width, tile), lambda i: (0, i)),
            pl.BlockSpec((tile, columns), lambda i: (i, 0)),
        ]
        + [pl.BlockSpec((SHARE, width), lambda i: (0, 0))] * count,
        out_specs=[pl.BlockSpec((SHARE, columns), lambda i: (0, 0))] * count,
        scratch_shapes=[pltpu.VMEM((count * SHARE, columns), f32)],
        compiler_params=pltpu.CompilerParams(vmem_limit_bytes=32 * MIB),
        cost_estimate=cost(
            2 * count * SHARE * hidden * (width + columns),
            2 * hidden * (width + columns),
            count * SHARE * hidden,
        ),
        name="encode",
    )(w_up, fused, *normed)


def sum_kernel(residual_ref, *rest):
    parts, (sums_ref, tail_ref) = rest[:-2], rest[-2:]
    total = residual_ref[...]
    for part in parts:
        total += part[...].astype(f32)
    sums_ref[...] = total.astype(bf16)
    tail_ref[...] = total[SMALLEST:, :].astype(bf16)


def add_up(residual, parts):
    rows, columns = residual.shape
    return pl.pallas_call(
        sum_kernel,
        out_shape=(
            jax.ShapeDtypeStruct((rows, columns), bf16),
            jax.ShapeDtypeStruct((rows - SMALLEST, columns), bf16),
        ),
        in_specs=[VMEM] * (1 + len(parts)),
        out_specs=(VMEM, VMEM),
        cost_estimate=cost(0, 2 * (3 + len(parts)) * rows * columns),
        name="add_up",
    )(residual, *parts)


def decode_kernel(
    visible_ref,
    keep_ref,
    targets_ref,
    mask_ref,
    position_ref,
    qkv_ref,
    out_ref,
    pred_ref,
    sums_ref,
    tail_ref,
    recon_ref,
    loss_ref,
    flat,
    errors,
):
    patch_count = position_ref.shape[0]
    patch = lax.broadcasted_iota(jnp.int32, (patch_count, patch_count), 0)
    slot = lax.broadcasted_iota(jnp.int32, (patch_count, patch_count), 1)
    chosen = ((keep_ref[...] == patch) & (slot < visible_ref[0])).astype(f32)
    seen = jnp.max(chosen, axis=1, keepdims=True)
    slots = chosen.astype(bf16)[:, :SHARE]
    late = jnp.where(slot >= SHARE, chosen, 0.0)
    moved = pltpu.roll(late, patch_count + VMAX - SHARE - visible_ref[0], 1)
    picked = dot(slots, sums_ref[...]) + dot(moved.astype(bf16)[:, : VMAX - SHARE], tail_ref[...])
    start = jnp.where(seen > 0, picked, mask_ref[...].astype(f32)) + position_ref[...].astype(f32)
    projections = dot(layer_norm(start).astype(bf16), qkv_ref[...]).astype(bf16)
    scale = 1.0 / math.sqrt(HSIZE)
    mixed = []
    for head in range(DD // HSIZE):
        columns = slice(head * HSIZE, (head + 1) * HSIZE)
        query = projections[:, :DD][:, columns]
        key = projections[:, DD : 2 * DD][:, columns]
        value = projections[:, 2 * DD :][:, columns]
        scores = lax.dot_general(
            query, key, (((1,), (1,)), ((), ())), preferred_element_type=f32
        ) * scale
        weights = jnp.exp(scores - jnp.max(scores, axis=-1, keepdims=True))
        probs = (weights / jnp.sum(weights, axis=-1, keepdims=True)).astype(bf16)
        mixed.append(dot(probs, value).astype(bf16))
    after = start + dot(jnp.concatenate(mixed, axis=1), out_ref[...])
    prediction = dot(layer_norm(after).astype(bf16), pred_ref[...])
    group = 4
    wide = group * PIX
    flat[:, :PIX] = prediction[:, :PIX]
    lines = patch_count // group
    together = jnp.concatenate(
        [flat[pl.ds(i, lines, stride=group), :][:, :PIX] for i in range(group)], axis=1
    )
    for line in range(lines):
        place = slice(line * wide, (line + 1) * wide)
        recon_ref[:, place] = together[line : line + 1, :].astype(bf16)
        errors[line : line + 1, :] = together[line : line + 1, :] - targets_ref[:, place].astype(f32)
    squares = errors[...] * errors[...]
    for i in range(group):
        flat[pl.ds(i, lines, stride=group), :PIX] = squares[:, i * PIX : (i + 1) * PIX]
    loss = jnp.sum(flat[:, :PIX], axis=1, keepdims=True) * (1.0 / PIX)
    loss = jnp.where(seen > 0, 0.0, loss)
    loss_ref[...] = jnp.sum(jnp.where(patch == slot, loss, 0.0), axis=0, keepdims=True)


def decode(visible, keep_index, targets, mask_token, position, weights, sums, tail):
    patch_count = position.shape[0]
    rest = (keep_index, targets, mask_token[None], position, *weights, sums, tail)
    return pl.pallas_call(
        decode_kernel,
        out_shape=(
            jax.ShapeDtypeStruct(targets.shape, bf16),
            jax.ShapeDtypeStruct((1, patch_count), f32),
        ),
        in_specs=[SMEM] + [VMEM] * len(rest),
        out_specs=(VMEM, VMEM),
        scratch_shapes=[
            pltpu.VMEM((patch_count, LANES), f32),
            pltpu.VMEM((patch_count // 4, 4 * PIX), f32),
        ],
        compiler_params=pltpu.CompilerParams(vmem_limit_bytes=24 * MIB),
        cost_estimate=cost(2 * patch_count * DD * (5 * DD), 2 * 6 * DD * DD, 8 * patch_count**2),
        name="decode",
    )(visible, *rest)


def body(
    dp,
    mp,
    patches,
    keep_index,
    visible,
    targets,
    w_up,
    w_down,
    dec_embed,
    dec_qkv,
    dec_out,
    dec_pred,
    mask_token,
    position,
):
    embed_piece = dec_embed.shape[0] // dp
    piece = dec_qkv.shape[0] // dp
    in_pieces = dp == 8 and embed_piece % 16 == 0 and piece % 16 == 0
    half = dp // 2
    weights = (dec_embed, dec_qkv, dec_out, dec_pred)
    tail, *part = first_parts(keep_index, patches, weights if in_pieces else (), dp)
    tail = xor_permute(tail, "dp", dp, half)
    if in_pieces:
        embed_pieces = gather_pieces(part[0], dp, mp)
    else:
        dec_embed = lax.all_gather(dec_embed, "mp", axis=0, tiled=True)
        embed_pieces = []
    rows, normed = select_rows(visible, keep_index, patches, tail)
    others = [xor_permute(normed, "mp", mp, k) for k in range(mp - 1, 0, -1)]
    if in_pieces:
        pieces = gather_pieces(part[1], dp, mp)
        weights = decoder_weights(weights[1:], pieces, mp, piece)
    else:
        weights = [lax.all_gather(w, "mp", axis=0, tiled=True) for w in weights[1:]]
    fused, residual = fuse_weights(rows, w_down, dec_embed, embed_pieces, mp, embed_piece)
    partial = encode([normed] + others, w_up, fused)
    parts = [partial[0]] + [
        xor_permute(s, "mp", mp, k) for k, s in zip(range(mp - 1, 0, -1), partial[1:])
    ]
    sums, own_tail = add_up(residual, parts)
    tail = xor_permute(own_tail, "dp", dp, half)
    return decode(visible, keep_index, targets, mask_token, position, weights, sums, tail)


def solution(mesh):
    return jax.shard_map(
        functools.partial(body, mesh.shape["dp"], mesh.shape["mp"]),
        mesh=mesh,
        in_specs=(
            P(("dp", "mp"), None, None),
            P(("dp", "mp"), None),
            P(("dp", "mp")),
            P(("dp", "mp"), None),
            P(None, "mp"),
            P("mp", None),
            P("mp", None),
            P("mp", None),
            P("mp", None),
            P("mp", None),
            P(),
            P(),
        ),
        out_specs=(P(("dp", "mp"), None), P(("dp", "mp"), None)),
        check_vma=False,
    )
```

```python
import functools
import math

import jax
import jax.numpy as jnp
from jax import lax
from jax.experimental import pallas as pl
from jax.experimental.pallas import tpu as pltpu
from jax.sharding import PartitionSpec as P

DD = 512
HSIZE = 64
PIX = 96
VMAX = 80
SHARE = 48
SMALLEST = 2 * SHARE - VMAX
LANES = 128
EPSILON = 1e-06
LIMIT = 14 << 20
LONG = 10**11

f32 = jnp.float32
bf16 = jnp.bfloat16
VMEM = pl.BlockSpec(memory_space=pltpu.VMEM)
SMEM = pl.BlockSpec(memory_space=pltpu.SMEM)
HBM = pl.BlockSpec(memory_space=pltpu.HBM)


def dot(left, right):
    return jnp.dot(left, right, preferred_element_type=f32)


def layer_norm(values):
    center = values - jnp.mean(values, axis=-1, keepdims=True)
    spread = jnp.mean(center * center, axis=-1, keepdims=True)
    return center * lax.rsqrt(spread + EPSILON)


def cost(flops, size):
    return pl.CostEstimate(flops=flops, bytes_accessed=size, transcendentals=0)


def stay(array):
    return pltpu.with_memory_space_constraint(array, pltpu.HBM)


def call(kernel, name, outs, ins, flops=0, scratch=(), after=()):
    count = len(ins)

    def run(*refs):
        kernel(*refs[:count], *refs[count + len(after) :])

    size = sum(2 * math.prod(a.shape) for a in (*ins, *outs))
    return pl.pallas_call(
        run,
        out_shape=outs,
        in_specs=[SMEM if a.ndim == 1 else VMEM for a in ins]
        + [pl.BlockSpec(memory_space=pl.ANY)] * len(after),
        out_specs=[VMEM] * len(outs),
        scratch_shapes=scratch,
        compiler_params=pltpu.CompilerParams(vmem_limit_bytes=LIMIT),
        cost_estimate=cost(flops, size),
        name=name,
    )(*ins, *after)


def near(*shape, dtype=bf16):
    return pltpu.VMEM(shape, dtype)


def xor_permute(values, axis, size, bit):
    return lax.ppermute(values, axis, [(i, i ^ bit) for i in range(size)])


def pick(chosen, values):
    return lax.dot_general(chosen, values, (((0,), (0,)), ((), ())), preferred_element_type=f32)


def rows_kernel(visible_ref, keep_ref, patches_ref, tail_ref, rows_ref, normed_ref):
    patch_count = patches_ref.shape[0]
    visible = visible_ref[0]
    square = (patch_count, patch_count)
    patch = lax.broadcasted_iota(jnp.int32, square, 0)
    slot = lax.broadcasted_iota(jnp.int32, square, 1)
    own = ((keep_ref[...] == patch) & (slot < visible)).astype(f32).astype(bf16)[:, :SHARE]
    other = (slot - visible == patch).astype(f32).astype(bf16)[: VMAX - SHARE, :SHARE]
    rows = pick(own, patches_ref[...]) + pick(other, tail_ref[...])
    rows_ref[...] = rows.astype(bf16)
    normed_ref[...] = layer_norm(rows).astype(bf16)


def begin_kernel(keep_in, patches_ref, *refs):
    if len(refs) > 5:
        weights, (keep_ref, rows_ref, tail_ref, part_ref, embed_part_ref, rest_ref, pred, sems) = refs[:4], refs[4:]
    else:
        weights, (keep_ref, rows_ref, tail_ref, sems) = (), refs
    copies = [
        pltpu.make_async_copy(patches_ref.at[0], rows_ref, sems.at[0]),
        pltpu.make_async_copy(keep_in, keep_ref, sems.at[1]),
    ]
    if weights:
        embed_ref, qkv_ref, out_ref, pred_ref = weights
        j = lax.axis_index("dp")
        count, wide = part_ref.shape[0], qkv_ref.shape[1]
        fold = embed_ref.shape[0] // qkv_ref.shape[0]
        own = pl.ds(pl.multiple_of(j * count, 16), count)
        start = fold * DD
        moves = [(pred_ref, pred)]
        for i in range(fold):
            rows = pl.ds(pl.multiple_of((j * fold + i) * count, 16), count)
            moves.append((embed_ref.at[rows, :], part_ref.at[:, i * DD : (i + 1) * DD]))
        moves.append((qkv_ref.at[own, :], part_ref.at[:, start : start + wide]))
        moves.append((out_ref.at[own, :], part_ref.at[:, start + wide : start + wide + DD]))
        copies += [pltpu.make_async_copy(x, y, sems.at[i]) for i, (x, y) in enumerate(moves, 2)]
    for copy in copies:
        copy.start()
    for copy in copies:
        copy.wait()
    if weights:
        columns = pick_columns(pred[...], j * count, count)
        last = start + wide + DD
        part_ref[:, last:] = jnp.zeros((count, LANES), bf16)
        part_ref[:, last : last + PIX] = columns.astype(bf16)
        embed_part_ref[...] = part_ref[:, :start]
        rest_ref[...] = part_ref[:, start:]
    patch_count = rows_ref.shape[0]
    patch = lax.broadcasted_iota(jnp.int32, (patch_count, patch_count), 0)
    chosen = (keep_ref[...] == patch).astype(f32).astype(bf16)[:, SHARE:VMAX]
    tail_ref[...] = pick(chosen, rows_ref[...]).astype(bf16)


def pick_columns(values, first, count):
    shape = (count, values.shape[1])
    place = lax.broadcasted_iota(jnp.int32, shape, 1) - lax.broadcasted_iota(jnp.int32, shape, 0)
    return lax.dot_general(
        (place == first).astype(f32).astype(bf16), values, (((1,), (1,)), ((), ())), preferred_element_type=f32
    )


def begin(keep_index, patches, weights, columns):
    _, patch_count, width = patches.shape
    arrays = (keep_index, patches, *weights)
    outs = [near(*keep_index.shape, dtype=jnp.int32), near(patch_count, width), near(VMAX - SHARE, width)]
    scratch = []
    if weights:
        outs += [near(weights[1].shape[0] // 8, c) for c in (sum(columns), *columns)]
        scratch.append(pltpu.VMEM(weights[3].shape, bf16))
    return pl.pallas_call(
        begin_kernel,
        out_shape=outs,
        in_specs=[HBM] * len(arrays),
        out_specs=[VMEM] * len(outs),
        scratch_shapes=scratch + [pltpu.SemaphoreType.DMA((9,))],
        compiler_params=pltpu.CompilerParams(vmem_limit_bytes=LIMIT),
        cost_estimate=cost(0, 2 * patch_count * width),
        name="begin",
    )(*[stay(a) for a in arrays])


def trade_kernel(embed_ref, rest_ref, out_ref):
    wide = embed_ref.shape[1]
    out_ref[:, :wide] = embed_ref[...]
    out_ref[:, wide:] = rest_ref[...]


def split_kernel(first, second, third, traded, embed_ref, rest_ref):
    start = second.shape[1]
    fold, count = start // DD, second.shape[0]
    for k, part in enumerate((first, second, traded)):
        for i in range(fold):
            place = (k * fold + i) * count
            embed_ref[place : place + count, :] = part[:, i * DD : (i + 1) * DD]
    rest_ref[:count, :] = first[:, start:]
    rest_ref[count : 2 * count, :] = traded[:, start:]
    rest_ref[2 * count :, :] = third[...]


def join_kernel(*refs):
    parts, out_ref = refs[:-1], refs[-1]
    count = parts[0].shape[0]
    for i, part in enumerate(parts):
        out_ref[i * count : (i + 1) * count, :] = part[...]


def join(name, parts, flops=0, after=()):
    rows, columns = parts[0].shape
    return call(join_kernel, name, [near(len(parts) * rows, columns)], parts, flops, after=after)[0]


PLANE = (0, 2, 4, 6)


def assemble(refs, own_rows, mp, piece, write):
    near_refs = refs[:-1]
    m = lax.axis_index("mp")
    j = lax.axis_index("dp")
    write(pl.multiple_of(m * own_rows, 16), own_rows, None, 0)
    block = (mp - 1) * piece
    for place, distance in enumerate(PLANE):
        for core in (0, 1):
            alone = not core and len(near_refs) > 1
            source = near_refs[place] if alone else refs[-1 if core else 0]
            base = 0 if alone else place * block
            for k in range(1, mp):
                row = (m ^ k) * own_rows + (j ^ distance ^ core) * piece
                write(pl.multiple_of(row, 16), piece, source, base + (k - 1) * piece)


def embed_kernel(mp, piece, own_ref, *rest):
    refs, full = rest[:-1], rest[-1]

    def write(row, count, source, base):
        if source is None:
            full[pl.ds(row, count), :] = own_ref[...]
        else:
            full[pl.ds(row, count), :] = source[base : base + count, :]

    assemble(refs, own_ref.shape[0], mp, piece, write)


def decoder_weights_kernel(mp, piece, qkv_ref, out_ref, pred_ref, *rest):
    refs, (full_qkv, full_out, full_pred) = rest[:-3], rest[-3:]
    wide = full_qkv.shape[1]

    def write(row, count, source, base):
        place = pl.ds(row, count)
        if source is None:
            full_qkv[place, :] = qkv_ref[...]
            full_out[place, :] = out_ref[...]
            full_pred[place, :PIX] = pred_ref[...].astype(f32).T.astype(bf16)
        else:
            part = pl.ds(base, count)
            full_qkv[place, :] = source[part, :wide]
            full_out[place, :] = source[part, wide : wide + DD]
            full_pred[place, :PIX] = source[part, wide + DD : wide + DD + PIX]

    assemble(refs, qkv_ref.shape[0], mp, piece, write)


def encode_kernel(up_ref, down_ref, rows_ref, *rest):
    blocks, partial_ref = rest[:-1], rest[-1]
    rows = jnp.concatenate([r[...] for r in blocks], axis=0)
    hidden = up_ref.shape[1]
    tile = 256 if hidden % 256 == 0 else hidden
    total = None
    for i in range(0, hidden, tile):
        units = jax.nn.gelu(dot(rows, up_ref[:, i : i + tile]), approximate=True).astype(bf16)
        term = dot(units, down_ref[i : i + tile, :])
        total = term if total is None else total + term
    partial_ref[:SHARE, :] = (rows_ref[...].astype(f32) + total[:SHARE]).astype(bf16)
    partial_ref[SHARE:, :] = total[SHARE:].astype(bf16)


def encode(up, down, rows, blocks):
    return call(
        encode_kernel,
        "encode",
        [near(len(blocks) * SHARE, up.shape[0])],
        (up, down, rows, *blocks),
        flops=LONG,
    )[0]


def embed_rows_kernel(embed_ref, rows_ref, *outs):
    embedded = dot(rows_ref[...], embed_ref[...])
    for i, out in enumerate(outs):
        out[...] = embedded[i * SHARE : (i + 1) * SHARE].astype(bf16)


def sum_kernel(*refs):
    parts, (sums_ref, tail_ref) = refs[:-2], refs[-2:]
    total = parts[0][...].astype(f32)
    for part in parts[1:]:
        total += part[...].astype(f32)
    sums_ref[...] = total.astype(bf16)
    tail_ref[...] = total[SMALLEST:, :].astype(bf16)


def decode_kernel(
    visible_ref,
    keep_ref,
    targets_ref,
    mask_ref,
    position_ref,
    qkv_ref,
    out_ref,
    pred_ref,
    sums_ref,
    tail_ref,
    recon_ref,
    loss_ref,
    flat,
    errors,
):
    patch_count = position_ref.shape[0]
    patch = lax.broadcasted_iota(jnp.int32, (patch_count, patch_count), 0)
    slot = lax.broadcasted_iota(jnp.int32, (patch_count, patch_count), 1)
    chosen = ((keep_ref[...] == patch) & (slot < visible_ref[0])).astype(f32)
    seen = jnp.max(chosen, axis=1, keepdims=True)
    slots = chosen.astype(bf16)[:, :SHARE]
    late = jnp.where(slot >= SHARE, chosen, 0.0)
    moved = pltpu.roll(late, patch_count + VMAX - SHARE - visible_ref[0], 1)
    picked = dot(slots, sums_ref[...]) + dot(moved.astype(bf16)[:, : VMAX - SHARE], tail_ref[...])
    start = jnp.where(seen > 0, picked, mask_ref[...].astype(f32)) + position_ref[...].astype(f32)
    projections = dot(layer_norm(start).astype(bf16), qkv_ref[...]).astype(bf16)
    scale = 1.0 / math.sqrt(HSIZE)
    mixed = []
    for head in range(DD // HSIZE):
        columns = slice(head * HSIZE, (head + 1) * HSIZE)
        query = projections[:, :DD][:, columns]
        key = projections[:, DD : 2 * DD][:, columns]
        value = projections[:, 2 * DD :][:, columns]
        scores = lax.dot_general(
            query, key, (((1,), (1,)), ((), ())), preferred_element_type=f32
        ) * scale
        weights = jnp.exp(scores - jnp.max(scores, axis=-1, keepdims=True))
        probs = (weights / jnp.sum(weights, axis=-1, keepdims=True)).astype(bf16)
        mixed.append(dot(probs, value).astype(bf16))
    after = start + dot(jnp.concatenate(mixed, axis=1), out_ref[...])
    prediction = dot(layer_norm(after).astype(bf16), pred_ref[...])
    group = 4
    wide = group * PIX
    flat[:, :PIX] = prediction[:, :PIX]
    lines = patch_count // group
    together = jnp.concatenate(
        [flat[pl.ds(i, lines, stride=group), :][:, :PIX] for i in range(group)], axis=1
    )
    for line in range(lines):
        place = slice(line * wide, (line + 1) * wide)
        recon_ref[:, place] = together[line : line + 1, :].astype(bf16)
        errors[line : line + 1, :] = together[line : line + 1, :] - targets_ref[:, place].astype(f32)
    squares = errors[...] * errors[...]
    for i in range(group):
        flat[pl.ds(i, lines, stride=group), :PIX] = squares[:, i * PIX : (i + 1) * PIX]
    loss = jnp.sum(flat[:, :PIX], axis=1, keepdims=True) * (1.0 / PIX)
    loss = jnp.where(seen > 0, 0.0, loss)
    loss_ref[...] = jnp.sum(jnp.where(patch == slot, loss, 0.0), axis=0, keepdims=True)


def body(
    dp,
    mp,
    patches,
    keep_index,
    visible,
    targets,
    w_up,
    w_down,
    dec_embed,
    dec_qkv,
    dec_out,
    dec_pred,
    mask_token,
    position,
):
    _, patch_count, width = patches.shape
    fold, piece = dec_embed.shape[0] // dec_qkv.shape[0], dec_qkv.shape[0] // dp
    in_pieces = (dp, mp) == (8, 4) and piece % 16 == 0
    pred_columns = dec_pred.T
    order = (1, *range(mp - 1, 1, -1))
    over_mp = lambda a, k: xor_permute(a, "mp", mp, k)
    over_dp = lambda a, bit: xor_permute(a, "dp", dp, bit)
    columns = (fold * DD, DD + dec_qkv.shape[1] + LANES)
    shards = (dec_embed, dec_qkv, dec_out, pred_columns)
    keep_index, patches, tail, *part = begin(
        keep_index, patches, shards if in_pieces else (), columns
    )
    tail = over_dp(tail, dp // 2)
    if in_pieces:
        second, third = over_mp(part[1], 2), over_mp(part[2], 3)
        (traded,) = call(trade_kernel, "trade", [near(piece, sum(columns))], (second, third), after=(tail,))
        first = over_mp(part[0], 1)
        fence = (traded,)
    else:
        fence = ()
    rows, normed = call(
        rows_kernel,
        "select_rows",
        [near(SHARE, width)] * 2,
        (visible, keep_index, patches, tail),
        after=fence,
    )
    others = {k: over_mp(normed, k) for k in order}
    if in_pieces:
        embed, rest = call(
            split_kernel,
            "split",
            [near((mp - 1) * fold * piece, DD), near((mp - 1) * piece, columns[1])],
            (first, second, third, over_mp(traded, 1)),
            flops=LONG,
            after=(normed,),
        )
        embeds = [embed] + [over_dp(embed, bit) for bit in PLANE[1:]]
        rests = join("join_near", [rest, over_dp(rest, PLANE[1])])
    else:
        full_embed, *weights = [
            lax.all_gather(w, "mp", axis=0, tiled=True) for w in (dec_embed, dec_qkv, dec_out, dec_pred)
        ]
    partial = encode(w_up, w_down, rows, (normed, *[others[k] for k in order]))
    if in_pieces:
        embeds.append(over_dp(join("join_embed", embeds, LONG, (rests, *others.values())), 1))
        (full_embed,) = call(
            functools.partial(embed_kernel, mp, fold * piece),
            "full_embed",
            [near(mp * dec_embed.shape[0], DD)],
            (shards[0], *embeds),
        )
    out, *sent = call(
        embed_rows_kernel,
        "embed_rows",
        [near(SHARE, DD)] * mp,
        (full_embed, partial),
        flops=2 * mp * SHARE * width * DD,
    )
    back = [over_mp(s, k) for k, s in zip(order, sent)]
    sums, own_tail = call(
        sum_kernel, "add_up", [near(SHARE, DD), near(SHARE - SMALLEST, DD)], (out, *back)
    )
    if in_pieces:
        rests = join("join_rest", [rests, over_dp(rests, PLANE[2])], after=(sums,))
        rests = (rests, over_dp(rests, 1))
        weights = call(
            functools.partial(decoder_weights_kernel, mp, piece),
            "decoder_weights",
            [near(mp * w.shape[0], w.shape[1]) for w in (dec_qkv, dec_out, dec_pred)],
            (*shards[1:], *rests),
        )
    return call(
        decode_kernel,
        "decode",
        [
            jax.ShapeDtypeStruct(targets.shape, bf16),
            jax.ShapeDtypeStruct((1, patch_count), f32),
        ],
        (
            visible,
            keep_index,
            targets,
            mask_token[None],
            position,
            *weights,
            sums,
            over_dp(own_tail, dp // 2),
        ),
        flops=10 * patch_count * DD * DD,
        scratch=[pltpu.VMEM((patch_count, LANES), f32), pltpu.VMEM((patch_count // 4, 4 * PIX), f32)],
    )


def solution(mesh):
    return jax.shard_map(
        functools.partial(body, mesh.shape["dp"], mesh.shape["mp"]),
        mesh=mesh,
        in_specs=(
            P(("dp", "mp"), None, None),
            P(("dp", "mp"), None),
            P(("dp", "mp")),
            P(("dp", "mp"), None),
            P(None, "mp"),
            P("mp", None),
            P("mp", None),
            P("mp", None),
            P("mp", None),
            P("mp", None),
            P(),
            P(),
        ),
        out_specs=(P(("dp", "mp"), None), P(("dp", "mp"), None)),
        check_vma=False,
    )
```

```python
import functools
import math

import jax
import jax.numpy as jnp
from jax import lax
from jax.experimental import pallas as pl
from jax.experimental.pallas import tpu as pltpu
from jax.sharding import PartitionSpec as P

DD = 512
HSIZE = 64
PIX = 96
VMAX = 80
SHARE = 48
SMALLEST = 2 * SHARE - VMAX
LANES = 128
EPSILON = 1e-06
LIMIT = 14 << 20
LONG = 10**11

f32 = jnp.float32
bf16 = jnp.bfloat16
VMEM = pl.BlockSpec(memory_space=pltpu.VMEM)
SMEM = pl.BlockSpec(memory_space=pltpu.SMEM)
HBM = pl.BlockSpec(memory_space=pltpu.HBM)


def dot(left, right):
    return jnp.dot(left, right, preferred_element_type=f32)


def layer_norm(values):
    center = values - jnp.mean(values, axis=-1, keepdims=True)
    spread = jnp.mean(center * center, axis=-1, keepdims=True)
    return center * lax.rsqrt(spread + EPSILON)


def cost(flops, size):
    return pl.CostEstimate(flops=flops, bytes_accessed=size, transcendentals=0)


def stay(array):
    return pltpu.with_memory_space_constraint(array, pltpu.HBM)


def call(kernel, name, outs, ins, flops=0, scratch=(), after=()):
    count = len(ins)

    def run(*refs):
        kernel(*refs[:count], *refs[count + len(after) :])

    size = sum(2 * math.prod(a.shape) for a in (*ins, *outs))
    return pl.pallas_call(
        run,
        out_shape=outs,
        in_specs=[SMEM if a.ndim == 1 else VMEM for a in ins]
        + [pl.BlockSpec(memory_space=pl.ANY)] * len(after),
        out_specs=[VMEM] * len(outs),
        scratch_shapes=scratch,
        compiler_params=pltpu.CompilerParams(vmem_limit_bytes=LIMIT),
        cost_estimate=cost(flops, size),
        name=name,
    )(*ins, *after)


def near(*shape, dtype=bf16):
    return pltpu.VMEM(shape, dtype)


def xor_permute(values, axis, size, bit):
    return lax.ppermute(values, axis, [(i, i ^ bit) for i in range(size)])


def pick(chosen, values):
    return lax.dot_general(chosen, values, (((0,), (0,)), ((), ())), preferred_element_type=f32)


def rows_kernel(visible_ref, keep_ref, patches_ref, tail_ref, rows_ref, normed_ref):
    patch_count = patches_ref.shape[0]
    visible = visible_ref[0]
    square = (patch_count, patch_count)
    patch = lax.broadcasted_iota(jnp.int32, square, 0)
    slot = lax.broadcasted_iota(jnp.int32, square, 1)
    own = ((keep_ref[...] == patch) & (slot < visible)).astype(f32).astype(bf16)[:, :SHARE]
    other = (slot - visible == patch).astype(f32).astype(bf16)[: VMAX - SHARE, :SHARE]
    rows = pick(own, patches_ref[...]) + pick(other, tail_ref[...])
    rows_ref[...] = rows.astype(bf16)
    normed_ref[...] = layer_norm(rows).astype(bf16)


def begin_kernel(keep_in, patches_ref, *refs):
    if len(refs) > 5:
        weights, (keep_ref, rows_ref, tail_ref, part_ref, embed_part_ref, rest_ref, pred, sems) = refs[:4], refs[4:]
    else:
        weights, (keep_ref, rows_ref, tail_ref, sems) = (), refs
    copies = [
        pltpu.make_async_copy(patches_ref.at[0], rows_ref, sems.at[0]),
        pltpu.make_async_copy(keep_in, keep_ref, sems.at[1]),
    ]
    if weights:
        embed_ref, qkv_ref, out_ref, pred_ref = weights
        j = lax.axis_index("dp")
        count, wide = part_ref.shape[0], qkv_ref.shape[1]
        fold = embed_ref.shape[0] // qkv_ref.shape[0]
        own = pl.ds(pl.multiple_of(j * count, 16), count)
        start = fold * DD
        moves = [(pred_ref, pred)]
        for i in range(fold):
            rows = pl.ds(pl.multiple_of((j * fold + i) * count, 16), count)
            moves.append((embed_ref.at[rows, :], part_ref.at[:, i * DD : (i + 1) * DD]))
        moves.append((qkv_ref.at[own, :], part_ref.at[:, start : start + wide]))
        moves.append((out_ref.at[own, :], part_ref.at[:, start + wide : start + wide + DD]))
        copies += [pltpu.make_async_copy(x, y, sems.at[i]) for i, (x, y) in enumerate(moves, 2)]
    for copy in copies:
        copy.start()
    for copy in copies:
        copy.wait()
    if weights:
        columns = pick_columns(pred[...], j * count, count)
        last = start + wide + DD
        part_ref[:, last:] = jnp.zeros((count, LANES), bf16)
        part_ref[:, last : last + PIX] = columns.astype(bf16)
        embed_part_ref[...] = part_ref[:, :start]
        rest_ref[...] = part_ref[:, start:]
    patch_count = rows_ref.shape[0]
    patch = lax.broadcasted_iota(jnp.int32, (patch_count, patch_count), 0)
    chosen = (keep_ref[...] == patch).astype(f32).astype(bf16)[:, SHARE:VMAX]
    tail_ref[...] = pick(chosen, rows_ref[...]).astype(bf16)


def pick_columns(values, first, count):
    shape = (count, values.shape[1])
    place = lax.broadcasted_iota(jnp.int32, shape, 1) - lax.broadcasted_iota(jnp.int32, shape, 0)
    return lax.dot_general(
        (place == first).astype(f32).astype(bf16), values, (((1,), (1,)), ((), ())), preferred_element_type=f32
    )


def begin(keep_index, patches, weights, columns):
    _, patch_count, width = patches.shape
    arrays = (keep_index, patches, *weights)
    outs = [near(*keep_index.shape, dtype=jnp.int32), near(patch_count, width), near(VMAX - SHARE, width)]
    scratch = []
    if weights:
        outs += [near(weights[1].shape[0] // 8, c) for c in (sum(columns), *columns)]
        scratch.append(pltpu.VMEM(weights[3].shape, bf16))
    return pl.pallas_call(
        begin_kernel,
        out_shape=outs,
        in_specs=[HBM] * len(arrays),
        out_specs=[VMEM] * len(outs),
        scratch_shapes=scratch + [pltpu.SemaphoreType.DMA((9,))],
        compiler_params=pltpu.CompilerParams(vmem_limit_bytes=LIMIT),
        cost_estimate=cost(0, 2 * patch_count * width),
        name="begin",
    )(*[stay(a) for a in arrays])


def trade_kernel(embed_ref, rest_ref, out_ref):
    wide = embed_ref.shape[1]
    out_ref[:, :wide] = embed_ref[...]
    out_ref[:, wide:] = rest_ref[...]


def split_kernel(first, second, third, traded, embed_ref, rest_ref):
    start = second.shape[1]
    fold, count = start // DD, second.shape[0]
    for k, part in enumerate((first, second, traded)):
        for i in range(fold):
            place = (k * fold + i) * count
            embed_ref[place : place + count, :] = part[:, i * DD : (i + 1) * DD]
    rest_ref[:count, :] = first[:, start:]
    rest_ref[count : 2 * count, :] = traded[:, start:]
    rest_ref[2 * count :, :] = third[...]


def join_kernel(*refs):
    parts, out_ref = refs[:-1], refs[-1]
    count = parts[0].shape[0]
    for i, part in enumerate(parts):
        out_ref[i * count : (i + 1) * count, :] = part[...]


def join(name, parts, flops=0, after=()):
    rows, columns = parts[0].shape
    return call(join_kernel, name, [near(len(parts) * rows, columns)], parts, flops, after=after)[0]


PLANE = (0, 2, 4, 6)


def assemble(refs, own_rows, mp, piece, write):
    near_refs = refs[:-1]
    m = lax.axis_index("mp")
    j = lax.axis_index("dp")
    write(pl.multiple_of(m * own_rows, 16), own_rows, None, 0)
    block = (mp - 1) * piece
    for place, distance in enumerate(PLANE):
        for core in (0, 1):
            alone = not core and len(near_refs) > 1
            source = near_refs[place] if alone else refs[-1 if core else 0]
            base = 0 if alone else place * block
            for k in range(1, mp):
                row = (m ^ k) * own_rows + (j ^ distance ^ core) * piece
                write(pl.multiple_of(row, 16), piece, source, base + (k - 1) * piece)


def embed_kernel(mp, piece, own_ref, *rest):
    refs, full = rest[:-1], rest[-1]

    def write(row, count, source, base):
        if source is None:
            full[pl.ds(row, count), :] = own_ref[...]
        else:
            full[pl.ds(row, count), :] = source[base : base + count, :]

    assemble(refs, own_ref.shape[0], mp, piece, write)


def decoder_weights_kernel(mp, piece, qkv_ref, out_ref, pred_ref, *rest):
    refs, (full_qkv, full_out, full_pred) = rest[:-3], rest[-3:]
    wide = full_qkv.shape[1]

    def write(row, count, source, base):
        place = pl.ds(row, count)
        if source is None:
            full_qkv[place, :] = qkv_ref[...]
            full_out[place, :] = out_ref[...]
            full_pred[place, :PIX] = pred_ref[...].astype(f32).T.astype(bf16)
        else:
            part = pl.ds(base, count)
            full_qkv[place, :] = source[part, :wide]
            full_out[place, :] = source[part, wide : wide + DD]
            full_pred[place, :PIX] = source[part, wide + DD : wide + DD + PIX]

    assemble(refs, qkv_ref.shape[0], mp, piece, write)


def encode_kernel(up_ref, down_ref, rows_ref, *rest):
    blocks, partial_ref = rest[:-1], rest[-1]
    rows = jnp.concatenate([r[...] for r in blocks], axis=0)
    hidden = up_ref.shape[1]
    tile = 256 if hidden % 256 == 0 else hidden
    total = None
    for i in range(0, hidden, tile):
        units = jax.nn.gelu(dot(rows, up_ref[:, i : i + tile]), approximate=True).astype(bf16)
        term = dot(units, down_ref[i : i + tile, :])
        total = term if total is None else total + term
    partial_ref[:SHARE, :] = (rows_ref[...].astype(f32) + total[:SHARE]).astype(bf16)
    partial_ref[SHARE:, :] = total[SHARE:].astype(bf16)


def encode(up, down, rows, blocks):
    return call(
        encode_kernel,
        "encode",
        [near(len(blocks) * SHARE, up.shape[0])],
        (up, down, rows, *blocks),
        flops=LONG,
    )[0]


def embed_rows_kernel(embed_ref, rows_ref, *outs):
    embedded = dot(rows_ref[...], embed_ref[...])
    for i, out in enumerate(outs):
        out[...] = embedded[i * SHARE : (i + 1) * SHARE].astype(bf16)


def sum_kernel(*refs):
    parts, (sums_ref, tail_ref) = refs[:-2], refs[-2:]
    total = parts[0][...].astype(f32)
    for part in parts[1:]:
        total += part[...].astype(f32)
    sums_ref[...] = total.astype(bf16)
    tail_ref[...] = total[SMALLEST:, :].astype(bf16)


def decode_kernel(
    visible_ref,
    keep_ref,
    targets_ref,
    mask_ref,
    position_ref,
    qkv_ref,
    out_ref,
    pred_ref,
    sums_ref,
    tail_ref,
    recon_ref,
    loss_ref,
    flat,
    errors,
):
    patch_count = position_ref.shape[0]
    patch = lax.broadcasted_iota(jnp.int32, (patch_count, patch_count), 0)
    slot = lax.broadcasted_iota(jnp.int32, (patch_count, patch_count), 1)
    chosen = ((keep_ref[...] == patch) & (slot < visible_ref[0])).astype(f32)
    seen = jnp.max(chosen, axis=1, keepdims=True)
    slots = chosen.astype(bf16)[:, :SHARE]
    late = jnp.where(slot >= SHARE, chosen, 0.0)
    moved = pltpu.roll(late, patch_count + VMAX - SHARE - visible_ref[0], 1)
    picked = dot(slots, sums_ref[...]) + dot(moved.astype(bf16)[:, : VMAX - SHARE], tail_ref[...])
    start = jnp.where(seen > 0, picked, mask_ref[...].astype(f32)) + position_ref[...].astype(f32)
    projections = dot(layer_norm(start).astype(bf16), qkv_ref[...]).astype(bf16)
    scale = 1.0 / math.sqrt(HSIZE)
    pair = LANES // HSIZE
    column = lax.broadcasted_iota(jnp.int32, (patch_count, LANES), 1) // HSIZE
    masks = [((column == i).astype(f32) * scale).astype(bf16) for i in range(pair)]
    values = projections[:, 2 * DD :].astype(f32).T.astype(bf16)
    mixed = []
    for first in range(0, DD, LANES):
        query = projections[:, first : first + LANES]
        query = jnp.concatenate([query * mask for mask in masks], axis=0)
        key = projections[:, DD + first : DD + first + LANES]
        scores = lax.dot_general(
            key, query, (((1,), (1,)), ((), ())), preferred_element_type=f32
        )
        weights = jnp.exp(scores - jnp.max(scores, axis=0, keepdims=True))
        total = 1.0 / jnp.sum(weights, axis=0, keepdims=True)
        weights = weights.astype(bf16)
        for i in range(pair):
            head = slice(first + i * HSIZE, first + (i + 1) * HSIZE)
            mine = slice(i * patch_count, (i + 1) * patch_count)
            mixed.append(dot(values[head, :], weights[:, mine]) * total[:, mine])
    mixed = jnp.concatenate(mixed, axis=0).astype(bf16)
    after = start + lax.dot_general(mixed, out_ref[...], (((0,), (0,)), ((), ())), preferred_element_type=f32)
    prediction = dot(layer_norm(after).astype(bf16), pred_ref[...])
    group = 4
    wide = group * PIX
    flat[:, :PIX] = prediction[:, :PIX]
    lines = patch_count // group
    together = jnp.concatenate(
        [flat[pl.ds(i, lines, stride=group), :][:, :PIX] for i in range(group)], axis=1
    )
    for line in range(lines):
        place = slice(line * wide, (line + 1) * wide)
        recon_ref[:, place] = together[line : line + 1, :].astype(bf16)
        errors[line : line + 1, :] = together[line : line + 1, :] - targets_ref[:, place].astype(f32)
    squares = errors[...] * errors[...]
    for i in range(group):
        flat[pl.ds(i, lines, stride=group), :PIX] = squares[:, i * PIX : (i + 1) * PIX]
    loss = jnp.sum(flat[:, :PIX], axis=1, keepdims=True) * (1.0 / PIX)
    loss = jnp.where(seen > 0, 0.0, loss)
    loss_ref[...] = jnp.sum(jnp.where(patch == slot, loss, 0.0), axis=0, keepdims=True)


def body(
    dp,
    mp,
    patches,
    keep_index,
    visible,
    targets,
    w_up,
    w_down,
    dec_embed,
    dec_qkv,
    dec_out,
    dec_pred,
    mask_token,
    position,
):
    _, patch_count, width = patches.shape
    fold, piece = dec_embed.shape[0] // dec_qkv.shape[0], dec_qkv.shape[0] // dp
    in_pieces = (dp, mp) == (8, 4) and piece % 16 == 0
    pred_columns = dec_pred.T
    order = (1, *range(mp - 1, 1, -1))
    over_mp = lambda a, k: xor_permute(a, "mp", mp, k)
    over_dp = lambda a, bit: xor_permute(a, "dp", dp, bit)
    columns = (fold * DD, DD + dec_qkv.shape[1] + LANES)
    shards = (dec_embed, dec_qkv, dec_out, pred_columns)
    keep_index, patches, tail, *part = begin(
        keep_index, patches, shards if in_pieces else (), columns
    )
    tail = over_dp(tail, dp // 2)
    if in_pieces:
        second, third = over_mp(part[1], 2), over_mp(part[2], 3)
        (traded,) = call(trade_kernel, "trade", [near(piece, sum(columns))], (second, third), after=(tail,))
        first = over_mp(part[0], 1)
        fence = (traded,)
    else:
        fence = ()
    rows, normed = call(
        rows_kernel,
        "select_rows",
        [near(SHARE, width)] * 2,
        (visible, keep_index, patches, tail),
        after=fence,
    )
    others = {k: over_mp(normed, k) for k in order}
    if in_pieces:
        embed, rest = call(
            split_kernel,
            "split",
            [near((mp - 1) * fold * piece, DD), near((mp - 1) * piece, columns[1])],
            (first, second, third, over_mp(traded, 1)),
            flops=LONG,
            after=(normed,),
        )
        embeds = [embed] + [over_dp(embed, bit) for bit in PLANE[1:]]
        rests = join("join_near", [rest, over_dp(rest, PLANE[1])])
    else:
        full_embed, *weights = [
            lax.all_gather(w, "mp", axis=0, tiled=True) for w in (dec_embed, dec_qkv, dec_out, dec_pred)
        ]
    partial = encode(w_up, w_down, rows, (normed, *[others[k] for k in order]))
    if in_pieces:
        embeds.append(over_dp(join("join_embed", embeds, LONG, (rests, *others.values())), 1))
        (full_embed,) = call(
            functools.partial(embed_kernel, mp, fold * piece),
            "full_embed",
            [near(mp * dec_embed.shape[0], DD)],
            (shards[0], *embeds),
        )
    out, *sent = call(
        embed_rows_kernel,
        "embed_rows",
        [near(SHARE, DD)] * mp,
        (full_embed, partial),
        flops=2 * mp * SHARE * width * DD,
    )
    back = [over_mp(s, k) for k, s in zip(order, sent)]
    sums, own_tail = call(
        sum_kernel, "add_up", [near(SHARE, DD), near(SHARE - SMALLEST, DD)], (out, *back)
    )
    if in_pieces:
        rests = join("join_rest", [rests, over_dp(rests, PLANE[2])], after=(sums,))
        rests = (rests, over_dp(rests, 1))
        weights = call(
            functools.partial(decoder_weights_kernel, mp, piece),
            "decoder_weights",
            [near(mp * w.shape[0], w.shape[1]) for w in (dec_qkv, dec_out, dec_pred)],
            (*shards[1:], *rests),
        )
    return call(
        decode_kernel,
        "decode",
        [
            jax.ShapeDtypeStruct(targets.shape, bf16),
            jax.ShapeDtypeStruct((1, patch_count), f32),
        ],
        (
            visible,
            keep_index,
            targets,
            mask_token[None],
            position,
            *weights,
            sums,
            over_dp(own_tail, dp // 2),
        ),
        flops=10 * patch_count * DD * DD,
        scratch=[pltpu.VMEM((patch_count, LANES), f32), pltpu.VMEM((patch_count // 4, 4 * PIX), f32)],
    )


def solution(mesh):
    return jax.shard_map(
        functools.partial(body, mesh.shape["dp"], mesh.shape["mp"]),
        mesh=mesh,
        in_specs=(
            P(("dp", "mp"), None, None),
            P(("dp", "mp"), None),
            P(("dp", "mp")),
            P(("dp", "mp"), None),
            P(None, "mp"),
            P("mp", None),
            P("mp", None),
            P("mp", None),
            P("mp", None),
            P("mp", None),
            P(),
            P(),
        ),
        out_specs=(P(("dp", "mp"), None), P(("dp", "mp"), None)),
        check_vma=False,
    )
```

```python
import functools
import math

import jax
import jax.numpy as jnp
from jax import lax
from jax.experimental import pallas as pl
from jax.experimental.pallas import tpu as pltpu
from jax.sharding import PartitionSpec as P

DD = 512
HSIZE = 64
PIX = 96
VMAX = 80
SHARE = 48
SMALLEST = 2 * SHARE - VMAX
LANES = 128
EPSILON = 1e-06
LIMIT = 14 << 20
LONG = 10**11

f32 = jnp.float32
bf16 = jnp.bfloat16
VMEM = pl.BlockSpec(memory_space=pltpu.VMEM)
SMEM = pl.BlockSpec(memory_space=pltpu.SMEM)
HBM = pl.BlockSpec(memory_space=pltpu.HBM)


def dot(left, right):
    return jnp.dot(left, right, preferred_element_type=f32)


def layer_norm(values):
    center = values - jnp.mean(values, axis=-1, keepdims=True)
    spread = jnp.mean(center * center, axis=-1, keepdims=True)
    return center * lax.rsqrt(spread + EPSILON)


def cost(flops, size):
    return pl.CostEstimate(flops=flops, bytes_accessed=size, transcendentals=0)


def stay(array):
    return pltpu.with_memory_space_constraint(array, pltpu.HBM)


def call(kernel, name, outs, ins, flops=0, scratch=(), after=()):
    count = len(ins)

    def run(*refs):
        kernel(*refs[:count], *refs[count + len(after) :])

    size = sum(2 * math.prod(a.shape) for a in (*ins, *outs)) if flops >= 0 else 0
    return pl.pallas_call(
        run,
        out_shape=outs,
        in_specs=[SMEM if a.ndim == 1 else VMEM for a in ins]
        + [pl.BlockSpec(memory_space=pl.ANY)] * len(after),
        out_specs=[VMEM] * len(outs),
        scratch_shapes=scratch,
        compiler_params=pltpu.CompilerParams(vmem_limit_bytes=LIMIT),
        cost_estimate=cost(max(flops, 0), size),
        name=name,
    )(*ins, *after)


def near(*shape, dtype=bf16):
    return pltpu.VMEM(shape, dtype)


def xor_permute(values, axis, size, bit):
    return lax.ppermute(values, axis, [(i, i ^ bit) for i in range(size)])


def pick(chosen, values):
    return lax.dot_general(chosen, values, (((0,), (0,)), ((), ())), preferred_element_type=f32)


def rows_kernel(visible_ref, keep_ref, patches_ref, tail_ref, rows_ref, normed_ref):
    patch_count = patches_ref.shape[0]
    visible = visible_ref[0]
    square = (patch_count, patch_count)
    patch = lax.broadcasted_iota(jnp.int32, square, 0)
    slot = lax.broadcasted_iota(jnp.int32, square, 1)
    own = ((keep_ref[...] == patch) & (slot < visible)).astype(f32).astype(bf16)[:, :SHARE]
    other = (slot - visible == patch).astype(f32).astype(bf16)[: VMAX - SHARE, :SHARE]
    rows = pick(own, patches_ref[...]) + pick(other, tail_ref[...])
    rows_ref[...] = rows.astype(bf16)
    normed_ref[...] = layer_norm(rows).astype(bf16)


def begin_kernel(keep_in, patches_ref, *refs):
    if len(refs) > 5:
        weights, (keep_ref, rows_ref, tail_ref, part_ref, pred, sems) = refs[:4], refs[4:]
    else:
        weights, (keep_ref, rows_ref, tail_ref, sems) = (), refs
    copies = [
        pltpu.make_async_copy(patches_ref.at[0], rows_ref, sems.at[0]),
        pltpu.make_async_copy(keep_in, keep_ref, sems.at[1]),
    ]
    if weights:
        embed_ref, qkv_ref, out_ref, pred_ref = weights
        j = lax.axis_index("dp")
        count, wide = part_ref.shape[0], qkv_ref.shape[1]
        fold = embed_ref.shape[0] // qkv_ref.shape[0]
        own = pl.ds(pl.multiple_of(j * count, 16), count)
        start = fold * DD
        moves = [(pred_ref, pred)]
        for i in range(fold):
            rows = pl.ds(pl.multiple_of((j * fold + i) * count, 16), count)
            moves.append((embed_ref.at[rows, :], part_ref.at[:, i * DD : (i + 1) * DD]))
        moves.append((qkv_ref.at[own, :], part_ref.at[:, start : start + wide]))
        moves.append((out_ref.at[own, :], part_ref.at[:, start + wide : start + wide + DD]))
        copies += [pltpu.make_async_copy(x, y, sems.at[i]) for i, (x, y) in enumerate(moves, 2)]
    for copy in copies:
        copy.start()
    for copy in copies:
        copy.wait()
    if weights:
        columns = pick_columns(pred[...], j * count, count)
        last = start + wide + DD
        part_ref[:, last:] = jnp.zeros((count, LANES), bf16)
        part_ref[:, last : last + PIX] = columns.astype(bf16)
    patch_count = rows_ref.shape[0]
    patch = lax.broadcasted_iota(jnp.int32, (patch_count, patch_count), 0)
    chosen = (keep_ref[...] == patch).astype(f32).astype(bf16)[:, SHARE:VMAX]
    tail_ref[...] = pick(chosen, rows_ref[...]).astype(bf16)


def pick_columns(values, first, count):
    shape = (count, values.shape[1])
    place = lax.broadcasted_iota(jnp.int32, shape, 1) - lax.broadcasted_iota(jnp.int32, shape, 0)
    return lax.dot_general(
        (place == first).astype(f32).astype(bf16), values, (((1,), (1,)), ((), ())), preferred_element_type=f32
    )


def begin(keep_index, patches, weights, columns):
    _, patch_count, width = patches.shape
    arrays = (keep_index, patches, *weights)
    outs = [near(*keep_index.shape, dtype=jnp.int32), near(patch_count, width), near(VMAX - SHARE, width)]
    scratch = []
    if weights:
        outs.append(near(weights[1].shape[0] // 8, columns))
        scratch.append(pltpu.VMEM(weights[3].shape, bf16))
    return pl.pallas_call(
        begin_kernel,
        out_shape=outs,
        in_specs=[HBM] * len(arrays),
        out_specs=[VMEM] * len(outs),
        scratch_shapes=scratch + [pltpu.SemaphoreType.DMA((9,))],
        compiler_params=pltpu.CompilerParams(vmem_limit_bytes=LIMIT),
        cost_estimate=cost(0, 2 * patch_count * width),
        name="begin",
    )(*[stay(a) for a in arrays])


def relay_kernel(in_ref, out_ref):
    out_ref[...] = in_ref[...]


def relay(name, values, flops=0, after=()):
    return call(relay_kernel, name, [near(*values.shape)], (values,), flops, after=after)[0]


def hold(name, after):
    return call(hold_kernel, name, [near(16, LANES)], (), LONG, after=after)[0]


def hold_kernel(out_ref):
    out_ref[...] = jnp.zeros(out_ref.shape, bf16)


def split_kernel(*refs):
    parts, (embed_ref, rest_ref) = refs[:-2], refs[-2:]
    count, wide = parts[0].shape[0], rest_ref.shape[1]
    fold = (parts[0].shape[1] - wide) // DD
    for k, part in enumerate(parts):
        for i in range(fold):
            place = (k * fold + i) * count
            embed_ref[place : place + count, :] = part[:, i * DD : (i + 1) * DD]
        rest_ref[k * count : (k + 1) * count, :] = part[:, fold * DD :]


def join_kernel(*refs):
    parts, out_ref = refs[:-1], refs[-1]
    count = parts[0].shape[0]
    for i, part in enumerate(parts):
        out_ref[i * count : (i + 1) * count, :] = part[...]


def join(name, parts, flops=0, after=()):
    rows, columns = parts[0].shape
    return call(join_kernel, name, [near(len(parts) * rows, columns)], parts, flops, after=after)[0]


PLANE = (0, 2, 4, 6)


def by_core(values, even, odd, size):
    return lax.ppermute(values, "dp", [(i, i ^ (odd if i & 1 else even)) for i in range(size)])


def plane_gather(name, own, size, after=()):
    (pair,) = call(
        join_kernel, f"pair_{name}", [near(2 * own.shape[0], own.shape[1])], (own, by_core(own, 2, 4, size)), after=after
    )
    other = xor_permute(pair, "dp", size, 1)
    return pair, other, by_core(other, 2, 4, size)


def direct_owners(j):
    return *[(j ^ i,) for i in PLANE], [j ^ i ^ 1 for i in PLANE]


def gathered_owners(j):
    side = 2 + 2 * (j & 1)
    return (j, j ^ side), (j ^ 1, j ^ 7 ^ side), (j ^ 1 ^ side, j ^ 7), (j ^ 6 ^ side, j ^ 6)


def assemble(refs, owners, own_rows, mp, piece, write):
    m = lax.axis_index("mp")
    write(pl.multiple_of(m * own_rows, 16), own_rows, None, 0)
    count = (mp - 1) * piece
    for source, devices in zip(refs, owners(lax.axis_index("dp"))):
        for block, owner in enumerate(devices):
            for k in range(1, mp):
                row = (m ^ k) * own_rows + owner * piece
                write(pl.multiple_of(row, 16), piece, source, block * count + (k - 1) * piece)


def embed_kernel(mp, piece, own_ref, *rest):
    refs, full = rest[:-1], rest[-1]

    def write(row, count, source, base):
        if source is None:
            full[pl.ds(row, count), :] = own_ref[...]
        else:
            full[pl.ds(row, count), :] = source[base : base + count, :]

    assemble(refs, direct_owners, own_ref.shape[0], mp, piece, write)


def decoder_weights_kernel(mp, piece, qkv_ref, out_ref, pred_ref, *rest):
    refs, (full_qkv, full_out, full_pred) = rest[:-3], rest[-3:]
    wide = full_qkv.shape[1]

    def write(row, count, source, base):
        place = pl.ds(row, count)
        if source is None:
            full_qkv[place, :] = qkv_ref[...]
            full_out[place, :] = out_ref[...]
            full_pred[place, :PIX] = pred_ref[...].astype(f32).T.astype(bf16)
        else:
            part = pl.ds(base, count)
            full_qkv[place, :] = source[part, :wide]
            full_out[place, :] = source[part, wide : wide + DD]
            full_pred[place, :PIX] = source[part, wide + DD : wide + DD + PIX]

    assemble(refs, gathered_owners, qkv_ref.shape[0], mp, piece, write)


def encode_kernel(own, up_ref, down_ref, *rest):
    blocks, partial_ref = rest[own:-1], rest[-1]
    rows = jnp.concatenate([r[...] for r in blocks], axis=0)
    hidden = up_ref.shape[1]
    tile = 256 if hidden % 256 == 0 else hidden
    total = None
    for i in range(0, hidden, tile):
        units = jax.nn.gelu(dot(rows, up_ref[:, i : i + tile]), approximate=True).astype(bf16)
        term = dot(units, down_ref[i : i + tile, :])
        total = term if total is None else total + term
    if own:
        partial_ref[:SHARE, :] = (rest[0][...].astype(f32) + total[:SHARE]).astype(bf16)
        partial_ref[SHARE:, :] = total[SHARE:].astype(bf16)
    else:
        partial_ref[...] = total.astype(bf16)


def encode(name, up, down, blocks, rows=None, flops=0, after=()):
    own = () if rows is None else (rows,)
    return call(
        functools.partial(encode_kernel, len(own)),
        name,
        [near(len(blocks) * SHARE, up.shape[0])],
        (up, down, *own, *blocks),
        flops,
        after=after,
    )[0]


def embed_rows_kernel(embed_ref, *refs):
    partials = [ref for ref in refs if ref.shape[1] == embed_ref.shape[0]]
    outs = refs[len(partials) :]
    rows = jnp.concatenate([p[...] for p in partials], axis=0)
    embedded = dot(rows, embed_ref[...]).astype(bf16)
    blocks = [embedded[i : i + SHARE] for i in range(0, rows.shape[0], SHARE)]
    if len(partials) == 2:
        blocks = [blocks[0], blocks[2], blocks[1], blocks[3]]
    for out, block in zip(outs, blocks):
        out[...] = block


def sum_kernel(*refs):
    parts, (sums_ref, tail_ref) = refs[:-2], refs[-2:]
    total = parts[0][...].astype(f32)
    for part in parts[1:]:
        total += part[...].astype(f32)
    sums_ref[...] = total.astype(bf16)
    tail_ref[...] = total[SMALLEST:, :].astype(bf16)


def decode_kernel(
    visible_ref,
    keep_ref,
    targets_ref,
    mask_ref,
    position_ref,
    qkv_ref,
    out_ref,
    pred_ref,
    sums_ref,
    tail_ref,
    recon_ref,
    loss_ref,
    flat,
    errors,
):
    patch_count = position_ref.shape[0]
    patch = lax.broadcasted_iota(jnp.int32, (patch_count, patch_count), 0)
    slot = lax.broadcasted_iota(jnp.int32, (patch_count, patch_count), 1)
    chosen = ((keep_ref[...] == patch) & (slot < visible_ref[0])).astype(f32)
    seen = jnp.max(chosen, axis=1, keepdims=True)
    slots = chosen.astype(bf16)[:, :SHARE]
    late = jnp.where(slot >= SHARE, chosen, 0.0)
    moved = pltpu.roll(late, patch_count + VMAX - SHARE - visible_ref[0], 1)
    picked = dot(slots, sums_ref[...]) + dot(moved.astype(bf16)[:, : VMAX - SHARE], tail_ref[...])
    start = jnp.where(seen > 0, picked, mask_ref[...].astype(f32)) + position_ref[...].astype(f32)
    projections = dot(layer_norm(start).astype(bf16), qkv_ref[...]).astype(bf16)
    scale = 1.0 / math.sqrt(HSIZE)
    pair = LANES // HSIZE
    column = lax.broadcasted_iota(jnp.int32, (patch_count, LANES), 1) // HSIZE
    masks = [((column == i).astype(f32) * scale).astype(bf16) for i in range(pair)]
    values = projections[:, 2 * DD :].astype(f32).T.astype(bf16)
    mixed = []
    for first in range(0, DD, LANES):
        query = projections[:, first : first + LANES]
        query = jnp.concatenate([query * mask for mask in masks], axis=0)
        key = projections[:, DD + first : DD + first + LANES]
        scores = lax.dot_general(
            key, query, (((1,), (1,)), ((), ())), preferred_element_type=f32
        )
        weights = jnp.exp(scores - jnp.max(scores, axis=0, keepdims=True))
        total = 1.0 / jnp.sum(weights, axis=0, keepdims=True)
        weights = weights.astype(bf16)
        for i in range(pair):
            head = slice(first + i * HSIZE, first + (i + 1) * HSIZE)
            mine = slice(i * patch_count, (i + 1) * patch_count)
            mixed.append(dot(values[head, :], weights[:, mine]) * total[:, mine])
    mixed = jnp.concatenate(mixed, axis=0).astype(bf16)
    after = start + lax.dot_general(mixed, out_ref[...], (((0,), (0,)), ((), ())), preferred_element_type=f32)
    prediction = dot(layer_norm(after).astype(bf16), pred_ref[...])
    group = 4
    wide = group * PIX
    flat[:, :PIX] = prediction[:, :PIX]
    lines = patch_count // group
    together = jnp.concatenate(
        [flat[pl.ds(i, lines, stride=group), :][:, :PIX] for i in range(group)], axis=1
    )
    for line in range(lines):
        place = slice(line * wide, (line + 1) * wide)
        recon_ref[:, place] = together[line : line + 1, :].astype(bf16)
        errors[line : line + 1, :] = together[line : line + 1, :] - targets_ref[:, place].astype(f32)
    squares = errors[...] * errors[...]
    for i in range(group):
        flat[pl.ds(i, lines, stride=group), :PIX] = squares[:, i * PIX : (i + 1) * PIX]
    loss = jnp.sum(flat[:, :PIX], axis=1, keepdims=True) * (1.0 / PIX)
    loss = jnp.where(seen > 0, 0.0, loss)
    loss_ref[...] = jnp.sum(jnp.where(patch == slot, loss, 0.0), axis=0, keepdims=True)


def body(
    dp,
    mp,
    patches,
    keep_index,
    visible,
    targets,
    w_up,
    w_down,
    dec_embed,
    dec_qkv,
    dec_out,
    dec_pred,
    mask_token,
    position,
):
    _, patch_count, width = patches.shape
    fold, piece = dec_embed.shape[0] // dec_qkv.shape[0], dec_qkv.shape[0] // dp
    in_pieces = (dp, mp) == (8, 4) and piece % 16 == 0
    pred_columns = dec_pred.T
    over_mp = lambda a, k: xor_permute(a, "mp", mp, k)
    over_dp = lambda a, bit: xor_permute(a, "dp", dp, bit)
    wide = DD + dec_qkv.shape[1] + LANES
    shards = (dec_embed, dec_qkv, dec_out, pred_columns)
    keep_index, patches, tail, *part = begin(
        keep_index, patches, shards if in_pieces else (), fold * DD + wide
    )
    tail = over_dp(tail, dp // 2)
    fence = ()
    if in_pieces:
        parts = [over_mp(part[0], 1), over_mp(part[0], 2)]
        passed = relay("pass_part", parts[1], after=(tail,))
        parts.append(over_mp(passed, 1))
        embed, rest = call(
            split_kernel,
            "split",
            [near((mp - 1) * fold * piece, DD), near((mp - 1) * piece, wide)],
            parts,
        )
        fence = (embed,)
    rows, normed = call(
        rows_kernel,
        "select_rows",
        [near(SHARE, width)] * 2,
        (visible, keep_index, patches, tail),
        LONG,
        after=fence,
    )
    if in_pieces:
        others = [over_mp(normed, 1), over_mp(normed, 2)]
        embeds = [embed] + [over_dp(embed, bit) for bit in PLANE[1:]]
        passed = relay("pass_rows", others[1], LONG, (w_up, w_down, embed))
        others.append(over_mp(passed, 1))
        partials = [
            encode("encode_near", w_up, w_down, (normed, passed), rows, -1, (passed,)),
            encode("encode", w_up, w_down, (others[0], others[2]), flops=LONG),
        ]
        rests = plane_gather("rest", rest, dp, partials[:1])
    else:
        full_embed, *weights = [
            lax.all_gather(w, "mp", axis=0, tiled=True) for w in (dec_embed, dec_qkv, dec_out, dec_pred)
        ]
        others = [over_mp(normed, k) for k in range(1, mp)]
        partials = [encode("encode", w_up, w_down, (normed, *others), rows)]
    if in_pieces:
        embeds.append(over_dp(join("join_embed", embeds, after=partials[:1]), 1))
        (full_embed,) = call(
            functools.partial(embed_kernel, mp, fold * piece),
            "full_embed",
            [near(mp * dec_embed.shape[0], DD)],
            (shards[0], *embeds),
        )
    out, *sent = call(
        embed_rows_kernel,
        "embed_rows",
        [near(SHARE, DD)] * mp,
        (full_embed, *partials),
        flops=LONG,
    )
    back = [over_mp(sent[k - 1], k) for k in range(mp - 1, 0, -1)]
    sums, own_tail = call(
        sum_kernel, "add_up", [near(SHARE, DD), near(SHARE - SMALLEST, DD)], (out, *back)
    )
    if in_pieces:
        rests = (*rests, over_dp(relay("pass_rest", rests[2], after=(sums,)), 1))
        weights = call(
            functools.partial(decoder_weights_kernel, mp, piece),
            "decoder_weights",
            [near(mp * w.shape[0], w.shape[1]) for w in (dec_qkv, dec_out, dec_pred)],
            (*shards[1:], *rests),
        )
    return call(
        decode_kernel,
        "decode",
        [
            jax.ShapeDtypeStruct(targets.shape, bf16),
            jax.ShapeDtypeStruct((1, patch_count), f32),
        ],
        (
            visible,
            keep_index,
            targets,
            mask_token[None],
            position,
            *weights,
            sums,
            over_dp(own_tail, dp // 2),
        ),
        flops=10 * patch_count * DD * DD,
        scratch=[pltpu.VMEM((patch_count, LANES), f32), pltpu.VMEM((patch_count // 4, 4 * PIX), f32)],
    )


def solution(mesh):
    return jax.shard_map(
        functools.partial(body, mesh.shape["dp"], mesh.shape["mp"]),
        mesh=mesh,
        in_specs=(
            P(("dp", "mp"), None, None),
            P(("dp", "mp"), None),
            P(("dp", "mp")),
            P(("dp", "mp"), None),
            P(None, "mp"),
            P("mp", None),
            P("mp", None),
            P("mp", None),
            P("mp", None),
            P("mp", None),
            P(),
            P(),
        ),
        out_specs=(P(("dp", "mp"), None), P(("dp", "mp"), None)),
        check_vma=False,
    )
```

```python
import functools
import math

import jax
import jax.numpy as jnp
from jax import lax
from jax.experimental import pallas as pl
from jax.experimental.pallas import tpu as pltpu
from jax.sharding import PartitionSpec as P

DD = 512
HSIZE = 64
PIX = 96
VMAX = 80
SHARE = 48
SMALLEST = 2 * SHARE - VMAX
LANES = 128
EPSILON = 1e-06
LIMIT = 14 << 20
LONG = 10**11

f32 = jnp.float32
bf16 = jnp.bfloat16
VMEM = pl.BlockSpec(memory_space=pltpu.VMEM)
SMEM = pl.BlockSpec(memory_space=pltpu.SMEM)
HBM = pl.BlockSpec(memory_space=pltpu.HBM)


def dot(left, right):
    return jnp.dot(left, right, preferred_element_type=f32)


def layer_norm(values):
    center = values - jnp.mean(values, axis=-1, keepdims=True)
    spread = jnp.mean(center * center, axis=-1, keepdims=True)
    return center * lax.rsqrt(spread + EPSILON)


def cost(flops, size):
    return pl.CostEstimate(flops=flops, bytes_accessed=size, transcendentals=0)


def stay(array):
    return pltpu.with_memory_space_constraint(array, pltpu.HBM)


def call(kernel, name, outs, ins, flops=0, scratch=(), after=()):
    count = len(ins)

    def run(*refs):
        kernel(*refs[:count], *refs[count + len(after) :])

    size = sum(2 * math.prod(a.shape) for a in (*ins, *outs)) if flops >= 0 else 0
    return pl.pallas_call(
        run,
        out_shape=outs,
        in_specs=[SMEM if a.ndim == 1 else VMEM for a in ins]
        + [pl.BlockSpec(memory_space=pl.ANY)] * len(after),
        out_specs=[VMEM] * len(outs),
        scratch_shapes=scratch,
        compiler_params=pltpu.CompilerParams(vmem_limit_bytes=LIMIT),
        cost_estimate=cost(max(flops, 0), size),
        name=name,
    )(*ins, *after)


def near(*shape, dtype=bf16):
    return pltpu.VMEM(shape, dtype)


def xor_permute(values, axis, size, bit):
    return lax.ppermute(values, axis, [(i, i ^ bit) for i in range(size)])


def pick(chosen, values):
    return lax.dot_general(chosen, values, (((0,), (0,)), ((), ())), preferred_element_type=f32)


def rows_kernel(visible_ref, keep_ref, patches_ref, tail_ref, rows_ref, normed_ref):
    patch_count = patches_ref.shape[0]
    visible = visible_ref[0]
    square = (patch_count, patch_count)
    patch = lax.broadcasted_iota(jnp.int32, square, 0)
    slot = lax.broadcasted_iota(jnp.int32, square, 1)
    own = ((keep_ref[...] == patch) & (slot < visible)).astype(f32).astype(bf16)[:, :SHARE]
    other = (slot - visible == patch).astype(f32).astype(bf16)[: VMAX - SHARE, :SHARE]
    rows = pick(own, patches_ref[...]) + pick(other, tail_ref[...])
    rows_ref[...] = rows.astype(bf16)
    normed_ref[...] = layer_norm(rows).astype(bf16)


def run_copies(moves, sems):
    copies = [pltpu.make_async_copy(x, y, sems.at[i]) for i, (x, y) in enumerate(moves)]
    for copy in copies:
        copy.start()
    for copy in copies:
        copy.wait()


def part_kernel(embed_ref, qkv_ref, out_ref, pred_ref, part_ref, pred, sems):
    j = lax.axis_index("dp")
    count, wide = part_ref.shape[0], qkv_ref.shape[1]
    fold = embed_ref.shape[0] // qkv_ref.shape[0]
    own = pl.ds(pl.multiple_of(j * count, 16), count)
    start = fold * DD
    moves = [(pred_ref, pred)]
    for i in range(fold):
        rows = pl.ds(pl.multiple_of((j * fold + i) * count, 16), count)
        moves.append((embed_ref.at[rows, :], part_ref.at[:, i * DD : (i + 1) * DD]))
    moves.append((qkv_ref.at[own, :], part_ref.at[:, start : start + wide]))
    moves.append((out_ref.at[own, :], part_ref.at[:, start + wide : start + wide + DD]))
    run_copies(moves, sems)
    columns = pick_columns(pred[...], j * count, count)
    last = start + wide + DD
    part_ref[:, last:] = jnp.zeros((count, LANES), bf16)
    part_ref[:, last : last + PIX] = columns.astype(bf16)


def tail_kernel(keep_in, patches_ref, keep_ref, rows_ref, tail_ref, sems):
    run_copies([(patches_ref.at[0], rows_ref), (keep_in, keep_ref)], sems)
    patch_count = rows_ref.shape[0]
    patch = lax.broadcasted_iota(jnp.int32, (patch_count, patch_count), 0)
    chosen = (keep_ref[...] == patch).astype(f32).astype(bf16)[:, SHARE:VMAX]
    tail_ref[...] = pick(chosen, rows_ref[...]).astype(bf16)


def pick_columns(values, first, count):
    shape = (count, values.shape[1])
    place = lax.broadcasted_iota(jnp.int32, shape, 1) - lax.broadcasted_iota(jnp.int32, shape, 0)
    return lax.dot_general(
        (place == first).astype(f32).astype(bf16), values, (((1,), (1,)), ((), ())), preferred_element_type=f32
    )


def call_on_hbm(kernel, name, outs, ins, scratch, after=()):
    def run(*refs):
        kernel(*refs[: len(ins)], *refs[len(ins) + len(after) :])

    return pl.pallas_call(
        run,
        out_shape=outs,
        in_specs=[HBM] * len(ins) + [pl.BlockSpec(memory_space=pl.ANY)] * len(after),
        out_specs=[VMEM] * len(outs),
        scratch_shapes=scratch,
        compiler_params=pltpu.CompilerParams(vmem_limit_bytes=LIMIT),
        cost_estimate=cost(0, 2 * max(a.size for a in ins)),
        name=name,
    )(*[stay(a) for a in ins], *after)


def relay_kernel(in_ref, out_ref):
    out_ref[...] = in_ref[...]


def relay(name, values, flops=0, after=()):
    return call(relay_kernel, name, [near(*values.shape)], (values,), flops, after=after)[0]


def hold(name, after):
    return call(hold_kernel, name, [near(16, LANES)], (), LONG, after=after)[0]


def hold_kernel(out_ref):
    out_ref[...] = jnp.zeros(out_ref.shape, bf16)


def split_kernel(*refs):
    parts, (embed_ref, rest_ref) = refs[:-2], refs[-2:]
    count, wide = parts[0].shape[0], rest_ref.shape[1]
    fold = (parts[0].shape[1] - wide) // DD
    for k, part in enumerate(parts):
        for i in range(fold):
            place = (k * fold + i) * count
            embed_ref[place : place + count, :] = part[:, i * DD : (i + 1) * DD]
        rest_ref[k * count : (k + 1) * count, :] = part[:, fold * DD :]


def join_kernel(*refs):
    parts, out_ref = refs[:-1], refs[-1]
    count = parts[0].shape[0]
    for i, part in enumerate(parts):
        out_ref[i * count : (i + 1) * count, :] = part[...]


def join(name, parts, flops=0, after=()):
    rows, columns = parts[0].shape
    return call(join_kernel, name, [near(len(parts) * rows, columns)], parts, flops, after=after)[0]


PLANE = (0, 2, 4, 6)


def by_core(values, even, odd, size):
    return lax.ppermute(values, "dp", [(i, i ^ (odd if i & 1 else even)) for i in range(size)])


def plane_gather(name, own, size, after=()):
    (pair,) = call(
        join_kernel, f"pair_{name}", [near(2 * own.shape[0], own.shape[1])], (own, by_core(own, 2, 4, size)), after=after
    )
    other = xor_permute(pair, "dp", size, 1)
    return pair, other, by_core(other, 2, 4, size)


def direct_owners(j):
    return *[(j ^ i,) for i in PLANE], [j ^ i ^ 1 for i in PLANE]


def gathered_owners(j):
    side = 2 + 2 * (j & 1)
    return (j, j ^ side), (j ^ 1, j ^ 7 ^ side), (j ^ 1 ^ side, j ^ 7), (j ^ 6 ^ side, j ^ 6)


def assemble(refs, owners, own_rows, mp, piece, write):
    m = lax.axis_index("mp")
    write(pl.multiple_of(m * own_rows, 16), own_rows, None, 0)
    count = (mp - 1) * piece
    for source, devices in zip(refs, owners(lax.axis_index("dp"))):
        for block, owner in enumerate(devices):
            for k in range(1, mp):
                row = (m ^ k) * own_rows + owner * piece
                write(pl.multiple_of(row, 16), piece, source, block * count + (k - 1) * piece)


def embed_kernel(mp, piece, own_ref, *rest):
    refs, full = rest[:-1], rest[-1]

    def write(row, count, source, base):
        if source is None:
            full[pl.ds(row, count), :] = own_ref[...]
        else:
            full[pl.ds(row, count), :] = source[base : base + count, :]

    assemble(refs, direct_owners, own_ref.shape[0], mp, piece, write)


def decoder_weights_kernel(mp, piece, qkv_ref, out_ref, pred_ref, *rest):
    refs, (full_qkv, full_out, full_pred) = rest[:-3], rest[-3:]
    wide = full_qkv.shape[1]

    def write(row, count, source, base):
        place = pl.ds(row, count)
        if source is None:
            full_qkv[place, :] = qkv_ref[...]
            full_out[place, :] = out_ref[...]
            full_pred[place, :PIX] = pred_ref[...].astype(f32).T.astype(bf16)
        else:
            part = pl.ds(base, count)
            full_qkv[place, :] = source[part, :wide]
            full_out[place, :] = source[part, wide : wide + DD]
            full_pred[place, :PIX] = source[part, wide + DD : wide + DD + PIX]

    assemble(refs, gathered_owners, qkv_ref.shape[0], mp, piece, write)


def encode_kernel(own, up_ref, down_ref, *rest):
    blocks, partial_ref = rest[own:-1], rest[-1]
    rows = jnp.concatenate([r[...] for r in blocks], axis=0)
    hidden = up_ref.shape[1]
    tile = 256 if hidden % 256 == 0 else hidden
    total = None
    for i in range(0, hidden, tile):
        units = jax.nn.gelu(dot(rows, up_ref[:, i : i + tile]), approximate=True).astype(bf16)
        term = dot(units, down_ref[i : i + tile, :])
        total = term if total is None else total + term
    if own:
        partial_ref[:SHARE, :] = (rest[0][...].astype(f32) + total[:SHARE]).astype(bf16)
        partial_ref[SHARE:, :] = total[SHARE:].astype(bf16)
    else:
        partial_ref[...] = total.astype(bf16)


def encode(name, up, down, blocks, rows=None, flops=0, after=()):
    own = () if rows is None else (rows,)
    return call(
        functools.partial(encode_kernel, len(own)),
        name,
        [near(len(blocks) * SHARE, up.shape[0])],
        (up, down, *own, *blocks),
        flops,
        after=after,
    )[0]


def embed_rows_kernel(embed_ref, *refs):
    partials = [ref for ref in refs if ref.shape[1] == embed_ref.shape[0]]
    outs = refs[len(partials) :]
    rows = jnp.concatenate([p[...] for p in partials], axis=0)
    embedded = dot(rows, embed_ref[...]).astype(bf16)
    blocks = [embedded[i : i + SHARE] for i in range(0, rows.shape[0], SHARE)]
    if len(partials) == 2:
        blocks = [blocks[0], blocks[2], blocks[1], blocks[3]]
    for out, block in zip(outs, blocks):
        out[...] = block


def sum_kernel(*refs):
    parts, (sums_ref, tail_ref) = refs[:-2], refs[-2:]
    total = parts[0][...].astype(f32)
    for part in parts[1:]:
        total += part[...].astype(f32)
    sums_ref[...] = total.astype(bf16)
    tail_ref[...] = total[SMALLEST:, :].astype(bf16)


def decode_kernel(
    visible_ref,
    keep_ref,
    targets_ref,
    mask_ref,
    position_ref,
    qkv_ref,
    out_ref,
    pred_ref,
    sums_ref,
    tail_ref,
    recon_ref,
    loss_ref,
    flat,
    errors,
):
    patch_count = position_ref.shape[0]
    patch = lax.broadcasted_iota(jnp.int32, (patch_count, patch_count), 0)
    slot = lax.broadcasted_iota(jnp.int32, (patch_count, patch_count), 1)
    chosen = ((keep_ref[...] == patch) & (slot < visible_ref[0])).astype(f32)
    seen = jnp.max(chosen, axis=1, keepdims=True)
    slots = chosen.astype(bf16)[:, :SHARE]
    late = jnp.where(slot >= SHARE, chosen, 0.0)
    moved = pltpu.roll(late, patch_count + VMAX - SHARE - visible_ref[0], 1)
    picked = dot(slots, sums_ref[...]) + dot(moved.astype(bf16)[:, : VMAX - SHARE], tail_ref[...])
    start = jnp.where(seen > 0, picked, mask_ref[...].astype(f32)) + position_ref[...].astype(f32)
    projections = dot(layer_norm(start).astype(bf16), qkv_ref[...]).astype(bf16)
    scale = 1.0 / math.sqrt(HSIZE)
    pair = LANES // HSIZE
    column = lax.broadcasted_iota(jnp.int32, (patch_count, LANES), 1) // HSIZE
    masks = [((column == i).astype(f32) * scale).astype(bf16) for i in range(pair)]
    values = projections[:, 2 * DD :].astype(f32).T.astype(bf16)
    mixed = []
    for first in range(0, DD, LANES):
        query = projections[:, first : first + LANES]
        query = jnp.concatenate([query * mask for mask in masks], axis=0)
        key = projections[:, DD + first : DD + first + LANES]
        scores = lax.dot_general(
            key, query, (((1,), (1,)), ((), ())), preferred_element_type=f32
        )
        weights = jnp.exp(scores - jnp.max(scores, axis=0, keepdims=True))
        total = 1.0 / jnp.sum(weights, axis=0, keepdims=True)
        weights = weights.astype(bf16)
        for i in range(pair):
            head = slice(first + i * HSIZE, first + (i + 1) * HSIZE)
            mine = slice(i * patch_count, (i + 1) * patch_count)
            mixed.append(dot(values[head, :], weights[:, mine]) * total[:, mine])
    mixed = jnp.concatenate(mixed, axis=0).astype(bf16)
    after = start + lax.dot_general(mixed, out_ref[...], (((0,), (0,)), ((), ())), preferred_element_type=f32)
    prediction = dot(layer_norm(after).astype(bf16), pred_ref[...])
    group = 4
    wide = group * PIX
    flat[:, :PIX] = prediction[:, :PIX]
    lines = patch_count // group
    together = jnp.concatenate(
        [flat[pl.ds(i, lines, stride=group), :][:, :PIX] for i in range(group)], axis=1
    )
    for line in range(lines):
        place = slice(line * wide, (line + 1) * wide)
        recon_ref[:, place] = together[line : line + 1, :].astype(bf16)
        errors[line : line + 1, :] = together[line : line + 1, :] - targets_ref[:, place].astype(f32)
    squares = errors[...] * errors[...]
    for i in range(group):
        flat[pl.ds(i, lines, stride=group), :PIX] = squares[:, i * PIX : (i + 1) * PIX]
    loss = jnp.sum(flat[:, :PIX], axis=1, keepdims=True) * (1.0 / PIX)
    loss = jnp.where(seen > 0, 0.0, loss)
    loss_ref[...] = jnp.sum(jnp.where(patch == slot, loss, 0.0), axis=0, keepdims=True)


def body(
    dp,
    mp,
    patches,
    keep_index,
    visible,
    targets,
    w_up,
    w_down,
    dec_embed,
    dec_qkv,
    dec_out,
    dec_pred,
    mask_token,
    position,
):
    _, patch_count, width = patches.shape
    fold, piece = dec_embed.shape[0] // dec_qkv.shape[0], dec_qkv.shape[0] // dp
    in_pieces = (dp, mp) == (8, 4) and piece % 16 == 0
    pred_columns = dec_pred.T
    over_mp = lambda a, k: xor_permute(a, "mp", mp, k)
    over_dp = lambda a, bit: xor_permute(a, "dp", dp, bit)
    wide = DD + dec_qkv.shape[1] + LANES
    shards = (dec_embed, dec_qkv, dec_out, pred_columns)
    part = []
    if in_pieces:
        part = call_on_hbm(
            part_kernel,
            "part",
            [near(piece, fold * DD + wide)],
            shards,
            [pltpu.VMEM(pred_columns.shape, bf16), pltpu.SemaphoreType.DMA((fold + 3,))],
        )
    keep_index, patches, tail = call_on_hbm(
        tail_kernel,
        "tail",
        [
            near(*keep_index.shape, dtype=jnp.int32),
            near(patch_count, width),
            near(VMAX - SHARE, width),
        ],
        (keep_index, patches),
        [pltpu.SemaphoreType.DMA((2,))],
        part,
    )
    fence = ()
    if in_pieces:
        far = over_mp(part[0], 2)
        parts = [over_mp(part[0], 1), far]
    tail = over_dp(tail, dp // 2)
    if in_pieces:
        passed = relay("pass_part", far, after=(tail, parts[0]))
        parts.append(over_mp(passed, 1))
        embed, rest = call(
            split_kernel,
            "split",
            [near((mp - 1) * fold * piece, DD), near((mp - 1) * piece, wide)],
            parts,
        )
        fence = (embed,)
    rows, normed = call(
        rows_kernel,
        "select_rows",
        [near(SHARE, width)] * 2,
        (visible, keep_index, patches, tail),
        LONG,
        after=fence,
    )
    if in_pieces:
        others = [over_mp(normed, 1), over_mp(normed, 2)]
        embeds = [embed] + [over_dp(embed, bit) for bit in PLANE[1:]]
        passed = relay("pass_rows", others[1], LONG, (w_up, w_down, embed))
        others.append(over_mp(passed, 1))
        partials = [
            encode("encode_near", w_up, w_down, (normed, passed), rows, -1, (passed,)),
            encode("encode", w_up, w_down, (others[0], others[2]), flops=LONG),
        ]
        rests = plane_gather("rest", rest, dp, partials[:1])
    else:
        full_embed, *weights = [
            lax.all_gather(w, "mp", axis=0, tiled=True) for w in (dec_embed, dec_qkv, dec_out, dec_pred)
        ]
        others = [over_mp(normed, k) for k in range(1, mp)]
        partials = [encode("encode", w_up, w_down, (normed, *others), rows)]
    if in_pieces:
        embeds.append(over_dp(join("join_embed", embeds, after=partials[:1]), 1))
        (full_embed,) = call(
            functools.partial(embed_kernel, mp, fold * piece),
            "full_embed",
            [near(mp * dec_embed.shape[0], DD)],
            (shards[0], *embeds),
        )
    out, *sent = call(
        embed_rows_kernel,
        "embed_rows",
        [near(SHARE, DD)] * mp,
        (full_embed, *partials),
        flops=LONG,
    )
    back = [over_mp(sent[k - 1], k) for k in range(mp - 1, 0, -1)]
    sums, own_tail = call(
        sum_kernel, "add_up", [near(SHARE, DD), near(SHARE - SMALLEST, DD)], (out, *back)
    )
    if in_pieces:
        rests = (*rests, over_dp(relay("pass_rest", rests[2], after=(sums,)), 1))
        weights = call(
            functools.partial(decoder_weights_kernel, mp, piece),
            "decoder_weights",
            [near(mp * w.shape[0], w.shape[1]) for w in (dec_qkv, dec_out, dec_pred)],
            (*shards[1:], *rests),
        )
    return call(
        decode_kernel,
        "decode",
        [
            jax.ShapeDtypeStruct(targets.shape, bf16),
            jax.ShapeDtypeStruct((1, patch_count), f32),
        ],
        (
            visible,
            keep_index,
            targets,
            mask_token[None],
            position,
            *weights,
            sums,
            over_dp(own_tail, dp // 2),
        ),
        flops=10 * patch_count * DD * DD,
        scratch=[pltpu.VMEM((patch_count, LANES), f32), pltpu.VMEM((patch_count // 4, 4 * PIX), f32)],
    )


def solution(mesh):
    return jax.shard_map(
        functools.partial(body, mesh.shape["dp"], mesh.shape["mp"]),
        mesh=mesh,
        in_specs=(
            P(("dp", "mp"), None, None),
            P(("dp", "mp"), None),
            P(("dp", "mp")),
            P(("dp", "mp"), None),
            P(None, "mp"),
            P("mp", None),
            P("mp", None),
            P("mp", None),
            P("mp", None),
            P("mp", None),
            P(),
            P(),
        ),
        out_specs=(P(("dp", "mp"), None), P(("dp", "mp"), None)),
        check_vma=False,
    )
```

```python
import functools
import math

import jax
import jax.numpy as jnp
from jax import lax
from jax.experimental import pallas as pl
from jax.experimental.pallas import tpu as pltpu
from jax.sharding import PartitionSpec as P

DD = 512
HSIZE = 64
PIX = 96
VMAX = 80
SHARE = 48
SMALLEST = 2 * SHARE - VMAX
LANES = 128
EPSILON = 1e-06
LIMIT = 14 << 20
LONG = 10**11

f32 = jnp.float32
bf16 = jnp.bfloat16
VMEM = pl.BlockSpec(memory_space=pltpu.VMEM)
SMEM = pl.BlockSpec(memory_space=pltpu.SMEM)
HBM = pl.BlockSpec(memory_space=pltpu.HBM)


def dot(left, right):
    return jnp.dot(left, right, preferred_element_type=f32)


def layer_norm(values):
    center = values - jnp.mean(values, axis=-1, keepdims=True)
    spread = jnp.mean(center * center, axis=-1, keepdims=True)
    return center * lax.rsqrt(spread + EPSILON)


def cost(flops, size):
    return pl.CostEstimate(flops=flops, bytes_accessed=size, transcendentals=0)


def stay(array):
    return pltpu.with_memory_space_constraint(array, pltpu.HBM)


def call(kernel, name, outs, ins, flops=0, scratch=(), after=()):
    count = len(ins)

    def run(*refs):
        kernel(*refs[:count], *refs[count + len(after) :])

    size = sum(2 * math.prod(a.shape) for a in (*ins, *outs)) if flops >= 0 else 0
    return pl.pallas_call(
        run,
        out_shape=outs,
        in_specs=[SMEM if a.ndim == 1 else VMEM for a in ins]
        + [pl.BlockSpec(memory_space=pl.ANY)] * len(after),
        out_specs=[VMEM] * len(outs),
        scratch_shapes=scratch,
        compiler_params=pltpu.CompilerParams(vmem_limit_bytes=LIMIT),
        cost_estimate=cost(max(flops, 0), size),
        name=name,
    )(*ins, *after)


def near(*shape, dtype=bf16):
    return pltpu.VMEM(shape, dtype)


def xor_permute(values, axis, size, bit):
    return lax.ppermute(values, axis, [(i, i ^ bit) for i in range(size)])


def pick(chosen, values):
    return lax.dot_general(chosen, values, (((0,), (0,)), ((), ())), preferred_element_type=f32)


def rows_kernel(visible_ref, keep_ref, patches_ref, tail_ref, rows_ref, normed_ref):
    patch_count = patches_ref.shape[0]
    visible = visible_ref[0]
    square = (patch_count, patch_count)
    patch = lax.broadcasted_iota(jnp.int32, square, 0)
    slot = lax.broadcasted_iota(jnp.int32, square, 1)
    own = ((keep_ref[...] == patch) & (slot < visible)).astype(f32).astype(bf16)[:, :SHARE]
    other = (slot - visible == patch).astype(f32).astype(bf16)[: VMAX - SHARE, :SHARE]
    rows = pick(own, patches_ref[...]) + pick(other, tail_ref[...])
    rows_ref[...] = rows.astype(bf16)
    normed_ref[...] = layer_norm(rows).astype(bf16)


def run_copies(moves, sems):
    copies = [pltpu.make_async_copy(x, y, sems.at[i]) for i, (x, y) in enumerate(moves)]
    for copy in copies:
        copy.start()
    for copy in copies:
        copy.wait()


def part_kernel(embed_ref, qkv_ref, out_ref, pred_ref, part_ref, pred, sems):
    j = lax.axis_index("dp")
    count, wide = part_ref.shape[0], qkv_ref.shape[1]
    fold = embed_ref.shape[0] // qkv_ref.shape[0]
    own = pl.ds(pl.multiple_of(j * count, 16), count)
    start = fold * DD
    moves = [(pred_ref, pred)]
    for i in range(fold):
        rows = pl.ds(pl.multiple_of((j * fold + i) * count, 16), count)
        moves.append((embed_ref.at[rows, :], part_ref.at[:, i * DD : (i + 1) * DD]))
    moves.append((qkv_ref.at[own, :], part_ref.at[:, start : start + wide]))
    moves.append((out_ref.at[own, :], part_ref.at[:, start + wide : start + wide + DD]))
    run_copies(moves, sems)
    columns = pick_columns(pred[...], j * count, count)
    last = start + wide + DD
    part_ref[:, last:] = jnp.zeros((count, LANES), bf16)
    part_ref[:, last : last + PIX] = columns.astype(bf16)


def tail_kernel(keep_in, patches_ref, keep_ref, rows_ref, tail_ref, sems):
    run_copies([(patches_ref.at[0], rows_ref), (keep_in, keep_ref)], sems)
    patch_count = rows_ref.shape[0]
    patch = lax.broadcasted_iota(jnp.int32, (patch_count, patch_count), 0)
    chosen = (keep_ref[...] == patch).astype(f32).astype(bf16)[:, SHARE:VMAX]
    tail_ref[...] = pick(chosen, rows_ref[...]).astype(bf16)


def pick_columns(values, first, count):
    shape = (count, values.shape[1])
    place = lax.broadcasted_iota(jnp.int32, shape, 1) - lax.broadcasted_iota(jnp.int32, shape, 0)
    return lax.dot_general(
        (place == first).astype(f32).astype(bf16), values, (((1,), (1,)), ((), ())), preferred_element_type=f32
    )


def call_on_hbm(kernel, name, outs, ins, scratch, after=()):
    def run(*refs):
        kernel(*refs[: len(ins)], *refs[len(ins) + len(after) :])

    return pl.pallas_call(
        run,
        out_shape=outs,
        in_specs=[HBM] * len(ins) + [pl.BlockSpec(memory_space=pl.ANY)] * len(after),
        out_specs=[VMEM] * len(outs),
        scratch_shapes=scratch,
        compiler_params=pltpu.CompilerParams(vmem_limit_bytes=LIMIT),
        cost_estimate=cost(LONG if after else 0, 2 * max(a.size for a in ins)),
        name=name,
    )(*[stay(a) for a in ins], *after)


def relay_kernel(in_ref, out_ref):
    out_ref[...] = in_ref[...]


def relay(name, values, flops=0, after=()):
    return call(relay_kernel, name, [near(*values.shape)], (values,), flops, after=after)[0]


def hold(name, after):
    return call(hold_kernel, name, [near(16, LANES)], (), LONG, after=after)[0]


def hold_kernel(out_ref):
    out_ref[...] = jnp.zeros(out_ref.shape, bf16)


def split_kernel(*refs):
    parts, (embed_ref, rest_ref) = refs[:-2], refs[-2:]
    count, wide = parts[0].shape[0], rest_ref.shape[1]
    fold = (parts[0].shape[1] - wide) // DD
    for k, part in enumerate(parts):
        for i in range(fold):
            place = (k * fold + i) * count
            embed_ref[place : place + count, :] = part[:, i * DD : (i + 1) * DD]
        rest_ref[k * count : (k + 1) * count, :] = part[:, fold * DD :]


def join_kernel(*refs):
    parts, out_ref = refs[:-1], refs[-1]
    count = parts[0].shape[0]
    for i, part in enumerate(parts):
        out_ref[i * count : (i + 1) * count, :] = part[...]


def join(name, parts, flops=0, after=()):
    rows, columns = parts[0].shape
    return call(join_kernel, name, [near(len(parts) * rows, columns)], parts, flops, after=after)[0]


PLANE = (0, 2, 4, 6)


def by_core(values, even, odd, size):
    return lax.ppermute(values, "dp", [(i, i ^ (odd if i & 1 else even)) for i in range(size)])


def plane_gather(name, own, size, after=()):
    (pair,) = call(
        join_kernel, f"pair_{name}", [near(2 * own.shape[0], own.shape[1])], (own, by_core(own, 2, 4, size)), after=after
    )
    other = xor_permute(pair, "dp", size, 1)
    return pair, other, by_core(other, 2, 4, size)


def direct_owners(j):
    return *[(j ^ i,) for i in PLANE], [j ^ i ^ 1 for i in PLANE]


def gathered_owners(j):
    side = 2 + 2 * (j & 1)
    return (j, j ^ side), (j ^ 1, j ^ 7 ^ side), (j ^ 1 ^ side, j ^ 7), (j ^ 6 ^ side, j ^ 6)


def assemble(refs, owners, own_rows, mp, piece, write):
    m = lax.axis_index("mp")
    write(pl.multiple_of(m * own_rows, 16), own_rows, None, 0)
    count = (mp - 1) * piece
    for source, devices in zip(refs, owners(lax.axis_index("dp"))):
        for block, owner in enumerate(devices):
            for k in range(1, mp):
                row = (m ^ k) * own_rows + owner * piece
                write(pl.multiple_of(row, 16), piece, source, block * count + (k - 1) * piece)


def embed_kernel(mp, piece, own_ref, *rest):
    refs, full = rest[:-1], rest[-1]

    def write(row, count, source, base):
        if source is None:
            full[pl.ds(row, count), :] = own_ref[...]
        else:
            full[pl.ds(row, count), :] = source[base : base + count, :]

    assemble(refs, direct_owners, own_ref.shape[0], mp, piece, write)


def decoder_weights_kernel(mp, piece, qkv_ref, out_ref, pred_ref, *rest):
    refs, (full_qkv, full_out, full_pred) = rest[:-3], rest[-3:]
    wide = full_qkv.shape[1]

    def write(row, count, source, base):
        place = pl.ds(row, count)
        if source is None:
            full_qkv[place, :] = qkv_ref[...]
            full_out[place, :] = out_ref[...]
            full_pred[place, :PIX] = pred_ref[...].astype(f32).T.astype(bf16)
        else:
            part = pl.ds(base, count)
            full_qkv[place, :] = source[part, :wide]
            full_out[place, :] = source[part, wide : wide + DD]
            full_pred[place, :PIX] = source[part, wide + DD : wide + DD + PIX]

    assemble(refs, gathered_owners, qkv_ref.shape[0], mp, piece, write)


def encode_kernel(own, up_ref, down_ref, *rest):
    blocks, partial_ref = rest[own:-1], rest[-1]
    rows = jnp.concatenate([r[...] for r in blocks], axis=0)
    hidden = up_ref.shape[1]
    tile = 256 if hidden % 256 == 0 else hidden
    total = None
    for i in range(0, hidden, tile):
        units = jax.nn.gelu(dot(rows, up_ref[:, i : i + tile]), approximate=True).astype(bf16)
        term = dot(units, down_ref[i : i + tile, :])
        total = term if total is None else total + term
    if own:
        partial_ref[:SHARE, :] = (rest[0][...].astype(f32) + total[:SHARE]).astype(bf16)
        if total.shape[0] > SHARE:
            partial_ref[SHARE:, :] = total[SHARE:].astype(bf16)
    else:
        partial_ref[...] = total.astype(bf16)


def encode(name, up, down, blocks, rows=None, flops=0, after=()):
    own = () if rows is None else (rows,)
    return call(
        functools.partial(encode_kernel, len(own)),
        name,
        [near(len(blocks) * SHARE, up.shape[0])],
        (up, down, *own, *blocks),
        flops,
        after=after,
    )[0]


def embed_rows_kernel(embed_ref, *refs):
    partials = [ref for ref in refs if ref.shape[1] == embed_ref.shape[0]]
    outs = refs[len(partials) :]
    rows = jnp.concatenate([p[...] for p in partials], axis=0)
    embedded = dot(rows, embed_ref[...]).astype(bf16)
    blocks = [embedded[i : i + SHARE] for i in range(0, rows.shape[0], SHARE)]
    for out, block in zip(outs, blocks):
        out[...] = block


def sum_kernel(*refs):
    parts, (sums_ref, tail_ref) = refs[:-2], refs[-2:]
    total = parts[0][...].astype(f32)
    for part in parts[1:]:
        total += part[...].astype(f32)
    sums_ref[...] = total.astype(bf16)
    tail_ref[...] = total[SMALLEST:, :].astype(bf16)


def decode_kernel(
    visible_ref,
    keep_ref,
    targets_ref,
    mask_ref,
    position_ref,
    qkv_ref,
    out_ref,
    pred_ref,
    sums_ref,
    tail_ref,
    recon_ref,
    loss_ref,
    flat,
    errors,
):
    patch_count = position_ref.shape[0]
    patch = lax.broadcasted_iota(jnp.int32, (patch_count, patch_count), 0)
    slot = lax.broadcasted_iota(jnp.int32, (patch_count, patch_count), 1)
    chosen = ((keep_ref[...] == patch) & (slot < visible_ref[0])).astype(f32)
    seen = jnp.max(chosen, axis=1, keepdims=True)
    slots = chosen.astype(bf16)[:, :SHARE]
    late = jnp.where(slot >= SHARE, chosen, 0.0)
    moved = pltpu.roll(late, patch_count + VMAX - SHARE - visible_ref[0], 1)
    picked = dot(slots, sums_ref[...]) + dot(moved.astype(bf16)[:, : VMAX - SHARE], tail_ref[...])
    start = jnp.where(seen > 0, picked, mask_ref[...].astype(f32)) + position_ref[...].astype(f32)
    projections = dot(layer_norm(start).astype(bf16), qkv_ref[...]).astype(bf16)
    scale = 1.0 / math.sqrt(HSIZE)
    pair = LANES // HSIZE
    column = lax.broadcasted_iota(jnp.int32, (patch_count, LANES), 1) // HSIZE
    masks = [((column == i).astype(f32) * scale).astype(bf16) for i in range(pair)]
    values = projections[:, 2 * DD :].astype(f32).T.astype(bf16)
    mixed = []
    for first in range(0, DD, LANES):
        query = projections[:, first : first + LANES]
        query = jnp.concatenate([query * mask for mask in masks], axis=0)
        key = projections[:, DD + first : DD + first + LANES]
        scores = lax.dot_general(
            key, query, (((1,), (1,)), ((), ())), preferred_element_type=f32
        )
        weights = jnp.exp(scores - jnp.max(scores, axis=0, keepdims=True))
        total = 1.0 / jnp.sum(weights, axis=0, keepdims=True)
        weights = weights.astype(bf16)
        for i in range(pair):
            head = slice(first + i * HSIZE, first + (i + 1) * HSIZE)
            mine = slice(i * patch_count, (i + 1) * patch_count)
            mixed.append(dot(values[head, :], weights[:, mine]) * total[:, mine])
    mixed = jnp.concatenate(mixed, axis=0).astype(bf16)
    after = start + lax.dot_general(mixed, out_ref[...], (((0,), (0,)), ((), ())), preferred_element_type=f32)
    prediction = dot(layer_norm(after).astype(bf16), pred_ref[...])
    group = 4
    wide = group * PIX
    flat[:, :PIX] = prediction[:, :PIX]
    lines = patch_count // group
    together = jnp.concatenate(
        [flat[pl.ds(i, lines, stride=group), :][:, :PIX] for i in range(group)], axis=1
    )
    for line in range(lines):
        place = slice(line * wide, (line + 1) * wide)
        recon_ref[:, place] = together[line : line + 1, :].astype(bf16)
        errors[line : line + 1, :] = together[line : line + 1, :] - targets_ref[:, place].astype(f32)
    squares = errors[...] * errors[...]
    for i in range(group):
        flat[pl.ds(i, lines, stride=group), :PIX] = squares[:, i * PIX : (i + 1) * PIX]
    loss = jnp.sum(flat[:, :PIX], axis=1, keepdims=True) * (1.0 / PIX)
    loss = jnp.where(seen > 0, 0.0, loss)
    loss_ref[...] = jnp.sum(jnp.where(patch == slot, loss, 0.0), axis=0, keepdims=True)


def body(
    dp,
    mp,
    patches,
    keep_index,
    visible,
    targets,
    w_up,
    w_down,
    dec_embed,
    dec_qkv,
    dec_out,
    dec_pred,
    mask_token,
    position,
):
    _, patch_count, width = patches.shape
    fold, piece = dec_embed.shape[0] // dec_qkv.shape[0], dec_qkv.shape[0] // dp
    in_pieces = (dp, mp) == (8, 4) and piece % 16 == 0
    pred_columns = dec_pred.T
    over_mp = lambda a, k: xor_permute(a, "mp", mp, k)
    over_dp = lambda a, bit: xor_permute(a, "dp", dp, bit)
    wide = DD + dec_qkv.shape[1] + LANES
    shards = (dec_embed, dec_qkv, dec_out, pred_columns)
    part = []
    if in_pieces:
        part = call_on_hbm(
            part_kernel,
            "part",
            [near(piece, fold * DD + wide)],
            shards,
            [pltpu.VMEM(pred_columns.shape, bf16), pltpu.SemaphoreType.DMA((fold + 3,))],
        )
    keep_index, patches, tail = call_on_hbm(
        tail_kernel,
        "tail",
        [
            near(*keep_index.shape, dtype=jnp.int32),
            near(patch_count, width),
            near(VMAX - SHARE, width),
        ],
        (keep_index, patches),
        [pltpu.SemaphoreType.DMA((2,))],
        part,
    )
    fence = ()
    if in_pieces:
        far = over_mp(part[0], 2)
        parts = [over_mp(part[0], 1), far]
    tail = over_dp(tail, dp // 2)
    if in_pieces:
        passed = relay("pass_part", far, after=(tail, parts[0]))
        parts.append(over_mp(passed, 1))
        fence = (passed, w_up, w_down)
    rows, normed = call(
        rows_kernel,
        "select_rows",
        [near(SHARE, width)] * 2,
        (visible, keep_index, patches, tail),
        LONG,
        after=fence,
    )
    if in_pieces:
        partials = [encode("encode_own", w_up, w_down, (normed,), rows, 5 * 10**9, (passed,))]
        embed, rest = call(
            split_kernel,
            "split",
            [near((mp - 1) * fold * piece, DD), near((mp - 1) * piece, wide)],
            parts,
            after=partials,
        )
        embeds = [embed] + [over_dp(embed, bit) for bit in PLANE[1:]]
        passed = relay("pass_rows", over_mp(normed, 2), LONG, (w_up, w_down, embed))
        others = [over_mp(relay("own_rows", normed, after=(passed,)), 1), passed, over_mp(passed, 1)]
        partials.append(encode("encode", w_up, w_down, others, flops=LONG))
        rests = plane_gather("rest", rest, dp, partials[:1])
    else:
        full_embed, *weights = [
            lax.all_gather(w, "mp", axis=0, tiled=True) for w in (dec_embed, dec_qkv, dec_out, dec_pred)
        ]
        others = [over_mp(normed, k) for k in range(1, mp)]
        partials = [encode("encode", w_up, w_down, (normed, *others), rows)]
    if in_pieces:
        embeds.append(over_dp(join("join_embed", embeds), 1))
        (full_embed,) = call(
            functools.partial(embed_kernel, mp, fold * piece),
            "full_embed",
            [near(mp * dec_embed.shape[0], DD)],
            (shards[0], *embeds),
        )
    out, *sent = call(
        embed_rows_kernel,
        "embed_rows",
        [near(SHARE, DD)] * mp,
        (full_embed, *partials),
        flops=LONG,
    )
    back = [over_mp(sent[k - 1], k) for k in range(mp - 1, 0, -1)]
    sums, own_tail = call(
        sum_kernel, "add_up", [near(SHARE, DD), near(SHARE - SMALLEST, DD)], (out, *back)
    )
    if in_pieces:
        rests = (*rests, over_dp(relay("pass_rest", rests[2], after=(sums,)), 1))
        weights = call(
            functools.partial(decoder_weights_kernel, mp, piece),
            "decoder_weights",
            [near(mp * w.shape[0], w.shape[1]) for w in (dec_qkv, dec_out, dec_pred)],
            (*shards[1:], *rests),
        )
    return call(
        decode_kernel,
        "decode",
        [
            jax.ShapeDtypeStruct(targets.shape, bf16),
            jax.ShapeDtypeStruct((1, patch_count), f32),
        ],
        (
            visible,
            keep_index,
            targets,
            mask_token[None],
            position,
            *weights,
            sums,
            over_dp(own_tail, dp // 2),
        ),
        flops=10 * patch_count * DD * DD,
        scratch=[pltpu.VMEM((patch_count, LANES), f32), pltpu.VMEM((patch_count // 4, 4 * PIX), f32)],
    )


def solution(mesh):
    return jax.shard_map(
        functools.partial(body, mesh.shape["dp"], mesh.shape["mp"]),
        mesh=mesh,
        in_specs=(
            P(("dp", "mp"), None, None),
            P(("dp", "mp"), None),
            P(("dp", "mp")),
            P(("dp", "mp"), None),
            P(None, "mp"),
            P("mp", None),
            P("mp", None),
            P("mp", None),
            P("mp", None),
            P("mp", None),
            P(),
            P(),
        ),
        out_specs=(P(("dp", "mp"), None), P(("dp", "mp"), None)),
        check_vma=False,
    )
```

```python
import functools
import math

import jax
import jax.numpy as jnp
from jax import lax
from jax.experimental import pallas as pl
from jax.experimental.pallas import tpu as pltpu
from jax.sharding import PartitionSpec as P

DD = 512
HSIZE = 64
PIX = 96
VMAX = 80
SHARE = 48
SMALLEST = 2 * SHARE - VMAX
LANES = 128
EPSILON = 1e-06
LIMIT = 14 << 20
LONG = 10**11

f32 = jnp.float32
bf16 = jnp.bfloat16
VMEM = pl.BlockSpec(memory_space=pltpu.VMEM)
SMEM = pl.BlockSpec(memory_space=pltpu.SMEM)
HBM = pl.BlockSpec(memory_space=pltpu.HBM)


def dot(left, right):
    return jnp.dot(left, right, preferred_element_type=f32)


def layer_norm(values):
    center = values - jnp.mean(values, axis=-1, keepdims=True)
    spread = jnp.mean(center * center, axis=-1, keepdims=True)
    return center * lax.rsqrt(spread + EPSILON)


def cost(flops, size):
    return pl.CostEstimate(flops=flops, bytes_accessed=size, transcendentals=0)


def stay(array):
    return pltpu.with_memory_space_constraint(array, pltpu.HBM)


def call(kernel, name, outs, ins, flops=0, scratch=(), after=()):
    count = len(ins)

    def run(*refs):
        kernel(*refs[:count], *refs[count + len(after) :])

    size = sum(2 * math.prod(a.shape) for a in (*ins, *outs)) if flops >= 0 else 0
    return pl.pallas_call(
        run,
        out_shape=outs,
        in_specs=[SMEM if a.ndim == 1 else VMEM for a in ins]
        + [pl.BlockSpec(memory_space=pl.ANY)] * len(after),
        out_specs=[VMEM] * len(outs),
        scratch_shapes=scratch,
        compiler_params=pltpu.CompilerParams(vmem_limit_bytes=LIMIT),
        cost_estimate=cost(max(flops, 0), size),
        name=name,
    )(*ins, *after)


def near(*shape, dtype=bf16):
    return pltpu.VMEM(shape, dtype)


def xor_permute(values, axis, size, bit):
    return lax.ppermute(values, axis, [(i, i ^ bit) for i in range(size)])


def pick(chosen, values):
    return lax.dot_general(chosen, values, (((0,), (0,)), ((), ())), preferred_element_type=f32)


def rows_kernel(visible_ref, keep_ref, patches_ref, tail_ref, rows_ref, normed_ref):
    patch_count = patches_ref.shape[0]
    visible = visible_ref[0]
    square = (patch_count, patch_count)
    patch = lax.broadcasted_iota(jnp.int32, square, 0)
    slot = lax.broadcasted_iota(jnp.int32, square, 1)
    own = ((keep_ref[...] == patch) & (slot < visible)).astype(f32).astype(bf16)[:, :SHARE]
    other = (slot - visible == patch).astype(f32).astype(bf16)[: VMAX - SHARE, :SHARE]
    rows = pick(own, patches_ref[...]) + pick(other, tail_ref[...])
    rows_ref[...] = rows.astype(bf16)
    normed_ref[...] = layer_norm(rows).astype(bf16)


def run_copies(moves, sems):
    copies = [pltpu.make_async_copy(x, y, sems.at[i]) for i, (x, y) in enumerate(moves)]
    for copy in copies:
        copy.start()
    for copy in copies:
        copy.wait()


def part_kernel(embed_ref, qkv_ref, out_ref, pred_ref, part_ref, sems):
    j = lax.axis_index("dp")
    count, wide = part_ref.shape[0], qkv_ref.shape[1]
    fold = embed_ref.shape[0] // qkv_ref.shape[0]
    own = pl.ds(pl.multiple_of(j * count, 16), count)
    start = fold * DD
    moves = []
    for i in range(fold):
        rows = pl.ds(pl.multiple_of((j * fold + i) * count, 16), count)
        moves.append((embed_ref.at[rows, :], part_ref.at[:, i * DD : (i + 1) * DD]))
    moves.append((qkv_ref.at[own, :], part_ref.at[:, start : start + wide]))
    start += wide
    moves.append((out_ref.at[own, :], part_ref.at[:, start : start + DD]))
    moves.append((pred_ref.at[pred_rows(j, count), :], part_ref.at[:, start + DD :]))
    run_copies(moves, sems)


def pred_rows(owner, count):
    return pl.ds(pl.multiple_of(jnp.minimum(owner, PIX // count - 1) * count, 16), count)


def tail_kernel(keep_in, patches_ref, keep_ref, rows_ref, tail_ref, sems):
    run_copies([(patches_ref.at[0], rows_ref), (keep_in, keep_ref)], sems)
    patch_count = rows_ref.shape[0]
    patch = lax.broadcasted_iota(jnp.int32, (patch_count, patch_count), 0)
    chosen = (keep_ref[...] == patch).astype(f32).astype(bf16)[:, SHARE:VMAX]
    tail_ref[...] = pick(chosen, rows_ref[...]).astype(bf16)


def call_on_hbm(kernel, name, outs, ins, scratch, after=()):
    def run(*refs):
        kernel(*refs[: len(ins)], *refs[len(ins) + len(after) :])

    return pl.pallas_call(
        run,
        out_shape=outs,
        in_specs=[HBM] * len(ins) + [pl.BlockSpec(memory_space=pl.ANY)] * len(after),
        out_specs=[VMEM] * len(outs),
        scratch_shapes=scratch,
        compiler_params=pltpu.CompilerParams(vmem_limit_bytes=LIMIT),
        cost_estimate=cost(LONG if after else 0, 2 * max(a.size for a in ins)),
        name=name,
    )(*[stay(a) for a in ins], *after)


def relay_kernel(in_ref, out_ref):
    out_ref[...] = in_ref[...]


def relay(name, values, flops=0, after=()):
    return call(relay_kernel, name, [near(*values.shape)], (values,), flops, after=after)[0]


def hold(name, after):
    return call(hold_kernel, name, [near(16, LANES)], (), LONG, after=after)[0]


def hold_kernel(out_ref):
    out_ref[...] = jnp.zeros(out_ref.shape, bf16)


def split_kernel(*refs):
    parts, (embed_ref, rest_ref) = refs[:-2], refs[-2:]
    count, wide = parts[0].shape[0], rest_ref.shape[1]
    fold = (parts[0].shape[1] - wide) // DD
    for k, part in enumerate(parts):
        for i in range(fold):
            place = (k * fold + i) * count
            embed_ref[place : place + count, :] = part[:, i * DD : (i + 1) * DD]
        rest_ref[k * count : (k + 1) * count, :] = part[:, fold * DD :]


def join_kernel(*refs):
    parts, out_ref = refs[:-1], refs[-1]
    count = parts[0].shape[0]
    for i, part in enumerate(parts):
        out_ref[i * count : (i + 1) * count, :] = part[...]


def join(name, parts, flops=0, after=()):
    rows, columns = parts[0].shape
    return call(join_kernel, name, [near(len(parts) * rows, columns)], parts, flops, after=after)[0]


PLANE = (0, 2, 4, 6)


def by_core(values, even, odd, size):
    return lax.ppermute(values, "dp", [(i, i ^ (odd if i & 1 else even)) for i in range(size)])


def plane_gather(name, own, size, after=()):
    (pair,) = call(
        join_kernel, f"pair_{name}", [near(2 * own.shape[0], own.shape[1])], (own, by_core(own, 2, 4, size)), after=after
    )
    other = xor_permute(pair, "dp", size, 1)
    return pair, other, by_core(other, 2, 4, size)


def direct_owners(j):
    return *[(j ^ i,) for i in PLANE], [j ^ i ^ 1 for i in PLANE]


def gathered_owners(j):
    side = 2 + 2 * (j & 1)
    return (j, j ^ side), (j ^ 1, j ^ 7 ^ side), (j ^ 1 ^ side, j ^ 7), (j ^ 6 ^ side, j ^ 6)


def assemble(refs, owners, own_rows, mp, piece, write):
    m = lax.axis_index("mp")
    write(pl.multiple_of(m * own_rows, 16), own_rows, None, 0, m, None)
    count = (mp - 1) * piece
    for source, devices in zip(refs, owners(lax.axis_index("dp"))):
        for block, owner in enumerate(devices):
            for k in range(1, mp):
                row = (m ^ k) * own_rows + owner * piece
                first = block * count + (k - 1) * piece
                write(pl.multiple_of(row, 16), piece, source, first, m ^ k, owner)


def embed_kernel(mp, piece, own_ref, *rest):
    refs, full = rest[:-1], rest[-1]

    def write(row, count, source, base, shard, owner):
        if source is None:
            full[pl.ds(row, count), :] = own_ref[...]
        else:
            full[pl.ds(row, count), :] = source[base : base + count, :]

    assemble(refs, direct_owners, own_ref.shape[0], mp, piece, write)


def decoder_weights_kernel(mp, piece, qkv_ref, out_ref, pred_ref, *rest):
    refs, (full_qkv, full_out, full_pred) = rest[:-3], rest[-3:]
    wide = full_qkv.shape[1]
    columns = pred_ref.shape[1]
    shard_columns = lambda shard: pl.ds(pl.multiple_of(shard * columns, LANES), columns)

    def write(row, count, source, base, shard, owner):
        place = pl.ds(row, count)
        if source is None:
            full_qkv[place, :] = qkv_ref[...]
            full_out[place, :] = out_ref[...]
            full_pred[:, shard_columns(shard)] = pred_ref[...]
        else:
            part = pl.ds(base, count)
            full_qkv[place, :] = source[part, :wide]
            full_out[place, :] = source[part, wide : wide + DD]
            pred = source[part, wide + DD :]
            full_pred[pred_rows(owner, count), shard_columns(shard)] = pred

    assemble(refs, gathered_owners, qkv_ref.shape[0], mp, piece, write)


def encode_kernel(own, up_ref, down_ref, *rest):
    blocks, partial_ref = rest[own:-1], rest[-1]
    rows = jnp.concatenate([r[...] for r in blocks], axis=0)
    hidden = up_ref.shape[1]
    tile = 256 if hidden % 256 == 0 else hidden
    total = None
    for i in range(0, hidden, tile):
        units = jax.nn.gelu(dot(rows, up_ref[:, i : i + tile]), approximate=True).astype(bf16)
        term = dot(units, down_ref[i : i + tile, :])
        total = term if total is None else total + term
    if own:
        partial_ref[:SHARE, :] = (rest[0][...].astype(f32) + total[:SHARE]).astype(bf16)
        if total.shape[0] > SHARE:
            partial_ref[SHARE:, :] = total[SHARE:].astype(bf16)
    else:
        partial_ref[...] = total.astype(bf16)


def encode(name, up, down, blocks, rows=None, flops=0, after=()):
    own = () if rows is None else (rows,)
    return call(
        functools.partial(encode_kernel, len(own)),
        name,
        [near(len(blocks) * SHARE, up.shape[0])],
        (up, down, *own, *blocks),
        flops,
        after=after,
    )[0]


def embed_rows_kernel(embed_ref, *refs):
    partials = [ref for ref in refs if ref.shape[1] == embed_ref.shape[0]]
    outs = refs[len(partials) :]
    rows = jnp.concatenate([p[...] for p in partials], axis=0)
    embedded = dot(rows, embed_ref[...]).astype(bf16)
    blocks = [embedded[i : i + SHARE] for i in range(0, rows.shape[0], SHARE)]
    if len(partials) == 3:
        blocks = [blocks[0], blocks[2], blocks[1], blocks[3]]
    for out, block in zip(outs, blocks):
        out[...] = block


def sum_kernel(*refs):
    parts, (sums_ref, tail_ref) = refs[:-2], refs[-2:]
    total = parts[0][...].astype(f32)
    for part in parts[1:]:
        total += part[...].astype(f32)
    sums_ref[...] = total.astype(bf16)
    tail_ref[...] = total[SMALLEST:, :].astype(bf16)


def decode_kernel(
    visible_ref,
    keep_ref,
    targets_ref,
    mask_ref,
    position_ref,
    qkv_ref,
    out_ref,
    pred_ref,
    sums_ref,
    tail_ref,
    recon_ref,
    loss_ref,
    flat,
    errors,
):
    patch_count = position_ref.shape[0]
    patch = lax.broadcasted_iota(jnp.int32, (patch_count, patch_count), 0)
    slot = lax.broadcasted_iota(jnp.int32, (patch_count, patch_count), 1)
    chosen = ((keep_ref[...] == patch) & (slot < visible_ref[0])).astype(f32)
    seen = jnp.max(chosen, axis=1, keepdims=True)
    slots = chosen.astype(bf16)[:, :SHARE]
    late = jnp.where(slot >= SHARE, chosen, 0.0)
    moved = pltpu.roll(late, patch_count + VMAX - SHARE - visible_ref[0], 1)
    picked = dot(slots, sums_ref[...]) + dot(moved.astype(bf16)[:, : VMAX - SHARE], tail_ref[...])
    start = jnp.where(seen > 0, picked, mask_ref[...].astype(f32)) + position_ref[...].astype(f32)
    projections = dot(layer_norm(start).astype(bf16), qkv_ref[...]).astype(bf16)
    scale = 1.0 / math.sqrt(HSIZE)
    pair = LANES // HSIZE
    column = lax.broadcasted_iota(jnp.int32, (patch_count, LANES), 1) // HSIZE
    masks = [((column == i).astype(f32) * scale).astype(bf16) for i in range(pair)]
    values = projections[:, 2 * DD :].astype(f32).T.astype(bf16)
    mixed = []
    for first in range(0, DD, LANES):
        query = projections[:, first : first + LANES]
        query = jnp.concatenate([query * mask for mask in masks], axis=0)
        key = projections[:, DD + first : DD + first + LANES]
        scores = lax.dot_general(
            key, query, (((1,), (1,)), ((), ())), preferred_element_type=f32
        )
        weights = jnp.exp(scores - jnp.max(scores, axis=0, keepdims=True))
        total = 1.0 / jnp.sum(weights, axis=0, keepdims=True)
        weights = weights.astype(bf16)
        for i in range(pair):
            head = slice(first + i * HSIZE, first + (i + 1) * HSIZE)
            mine = slice(i * patch_count, (i + 1) * patch_count)
            mixed.append(dot(values[head, :], weights[:, mine]) * total[:, mine])
    mixed = jnp.concatenate(mixed, axis=0).astype(bf16)
    after = start + lax.dot_general(mixed, out_ref[...], (((0,), (0,)), ((), ())), preferred_element_type=f32)
    prediction = lax.dot_general(
        layer_norm(after).astype(bf16), pred_ref[...], (((1,), (1,)), ((), ())), preferred_element_type=f32
    )
    group = 4
    wide = group * PIX
    flat[:, :PIX] = prediction[:, :PIX]
    lines = patch_count // group
    together = jnp.concatenate(
        [flat[pl.ds(i, lines, stride=group), :][:, :PIX] for i in range(group)], axis=1
    )
    for line in range(lines):
        place = slice(line * wide, (line + 1) * wide)
        recon_ref[:, place] = together[line : line + 1, :].astype(bf16)
        errors[line : line + 1, :] = together[line : line + 1, :] - targets_ref[:, place].astype(f32)
    squares = errors[...] * errors[...]
    for i in range(group):
        flat[pl.ds(i, lines, stride=group), :PIX] = squares[:, i * PIX : (i + 1) * PIX]
    loss = jnp.sum(flat[:, :PIX], axis=1, keepdims=True) * (1.0 / PIX)
    loss = jnp.where(seen > 0, 0.0, loss)
    loss_ref[...] = jnp.sum(jnp.where(patch == slot, loss, 0.0), axis=0, keepdims=True)


def body(
    dp,
    mp,
    patches,
    keep_index,
    visible,
    targets,
    w_up,
    w_down,
    dec_embed,
    dec_qkv,
    dec_out,
    dec_pred,
    mask_token,
    position,
):
    _, patch_count, width = patches.shape
    fold, piece = dec_embed.shape[0] // dec_qkv.shape[0], dec_qkv.shape[0] // dp
    in_pieces = (dp, mp) == (8, 4) and piece % 16 == 0
    pred_columns = dec_pred.T
    over_mp = lambda a, k: xor_permute(a, "mp", mp, k)
    over_dp = lambda a, bit: xor_permute(a, "dp", dp, bit)
    wide = DD + dec_qkv.shape[1] + LANES
    shards = (dec_embed, dec_qkv, dec_out, pred_columns)
    part = []
    if in_pieces:
        part = call_on_hbm(
            part_kernel,
            "part",
            [near(piece, fold * DD + wide)],
            shards,
            [pltpu.SemaphoreType.DMA((fold + 3,))],
        )
    keep_index, patches, tail = call_on_hbm(
        tail_kernel,
        "tail",
        [
            near(*keep_index.shape, dtype=jnp.int32),
            near(patch_count, width),
            near(VMAX - SHARE, width),
        ],
        (keep_index, patches),
        [pltpu.SemaphoreType.DMA((2,))],
        part,
    )
    fence = ()
    if in_pieces:
        far = over_mp(part[0], 2)
        parts = [over_mp(part[0], 1), far]
    tail = over_dp(tail, dp // 2)
    if in_pieces:
        passed = relay("pass_part", far, after=(tail, parts[0]))
        parts.append(over_mp(passed, 1))
        fence = (passed, w_up, w_down)
    rows, normed = call(
        rows_kernel,
        "select_rows",
        [near(SHARE, width)] * 2,
        (visible, keep_index, patches, tail),
        LONG,
        after=fence,
    )
    if in_pieces:
        partials = [encode("encode_own", w_up, w_down, (normed,), rows, 5 * 10**9, (passed,))]
        embed, rest = call(
            split_kernel,
            "split",
            [near((mp - 1) * fold * piece, DD), near((mp - 1) * piece, wide)],
            parts,
            after=partials,
        )
        embeds = [embed] + [over_dp(embed, bit) for bit in PLANE[1:]]
        passed = relay("pass_rows", over_mp(normed, 2), LONG, (w_up, w_down, embed))
        others = [over_mp(relay("own_rows", normed, after=(passed,)), 1), passed, over_mp(passed, 1)]
        partials.append(encode("encode_near", w_up, w_down, others[1:2], flops=-1))
        partials.append(encode("encode", w_up, w_down, (others[0], others[2]), flops=LONG))
        rests = plane_gather("rest", rest, dp, partials[:1])
    else:
        full_embed, *weights = [
            lax.all_gather(w, "mp", axis=0, tiled=True) for w in (dec_embed, dec_qkv, dec_out, dec_pred)
        ]
        weights[2] = weights[2].T
        others = [over_mp(normed, k) for k in range(1, mp)]
        partials = [encode("encode", w_up, w_down, (normed, *others), rows)]
    if in_pieces:
        embeds.append(over_dp(join("join_embed", embeds), 1))
        (full_embed,) = call(
            functools.partial(embed_kernel, mp, fold * piece),
            "full_embed",
            [near(mp * dec_embed.shape[0], DD)],
            (shards[0], *embeds),
        )
    out, *sent = call(
        embed_rows_kernel,
        "embed_rows",
        [near(SHARE, DD)] * mp,
        (full_embed, *partials),
        flops=LONG,
    )
    back = [over_mp(sent[k - 1], k) for k in range(mp - 1, 0, -1)]
    sums, own_tail = call(
        sum_kernel, "add_up", [near(SHARE, DD), near(SHARE - SMALLEST, DD)], (out, *back)
    )
    if in_pieces:
        rests = (*rests, over_dp(relay("pass_rest", rests[2], after=(sums,)), 1))
        weights = call(
            functools.partial(decoder_weights_kernel, mp, piece),
            "decoder_weights",
            [near(mp * w.shape[0], w.shape[1]) for w in (dec_qkv, dec_out)]
            + [near(PIX, mp * dec_pred.shape[0])],
            (*shards[1:], *rests),
        )
    return call(
        decode_kernel,
        "decode",
        [
            jax.ShapeDtypeStruct(targets.shape, bf16),
            jax.ShapeDtypeStruct((1, patch_count), f32),
        ],
        (
            visible,
            keep_index,
            targets,
            mask_token[None],
            position,
            *weights,
            sums,
            over_dp(own_tail, dp // 2),
        ),
        flops=10 * patch_count * DD * DD,
        scratch=[pltpu.VMEM((patch_count, LANES), f32), pltpu.VMEM((patch_count // 4, 4 * PIX), f32)],
    )


def solution(mesh):
    return jax.shard_map(
        functools.partial(body, mesh.shape["dp"], mesh.shape["mp"]),
        mesh=mesh,
        in_specs=(
            P(("dp", "mp"), None, None),
            P(("dp", "mp"), None),
            P(("dp", "mp")),
            P(("dp", "mp"), None),
            P(None, "mp"),
            P("mp", None),
            P("mp", None),
            P("mp", None),
            P("mp", None),
            P("mp", None),
            P(),
            P(),
        ),
        out_specs=(P(("dp", "mp"), None), P(("dp", "mp"), None)),
        check_vma=False,
    )
```

```python
import functools
import math

import jax
import jax.numpy as jnp
from jax import lax
from jax.experimental import pallas as pl
from jax.experimental.pallas import tpu as pltpu
from jax.sharding import PartitionSpec as P

DD = 512
HSIZE = 64
PIX = 96
VMAX = 80
SHARE = 48
SMALLEST = 2 * SHARE - VMAX
LANES = 128
EPSILON = 1e-06
LIMIT = 14 << 20
LONG = 10**11

f32 = jnp.float32
bf16 = jnp.bfloat16
VMEM = pl.BlockSpec(memory_space=pltpu.VMEM)
SMEM = pl.BlockSpec(memory_space=pltpu.SMEM)
HBM = pl.BlockSpec(memory_space=pltpu.HBM)


def dot(left, right):
    return jnp.dot(left, right, preferred_element_type=f32)


def layer_norm(values):
    center = values - jnp.mean(values, axis=-1, keepdims=True)
    spread = jnp.mean(center * center, axis=-1, keepdims=True)
    return center * lax.rsqrt(spread + EPSILON)


def cost(flops, size):
    return pl.CostEstimate(flops=flops, bytes_accessed=size, transcendentals=0)


def stay(array):
    return pltpu.with_memory_space_constraint(array, pltpu.HBM)


def call(kernel, name, outs, ins, flops=0, scratch=(), after=()):
    count = len(ins)

    def run(*refs):
        kernel(*refs[:count], *refs[count + len(after) :])

    size = sum(2 * math.prod(a.shape) for a in (*ins, *outs)) if flops >= 0 else 0
    return pl.pallas_call(
        run,
        out_shape=outs,
        in_specs=[SMEM if a.ndim == 1 else VMEM for a in ins]
        + [pl.BlockSpec(memory_space=pl.ANY)] * len(after),
        out_specs=[VMEM] * len(outs),
        scratch_shapes=scratch,
        compiler_params=pltpu.CompilerParams(vmem_limit_bytes=LIMIT),
        cost_estimate=cost(max(flops, 0), size),
        name=name,
    )(*ins, *after)


def near(*shape, dtype=bf16):
    return pltpu.VMEM(shape, dtype)


def xor_permute(values, axis, size, bit):
    return lax.ppermute(values, axis, [(i, i ^ bit) for i in range(size)])


def pick(chosen, values):
    return lax.dot_general(chosen, values, (((0,), (0,)), ((), ())), preferred_element_type=f32)


def rows_kernel(visible_ref, keep_ref, patches_ref, tail_ref, rows_ref, normed_ref):
    patch_count = patches_ref.shape[0]
    visible = visible_ref[0]
    square = (patch_count, patch_count)
    patch = lax.broadcasted_iota(jnp.int32, square, 0)
    slot = lax.broadcasted_iota(jnp.int32, square, 1)
    own = ((keep_ref[...] == patch) & (slot < visible)).astype(f32).astype(bf16)[:, :SHARE]
    other = (slot - visible == patch).astype(f32).astype(bf16)[: VMAX - SHARE, :SHARE]
    rows = pick(own, patches_ref[...]) + pick(other, tail_ref[...])
    rows_ref[...] = rows.astype(bf16)
    normed_ref[...] = layer_norm(rows).astype(bf16)


def run_copies(moves, sems):
    copies = [pltpu.make_async_copy(x, y, sems.at[i]) for i, (x, y) in enumerate(moves)]
    for copy in copies:
        copy.start()
    for copy in copies:
        copy.wait()


def part_kernel(embed_ref, qkv_ref, out_ref, pred_ref, part_ref, sems):
    j = lax.axis_index("dp")
    count, wide = part_ref.shape[0], qkv_ref.shape[1]
    fold = embed_ref.shape[0] // qkv_ref.shape[0]
    own = pl.ds(pl.multiple_of(j * count, 16), count)
    start = fold * DD
    moves = []
    for i in range(fold):
        rows = pl.ds(pl.multiple_of((j * fold + i) * count, 16), count)
        moves.append((embed_ref.at[rows, :], part_ref.at[:, i * DD : (i + 1) * DD]))
    moves.append((qkv_ref.at[own, :], part_ref.at[:, start : start + wide]))
    start += wide
    moves.append((out_ref.at[own, :], part_ref.at[:, start : start + DD]))
    moves.append((pred_ref.at[pred_rows(j, count), :], part_ref.at[:, start + DD :]))
    run_copies(moves, sems)


def pred_rows(owner, count):
    return pl.ds(pl.multiple_of(jnp.minimum(owner, PIX // count - 1) * count, 16), count)


def tail_kernel(keep_in, patches_ref, keep_ref, rows_ref, tail_ref, sems):
    run_copies([(patches_ref.at[0], rows_ref), (keep_in, keep_ref)], sems)
    patch_count = rows_ref.shape[0]
    patch = lax.broadcasted_iota(jnp.int32, (patch_count, patch_count), 0)
    chosen = (keep_ref[...] == patch).astype(f32).astype(bf16)[:, SHARE:VMAX]
    tail_ref[...] = pick(chosen, rows_ref[...]).astype(bf16)


def call_on_hbm(kernel, name, outs, ins, scratch, after=()):
    def run(*refs):
        kernel(*refs[: len(ins)], *refs[len(ins) + len(after) :])

    return pl.pallas_call(
        run,
        out_shape=outs,
        in_specs=[HBM] * len(ins) + [pl.BlockSpec(memory_space=pl.ANY)] * len(after),
        out_specs=[VMEM] * len(outs),
        scratch_shapes=scratch,
        compiler_params=pltpu.CompilerParams(vmem_limit_bytes=LIMIT),
        cost_estimate=cost(LONG if after else 0, 2 * max(a.size for a in ins)),
        name=name,
    )(*[stay(a) for a in ins], *after)


def relay_kernel(in_ref, out_ref):
    out_ref[...] = in_ref[...]


def relay(name, values, flops=0, after=()):
    return call(relay_kernel, name, [near(*values.shape)], (values,), flops, after=after)[0]


def hold(name, after):
    return call(hold_kernel, name, [near(16, LANES)], (), LONG, after=after)[0]


def hold_kernel(out_ref):
    out_ref[...] = jnp.zeros(out_ref.shape, bf16)


def split_kernel(*refs):
    parts, (embed_ref, rest_ref) = refs[:-2], refs[-2:]
    count, wide = parts[0].shape[0], rest_ref.shape[1]
    fold = (parts[0].shape[1] - wide) // DD
    for k, part in enumerate(parts):
        for i in range(fold):
            place = (k * fold + i) * count
            embed_ref[place : place + count, :] = part[:, i * DD : (i + 1) * DD]
        rest_ref[k * count : (k + 1) * count, :] = part[:, fold * DD :]


def join_kernel(*refs):
    parts, out_ref = refs[:-1], refs[-1]
    count = parts[0].shape[0]
    for i, part in enumerate(parts):
        out_ref[i * count : (i + 1) * count, :] = part[...]


def join(name, parts, flops=0, after=()):
    rows, columns = parts[0].shape
    return call(join_kernel, name, [near(len(parts) * rows, columns)], parts, flops, after=after)[0]


PLANE = (0, 2, 4, 6)


def by_core(values, even, odd, size):
    return lax.ppermute(values, "dp", [(i, i ^ (odd if i & 1 else even)) for i in range(size)])


def plane_gather(name, own, size, after=()):
    (pair,) = call(
        join_kernel, f"pair_{name}", [near(2 * own.shape[0], own.shape[1])], (own, by_core(own, 2, 4, size)), after=after
    )
    other = xor_permute(pair, "dp", size, 1)
    return pair, other, by_core(other, 2, 4, size)


def direct_owners(j):
    return *[(j ^ i,) for i in PLANE], [j ^ i ^ 1 for i in PLANE]


def gathered_owners(j):
    side = 2 + 2 * (j & 1)
    return (j, j ^ side), (j ^ 1, j ^ 7 ^ side), (j ^ 1 ^ side, j ^ 7), (j ^ 6 ^ side, j ^ 6)


def assemble(refs, owners, own_rows, mp, piece, write):
    m = lax.axis_index("mp")
    write(pl.multiple_of(m * own_rows, 16), own_rows, None, 0, m, None)
    count = (mp - 1) * piece
    for source, devices in zip(refs, owners(lax.axis_index("dp"))):
        for block, owner in enumerate(devices):
            for k in range(1, mp):
                row = (m ^ k) * own_rows + owner * piece
                first = block * count + (k - 1) * piece
                write(pl.multiple_of(row, 16), piece, source, first, m ^ k, owner)


def embed_kernel(mp, piece, own_ref, *rest):
    refs, full = rest[:-1], rest[-1]

    def write(row, count, source, base, shard, owner):
        if source is None:
            full[pl.ds(row, count), :] = own_ref[...]
        else:
            full[pl.ds(row, count), :] = source[base : base + count, :]

    assemble(refs, direct_owners, own_ref.shape[0], mp, piece, write)


def decoder_weights_kernel(mp, piece, qkv_ref, out_ref, pred_ref, *rest):
    refs, (full_qkv, full_out, full_pred) = rest[:-3], rest[-3:]
    wide = full_qkv.shape[1]
    columns = pred_ref.shape[1]
    shard_columns = lambda shard: pl.ds(pl.multiple_of(shard * columns, LANES), columns)

    def write(row, count, source, base, shard, owner):
        place = pl.ds(row, count)
        if source is None:
            full_qkv[place, :] = qkv_ref[...]
            full_out[place, :] = out_ref[...]
            full_pred[:, shard_columns(shard)] = pred_ref[...]
        else:
            part = pl.ds(base, count)
            full_qkv[place, :] = source[part, :wide]
            full_out[place, :] = source[part, wide : wide + DD]
            pred = source[part, wide + DD :]
            full_pred[pred_rows(owner, count), shard_columns(shard)] = pred

    assemble(refs, gathered_owners, qkv_ref.shape[0], mp, piece, write)


def encode_kernel(own, up_ref, down_ref, *rest):
    blocks, partial_ref = rest[own:-1], rest[-1]
    rows = jnp.concatenate([r[...] for r in blocks], axis=0)
    hidden = up_ref.shape[1]
    tile = 256 if hidden % 256 == 0 else hidden
    total = None
    for i in range(0, hidden, tile):
        units = jax.nn.gelu(dot(rows, up_ref[:, i : i + tile]), approximate=True).astype(bf16)
        term = dot(units, down_ref[i : i + tile, :])
        total = term if total is None else total + term
    if own:
        partial_ref[:SHARE, :] = (rest[0][...].astype(f32) + total[:SHARE]).astype(bf16)
        if total.shape[0] > SHARE:
            partial_ref[SHARE:, :] = total[SHARE:].astype(bf16)
    else:
        partial_ref[...] = total.astype(bf16)


def encode(name, up, down, blocks, rows=None, flops=0, after=()):
    own = () if rows is None else (rows,)
    return call(
        functools.partial(encode_kernel, len(own)),
        name,
        [near(len(blocks) * SHARE, up.shape[0])],
        (up, down, *own, *blocks),
        flops,
        after=after,
    )[0]


def embed_rows_kernel(embed_ref, *refs):
    partials = [ref for ref in refs if ref.shape[1] == embed_ref.shape[0]]
    outs = refs[len(partials) :]
    rows = jnp.concatenate([p[...] for p in partials], axis=0)
    embedded = dot(rows, embed_ref[...]).astype(bf16)
    blocks = [embedded[i : i + SHARE] for i in range(0, rows.shape[0], SHARE)]
    if len(partials) == 3:
        blocks = [blocks[0], blocks[2], blocks[1], blocks[3]]
    for out, block in zip(outs, blocks):
        out[...] = block


def sum_kernel(*refs):
    parts, (sums_ref, tail_ref) = refs[:-2], refs[-2:]
    total = parts[0][...].astype(f32)
    for part in parts[1:]:
        total += part[...].astype(f32)
    sums_ref[...] = total.astype(bf16)
    tail_ref[...] = total[SMALLEST:, :].astype(bf16)


def decode_kernel(
    visible_ref,
    keep_ref,
    targets_ref,
    mask_ref,
    position_ref,
    qkv_ref,
    out_ref,
    pred_ref,
    sums_ref,
    tail_ref,
    recon_ref,
    loss_ref,
    flat,
    errors,
):
    patch_count = position_ref.shape[0]
    patch = lax.broadcasted_iota(jnp.int32, (patch_count, patch_count), 0)
    slot = lax.broadcasted_iota(jnp.int32, (patch_count, patch_count), 1)
    chosen = ((keep_ref[...] == patch) & (slot < visible_ref[0])).astype(f32)
    seen = jnp.max(chosen, axis=1, keepdims=True)
    slots = chosen.astype(bf16)[:, :SHARE]
    late = jnp.where(slot >= SHARE, chosen, 0.0)
    shift = patch_count + VMAX - SHARE - jnp.maximum(visible_ref[0], SHARE)
    moved = pltpu.roll(late, shift, 1)
    picked = dot(slots, sums_ref[...]) + dot(moved.astype(bf16)[:, : VMAX - SHARE], tail_ref[...])
    start = jnp.where(seen > 0, picked, mask_ref[...].astype(f32)) + position_ref[...].astype(f32)
    projections = dot(layer_norm(start).astype(bf16), qkv_ref[...]).astype(bf16)
    scale = 1.0 / math.sqrt(HSIZE)
    pair = LANES // HSIZE
    column = lax.broadcasted_iota(jnp.int32, (patch_count, LANES), 1) // HSIZE
    masks = [((column == i).astype(f32) * scale).astype(bf16) for i in range(pair)]
    values = projections[:, 2 * DD :].astype(f32).T.astype(bf16)
    mixed = []
    for first in range(0, DD, LANES):
        query = projections[:, first : first + LANES]
        query = jnp.concatenate([query * mask for mask in masks], axis=0)
        key = projections[:, DD + first : DD + first + LANES]
        scores = lax.dot_general(
            key, query, (((1,), (1,)), ((), ())), preferred_element_type=f32
        )
        weights = jnp.exp(scores - jnp.max(scores, axis=0, keepdims=True))
        total = 1.0 / jnp.sum(weights, axis=0, keepdims=True)
        weights = weights.astype(bf16)
        for i in range(pair):
            head = slice(first + i * HSIZE, first + (i + 1) * HSIZE)
            mine = slice(i * patch_count, (i + 1) * patch_count)
            mixed.append(dot(values[head, :], weights[:, mine]) * total[:, mine])
    mixed = jnp.concatenate(mixed, axis=0).astype(bf16)
    after = start + lax.dot_general(mixed, out_ref[...], (((0,), (0,)), ((), ())), preferred_element_type=f32)
    prediction = lax.dot_general(
        layer_norm(after).astype(bf16), pred_ref[...], (((1,), (1,)), ((), ())), preferred_element_type=f32
    )
    group = 4
    wide = group * PIX
    flat[:, :PIX] = prediction[:, :PIX]
    lines = patch_count // group
    together = jnp.concatenate(
        [flat[pl.ds(i, lines, stride=group), :][:, :PIX] for i in range(group)], axis=1
    )
    for line in range(lines):
        place = slice(line * wide, (line + 1) * wide)
        recon_ref[:, place] = together[line : line + 1, :].astype(bf16)
        errors[line : line + 1, :] = together[line : line + 1, :] - targets_ref[:, place].astype(f32)
    squares = errors[...] * errors[...]
    for i in range(group):
        flat[pl.ds(i, lines, stride=group), :PIX] = squares[:, i * PIX : (i + 1) * PIX]
    loss = jnp.sum(flat[:, :PIX], axis=1, keepdims=True) * (1.0 / PIX)
    loss = jnp.where(seen > 0, 0.0, loss)
    loss_ref[...] = jnp.sum(jnp.where(patch == slot, loss, 0.0), axis=0, keepdims=True)


def body(
    dp,
    mp,
    patches,
    keep_index,
    visible,
    targets,
    w_up,
    w_down,
    dec_embed,
    dec_qkv,
    dec_out,
    dec_pred,
    mask_token,
    position,
):
    _, patch_count, width = patches.shape
    fold, piece = dec_embed.shape[0] // dec_qkv.shape[0], dec_qkv.shape[0] // dp
    in_pieces = (dp, mp) == (8, 4) and piece % 16 == 0
    pred_columns = dec_pred.T
    over_mp = lambda a, k: xor_permute(a, "mp", mp, k)
    over_dp = lambda a, bit: xor_permute(a, "dp", dp, bit)
    wide = DD + dec_qkv.shape[1] + LANES
    shards = (dec_embed, dec_qkv, dec_out, pred_columns)
    part = []
    if in_pieces:
        part = call_on_hbm(
            part_kernel,
            "part",
            [near(piece, fold * DD + wide)],
            shards,
            [pltpu.SemaphoreType.DMA((fold + 3,))],
        )
    keep_index, patches, tail = call_on_hbm(
        tail_kernel,
        "tail",
        [
            near(*keep_index.shape, dtype=jnp.int32),
            near(patch_count, width),
            near(VMAX - SHARE, width),
        ],
        (keep_index, patches),
        [pltpu.SemaphoreType.DMA((2,))],
        part,
    )
    fence = ()
    if in_pieces:
        far = over_mp(part[0], 2)
        parts = [over_mp(part[0], 1), far]
    tail = over_dp(tail, dp // 2)
    if in_pieces:
        passed = relay("pass_part", far, after=(parts[0],))
        parts.append(over_mp(passed, 1))
        fence = (passed, w_up, w_down)
    rows, normed = call(
        rows_kernel,
        "select_rows",
        [near(SHARE, width)] * 2,
        (visible, keep_index, patches, tail),
        LONG,
        after=fence,
    )
    if in_pieces:
        partials = [encode("encode_own", w_up, w_down, (normed,), rows, 5 * 10**9, (passed,))]
        embed, rest = call(
            split_kernel,
            "split",
            [near((mp - 1) * fold * piece, DD), near((mp - 1) * piece, wide)],
            parts,
            after=partials,
        )
        embeds = [embed] + [over_dp(embed, bit) for bit in PLANE[1:]]
        passed = relay("pass_rows", over_mp(normed, 2), LONG, (w_up, w_down, embed))
        others = [over_mp(relay("own_rows", normed, after=(passed,)), 1), passed, over_mp(passed, 1)]
        partials.append(encode("encode_near", w_up, w_down, others[1:2], flops=-1))
        partials.append(encode("encode", w_up, w_down, (others[0], others[2]), flops=LONG))
        rests = plane_gather("rest", rest, dp, partials[:1])
    else:
        full_embed, *weights = [
            lax.all_gather(w, "mp", axis=0, tiled=True) for w in (dec_embed, dec_qkv, dec_out, dec_pred)
        ]
        weights[2] = weights[2].T
        others = [over_mp(normed, k) for k in range(1, mp)]
        partials = [encode("encode", w_up, w_down, (normed, *others), rows)]
    if in_pieces:
        embeds.append(over_dp(join("join_embed", embeds), 1))
        (full_embed,) = call(
            functools.partial(embed_kernel, mp, fold * piece),
            "full_embed",
            [near(mp * dec_embed.shape[0], DD)],
            (shards[0], *embeds),
        )
    out, *sent = call(
        embed_rows_kernel,
        "embed_rows",
        [near(SHARE, DD)] * mp,
        (full_embed, *partials),
        flops=LONG,
    )
    back = [over_mp(sent[k - 1], k) for k in ((2, 3, 1) if mp == 4 else range(1, mp))]
    sums, own_tail = call(
        sum_kernel, "add_up", [near(SHARE, DD), near(SHARE - SMALLEST, DD)], (out, *back)
    )
    if in_pieces:
        rests = (*rests, over_dp(relay("pass_rest", rests[2], after=(sums,)), 1))
        weights = call(
            functools.partial(decoder_weights_kernel, mp, piece),
            "decoder_weights",
            [near(mp * w.shape[0], w.shape[1]) for w in (dec_qkv, dec_out)]
            + [near(PIX, mp * dec_pred.shape[0])],
            (*shards[1:], *rests),
        )
    return call(
        decode_kernel,
        "decode",
        [
            jax.ShapeDtypeStruct(targets.shape, bf16),
            jax.ShapeDtypeStruct((1, patch_count), f32),
        ],
        (
            visible,
            keep_index,
            targets,
            mask_token[None],
            position,
            *weights,
            sums,
            over_dp(own_tail, dp // 2),
        ),
        flops=10 * patch_count * DD * DD,
        scratch=[pltpu.VMEM((patch_count, LANES), f32), pltpu.VMEM((patch_count // 4, 4 * PIX), f32)],
    )


def solution(mesh):
    return jax.shard_map(
        functools.partial(body, mesh.shape["dp"], mesh.shape["mp"]),
        mesh=mesh,
        in_specs=(
            P(("dp", "mp"), None, None),
            P(("dp", "mp"), None),
            P(("dp", "mp")),
            P(("dp", "mp"), None),
            P(None, "mp"),
            P("mp", None),
            P("mp", None),
            P("mp", None),
            P("mp", None),
            P("mp", None),
            P(),
            P(),
        ),
        out_specs=(P(("dp", "mp"), None), P(("dp", "mp"), None)),
        check_vma=False,
    )
```

```python
import functools
import math

import jax
import jax.numpy as jnp
from jax import lax
from jax.experimental import pallas as pl
from jax.experimental.pallas import tpu as pltpu
from jax.sharding import PartitionSpec as P

DD = 512
HSIZE = 64
PIX = 96
VMAX = 80
SHARE = 48
SMALLEST = 2 * SHARE - VMAX
LANES = 128
EPSILON = 1e-06
LIMIT = 14 << 20
LONG = 10**11

f32 = jnp.float32
bf16 = jnp.bfloat16
VMEM = pl.BlockSpec(memory_space=pltpu.VMEM)
SMEM = pl.BlockSpec(memory_space=pltpu.SMEM)
HBM = pl.BlockSpec(memory_space=pltpu.HBM)


def dot(left, right):
    return jnp.dot(left, right, preferred_element_type=f32)


def layer_norm(values):
    center = values - jnp.mean(values, axis=-1, keepdims=True)
    spread = jnp.mean(center * center, axis=-1, keepdims=True)
    return center * lax.rsqrt(spread + EPSILON)


def cost(flops, size):
    return pl.CostEstimate(flops=flops, bytes_accessed=size, transcendentals=0)


def stay(array):
    return pltpu.with_memory_space_constraint(array, pltpu.HBM)


def call(kernel, name, outs, ins, flops=0, scratch=(), after=()):
    count = len(ins)

    def run(*refs):
        kernel(*refs[:count], *refs[count + len(after) :])

    size = sum(2 * math.prod(a.shape) for a in (*ins, *outs)) if flops >= 0 else 0
    return pl.pallas_call(
        run,
        out_shape=outs,
        in_specs=[SMEM if a.ndim == 1 else VMEM for a in ins]
        + [pl.BlockSpec(memory_space=pl.ANY)] * len(after),
        out_specs=[VMEM] * len(outs),
        scratch_shapes=scratch,
        compiler_params=pltpu.CompilerParams(vmem_limit_bytes=LIMIT),
        cost_estimate=cost(max(flops, 0), size),
        name=name,
    )(*ins, *after)


def near(*shape, dtype=bf16):
    return pltpu.VMEM(shape, dtype)


def xor_permute(values, axis, size, bit):
    return lax.ppermute(values, axis, [(i, i ^ bit) for i in range(size)])


def pick(chosen, values):
    return lax.dot_general(chosen, values, (((0,), (0,)), ((), ())), preferred_element_type=f32)


def rows_kernel(visible_ref, keep_ref, patches_ref, tail_ref, rows_ref, normed_ref):
    patch_count = patches_ref.shape[0]
    visible = visible_ref[0]
    square = (patch_count, patch_count)
    patch = lax.broadcasted_iota(jnp.int32, square, 0)
    slot = lax.broadcasted_iota(jnp.int32, square, 1)
    own = ((keep_ref[...] == patch) & (slot < visible)).astype(f32).astype(bf16)[:, :SHARE]
    other = (slot - visible == patch).astype(f32).astype(bf16)[: VMAX - SHARE, :SHARE]
    rows = pick(own, patches_ref[...]) + pick(other, tail_ref[...])
    rows_ref[...] = rows.astype(bf16)
    normed_ref[...] = layer_norm(rows).astype(bf16)


def run_copies(moves, sems):
    copies = [pltpu.make_async_copy(x, y, sems.at[i]) for i, (x, y) in enumerate(moves)]
    for copy in copies:
        copy.start()
    for copy in copies:
        copy.wait()


def part_kernel(embed_ref, qkv_ref, out_ref, pred_ref, part_ref, sems):
    j = lax.axis_index("dp")
    count, wide = part_ref.shape[0], qkv_ref.shape[1]
    fold = embed_ref.shape[0] // qkv_ref.shape[0]
    own = pl.ds(pl.multiple_of(j * count, 16), count)
    start = fold * DD
    moves = []
    for i in range(fold):
        rows = pl.ds(pl.multiple_of((j * fold + i) * count, 16), count)
        moves.append((embed_ref.at[rows, :], part_ref.at[:, i * DD : (i + 1) * DD]))
    moves.append((qkv_ref.at[own, :], part_ref.at[:, start : start + wide]))
    start += wide
    moves.append((out_ref.at[own, :], part_ref.at[:, start : start + DD]))
    moves.append((pred_ref.at[pred_rows(j, count), :], part_ref.at[:, start + DD :]))
    run_copies(moves, sems)


def pred_rows(owner, count):
    return pl.ds(pl.multiple_of(jnp.minimum(owner, PIX // count - 1) * count, 16), count)


def tail_kernel(keep_in, patches_ref, keep_ref, rows_ref, tail_ref, sems):
    run_copies([(patches_ref.at[0], rows_ref), (keep_in, keep_ref)], sems)
    patch_count = rows_ref.shape[0]
    patch = lax.broadcasted_iota(jnp.int32, (patch_count, patch_count), 0)
    chosen = (keep_ref[...] == patch).astype(f32).astype(bf16)[:, SHARE:VMAX]
    tail_ref[...] = pick(chosen, rows_ref[...]).astype(bf16)


def call_on_hbm(kernel, name, outs, ins, scratch, after=()):
    def run(*refs):
        kernel(*refs[: len(ins)], *refs[len(ins) + len(after) :])

    return pl.pallas_call(
        run,
        out_shape=outs,
        in_specs=[HBM] * len(ins) + [pl.BlockSpec(memory_space=pl.ANY)] * len(after),
        out_specs=[VMEM] * len(outs),
        scratch_shapes=scratch,
        compiler_params=pltpu.CompilerParams(vmem_limit_bytes=LIMIT),
        cost_estimate=cost(LONG if after else 0, 2 * max(a.size for a in ins)),
        name=name,
    )(*[stay(a) for a in ins], *after)


def relay_kernel(in_ref, out_ref):
    out_ref[...] = in_ref[...]


def relay(name, values, flops=0, after=()):
    return call(relay_kernel, name, [near(*values.shape)], (values,), flops, after=after)[0]


def hold(name, after):
    return call(hold_kernel, name, [near(16, LANES)], (), LONG, after=after)[0]


def hold_kernel(out_ref):
    out_ref[...] = jnp.zeros(out_ref.shape, bf16)


def split_kernel(*refs):
    parts, (embed_ref, rest_ref) = refs[:-2], refs[-2:]
    count, wide = parts[0].shape[0], rest_ref.shape[1]
    fold = (parts[0].shape[1] - wide) // DD
    for k, part in enumerate(parts):
        for i in range(fold):
            place = (k * fold + i) * count
            embed_ref[place : place + count, :] = part[:, i * DD : (i + 1) * DD]
        rest_ref[k * count : (k + 1) * count, :] = part[:, fold * DD :]


def join_kernel(*refs):
    parts, out_ref = refs[:-1], refs[-1]
    count = parts[0].shape[0]
    for i, part in enumerate(parts):
        out_ref[i * count : (i + 1) * count, :] = part[...]


def join(name, parts, flops=0, after=()):
    rows, columns = parts[0].shape
    return call(join_kernel, name, [near(len(parts) * rows, columns)], parts, flops, after=after)[0]


PLANE = (0, 2, 4, 6)


def by_core(values, even, odd, size):
    return lax.ppermute(values, "dp", [(i, i ^ (odd if i & 1 else even)) for i in range(size)])


def plane_gather(name, own, size, after=()):
    (pair,) = call(
        join_kernel, f"pair_{name}", [near(2 * own.shape[0], own.shape[1])], (own, by_core(own, 2, 4, size)), after=after
    )
    other = xor_permute(pair, "dp", size, 1)
    return pair, other, by_core(other, 2, 4, size)


def direct_owners(j):
    return *[(j ^ i,) for i in PLANE], [j ^ i ^ 1 for i in PLANE]


def gathered_owners(j):
    side = 2 + 2 * (j & 1)
    return (j, j ^ side), (j ^ 1, j ^ 7 ^ side), (j ^ 1 ^ side, j ^ 7), (j ^ 6 ^ side, j ^ 6)


def assemble(refs, owners, own_rows, mp, piece, write):
    m = lax.axis_index("mp")
    write(pl.multiple_of(m * own_rows, 16), own_rows, None, 0, m, None)
    count = (mp - 1) * piece
    for source, devices in zip(refs, owners(lax.axis_index("dp"))):
        for block, owner in enumerate(devices):
            for k in range(1, mp):
                row = (m ^ k) * own_rows + owner * piece
                first = block * count + (k - 1) * piece
                write(pl.multiple_of(row, 16), piece, source, first, m ^ k, owner)


def embed_kernel(mp, piece, own_ref, *rest):
    refs, full = rest[:-1], rest[-1]

    def write(row, count, source, base, shard, owner):
        if source is None:
            full[pl.ds(row, count), :] = own_ref[...]
        else:
            full[pl.ds(row, count), :] = source[base : base + count, :]

    assemble(refs, direct_owners, own_ref.shape[0], mp, piece, write)


def decoder_weights_kernel(mp, piece, qkv_ref, out_ref, pred_ref, *rest):
    refs, (full_qkv, full_out, full_pred) = rest[:-3], rest[-3:]
    wide = full_qkv.shape[1]
    columns = pred_ref.shape[1]
    shard_columns = lambda shard: pl.ds(pl.multiple_of(shard * columns, LANES), columns)

    def write(row, count, source, base, shard, owner):
        place = pl.ds(row, count)
        if source is None:
            full_qkv[place, :] = qkv_ref[...]
            full_out[place, :] = out_ref[...]
            full_pred[:, shard_columns(shard)] = pred_ref[...]
        else:
            part = pl.ds(base, count)
            full_qkv[place, :] = source[part, :wide]
            full_out[place, :] = source[part, wide : wide + DD]
            pred = source[part, wide + DD :]
            full_pred[pred_rows(owner, count), shard_columns(shard)] = pred

    assemble(refs, gathered_owners, qkv_ref.shape[0], mp, piece, write)


def encode_kernel(own, up_ref, down_ref, *rest):
    blocks, partial_ref = rest[own:-1], rest[-1]
    rows = jnp.concatenate([r[...] for r in blocks], axis=0)
    hidden = up_ref.shape[1]
    tile = 256 if hidden % 256 == 0 else hidden
    total = None
    for i in range(0, hidden, tile):
        units = jax.nn.gelu(dot(rows, up_ref[:, i : i + tile]), approximate=True).astype(bf16)
        term = dot(units, down_ref[i : i + tile, :])
        total = term if total is None else total + term
    if own:
        partial_ref[:SHARE, :] = (rest[0][...].astype(f32) + total[:SHARE]).astype(bf16)
        if total.shape[0] > SHARE:
            partial_ref[SHARE:, :] = total[SHARE:].astype(bf16)
    else:
        partial_ref[...] = total.astype(bf16)


def encode(name, up, down, blocks, rows=None, flops=0, after=()):
    own = () if rows is None else (rows,)
    return call(
        functools.partial(encode_kernel, len(own)),
        name,
        [near(len(blocks) * SHARE, up.shape[0])],
        (up, down, *own, *blocks),
        flops,
        after=after,
    )[0]


def embed_rows_kernel(embed_ref, *refs):
    partials = [ref for ref in refs if ref.shape[1] == embed_ref.shape[0]]
    outs = refs[len(partials) :]
    rows = jnp.concatenate([p[...] for p in partials], axis=0)
    embedded = dot(rows, embed_ref[...]).astype(bf16)
    blocks = [embedded[i : i + SHARE] for i in range(0, rows.shape[0], SHARE)]
    if len(partials) == 3:
        blocks = [blocks[0], blocks[2], blocks[1], blocks[3]]
    for out, block in zip(outs, blocks):
        out[...] = block


def sum_kernel(*refs):
    parts, (sums_ref, tail_ref) = refs[:-2], refs[-2:]
    total = parts[0][...].astype(f32)
    for part in parts[1:]:
        total += part[...].astype(f32)
    sums_ref[...] = total.astype(bf16)
    tail_ref[...] = total[SMALLEST:, :].astype(bf16)


def decode_kernel(
    visible_ref,
    keep_ref,
    targets_ref,
    mask_ref,
    position_ref,
    qkv_ref,
    out_ref,
    pred_ref,
    sums_ref,
    tail_ref,
    recon_ref,
    loss_ref,
    flat,
    errors,
):
    patch_count = position_ref.shape[0]
    patch = lax.broadcasted_iota(jnp.int32, (patch_count, patch_count), 0)
    slot = lax.broadcasted_iota(jnp.int32, (patch_count, patch_count), 1)
    chosen = ((keep_ref[...] == patch) & (slot < visible_ref[0])).astype(f32)
    seen = jnp.max(chosen, axis=1, keepdims=True)
    slots = chosen.astype(bf16)[:, :SHARE]
    late = jnp.where(slot >= SHARE, chosen, 0.0)
    shift = patch_count + VMAX - SHARE - jnp.maximum(visible_ref[0], SHARE)
    moved = pltpu.roll(late, shift, 1)
    picked = dot(slots, sums_ref[...]) + dot(moved.astype(bf16)[:, : VMAX - SHARE], tail_ref[...])
    start = jnp.where(seen > 0, picked, mask_ref[...].astype(f32)) + position_ref[...].astype(f32)
    projections = dot(layer_norm(start).astype(bf16), qkv_ref[...]).astype(bf16)
    scale = 1.0 / math.sqrt(HSIZE)
    pair = LANES // HSIZE
    column = lax.broadcasted_iota(jnp.int32, (patch_count, LANES), 1) // HSIZE
    masks = [((column == i).astype(f32) * scale).astype(bf16) for i in range(pair)]
    values = projections[:, 2 * DD :].astype(f32).T.astype(bf16)
    mixed = []
    for first in range(0, DD, LANES):
        query = projections[:, first : first + LANES]
        query = jnp.concatenate([query * mask for mask in masks], axis=0)
        key = projections[:, DD + first : DD + first + LANES]
        scores = lax.dot_general(
            key, query, (((1,), (1,)), ((), ())), preferred_element_type=f32
        )
        weights = jnp.exp(scores - jnp.max(scores, axis=0, keepdims=True))
        total = 1.0 / jnp.sum(weights, axis=0, keepdims=True)
        weights = weights.astype(bf16)
        for i in range(pair):
            head = slice(first + i * HSIZE, first + (i + 1) * HSIZE)
            mine = slice(i * patch_count, (i + 1) * patch_count)
            mixed.append(dot(values[head, :], weights[:, mine]) * total[:, mine])
    mixed = jnp.concatenate(mixed, axis=0).astype(bf16)
    after = start + lax.dot_general(mixed, out_ref[...], (((0,), (0,)), ((), ())), preferred_element_type=f32)
    prediction = lax.dot_general(
        layer_norm(after).astype(bf16), pred_ref[...], (((1,), (1,)), ((), ())), preferred_element_type=f32
    )
    group = 4
    wide = group * PIX
    flat[:, :PIX] = prediction[:, :PIX]
    lines = patch_count // group
    together = jnp.concatenate(
        [flat[pl.ds(i, lines, stride=group), :][:, :PIX] for i in range(group)], axis=1
    )
    for line in range(lines):
        place = slice(line * wide, (line + 1) * wide)
        recon_ref[:, place] = together[line : line + 1, :].astype(bf16)
        errors[line : line + 1, :] = together[line : line + 1, :] - targets_ref[:, place].astype(f32)
    squares = errors[...] * errors[...]
    for i in range(group):
        flat[pl.ds(i, lines, stride=group), :PIX] = squares[:, i * PIX : (i + 1) * PIX]
    loss = jnp.sum(flat[:, :PIX], axis=1, keepdims=True) * (1.0 / PIX)
    loss = jnp.where(seen > 0, 0.0, loss)
    loss_ref[...] = jnp.sum(jnp.where(patch == slot, loss, 0.0), axis=0, keepdims=True)


def body(
    dp,
    mp,
    patches,
    keep_index,
    visible,
    targets,
    w_up,
    w_down,
    dec_embed,
    dec_qkv,
    dec_out,
    dec_pred,
    mask_token,
    position,
):
    _, patch_count, width = patches.shape
    fold, piece = dec_embed.shape[0] // dec_qkv.shape[0], dec_qkv.shape[0] // dp
    in_pieces = (dp, mp) == (8, 4) and piece % 16 == 0
    pred_columns = dec_pred.T
    over_mp = lambda a, k: xor_permute(a, "mp", mp, k)
    over_dp = lambda a, bit: xor_permute(a, "dp", dp, bit)
    wide = DD + dec_qkv.shape[1] + LANES
    shards = (dec_embed, dec_qkv, dec_out, pred_columns)
    part = []
    if in_pieces:
        part = call_on_hbm(
            part_kernel,
            "part",
            [near(piece, fold * DD + wide)],
            shards,
            [pltpu.SemaphoreType.DMA((fold + 3,))],
        )
    keep_index, patches, tail = call_on_hbm(
        tail_kernel,
        "tail",
        [
            near(*keep_index.shape, dtype=jnp.int32),
            near(patch_count, width),
            near(VMAX - SHARE, width),
        ],
        (keep_index, patches),
        [pltpu.SemaphoreType.DMA((2,))],
        part,
    )
    fence = ()
    if in_pieces:
        far = over_mp(part[0], 2)
        parts = [over_mp(part[0], 1), far]
    tail = over_dp(tail, dp // 2)
    if in_pieces:
        passed = relay("pass_part", far, after=(parts[0],))
        parts.append(over_mp(passed, 1))
        fence = (passed, w_up, w_down)
    rows, normed = call(
        rows_kernel,
        "select_rows",
        [near(SHARE, width)] * 2,
        (visible, keep_index, patches, tail),
        LONG,
        after=fence,
    )
    if in_pieces:
        partials = [encode("encode_own", w_up, w_down, (normed,), rows, 5 * 10**9, (passed,))]
        embed, rest = call(
            split_kernel,
            "split",
            [near((mp - 1) * fold * piece, DD), near((mp - 1) * piece, wide)],
            parts,
            after=partials,
        )
        embeds = [embed] + [over_dp(embed, bit) for bit in PLANE[1:]]
        passed = relay("pass_rows", over_mp(normed, 2), LONG, (embed,))
        others = [over_mp(relay("own_rows", normed, after=(embed,)), 1), passed, over_mp(passed, 1)]
        partials.append(encode("encode_near", w_up, w_down, others[1:2], flops=-1))
        partials.append(encode("encode", w_up, w_down, (others[0], others[2]), flops=LONG))
        rests = plane_gather("rest", rest, dp, partials[:1])
    else:
        full_embed, *weights = [
            lax.all_gather(w, "mp", axis=0, tiled=True) for w in (dec_embed, dec_qkv, dec_out, dec_pred)
        ]
        weights[2] = weights[2].T
        others = [over_mp(normed, k) for k in range(1, mp)]
        partials = [encode("encode", w_up, w_down, (normed, *others), rows)]
    if in_pieces:
        embeds.append(over_dp(join("join_embed", embeds), 1))
        (full_embed,) = call(
            functools.partial(embed_kernel, mp, fold * piece),
            "full_embed",
            [near(mp * dec_embed.shape[0], DD)],
            (shards[0], *embeds),
        )
    out, *sent = call(
        embed_rows_kernel,
        "embed_rows",
        [near(SHARE, DD)] * mp,
        (full_embed, *partials),
        flops=LONG,
    )
    back = [over_mp(sent[k - 1], k) for k in ((2, 3, 1) if mp == 4 else range(1, mp))]
    sums, own_tail = call(
        sum_kernel, "add_up", [near(SHARE, DD), near(SHARE - SMALLEST, DD)], (out, *back)
    )
    if in_pieces:
        rests = (*rests, over_dp(relay("pass_rest", rests[2], after=(sums,)), 1))
        weights = call(
            functools.partial(decoder_weights_kernel, mp, piece),
            "decoder_weights",
            [near(mp * w.shape[0], w.shape[1]) for w in (dec_qkv, dec_out)]
            + [near(PIX, mp * dec_pred.shape[0])],
            (*shards[1:], *rests),
        )
    return call(
        decode_kernel,
        "decode",
        [
            jax.ShapeDtypeStruct(targets.shape, bf16),
            jax.ShapeDtypeStruct((1, patch_count), f32),
        ],
        (
            visible,
            keep_index,
            targets,
            mask_token[None],
            position,
            *weights,
            sums,
            over_dp(own_tail, dp // 2),
        ),
        flops=10 * patch_count * DD * DD,
        scratch=[pltpu.VMEM((patch_count, LANES), f32), pltpu.VMEM((patch_count // 4, 4 * PIX), f32)],
    )


def solution(mesh):
    return jax.shard_map(
        functools.partial(body, mesh.shape["dp"], mesh.shape["mp"]),
        mesh=mesh,
        in_specs=(
            P(("dp", "mp"), None, None),
            P(("dp", "mp"), None),
            P(("dp", "mp")),
            P(("dp", "mp"), None),
            P(None, "mp"),
            P("mp", None),
            P("mp", None),
            P("mp", None),
            P("mp", None),
            P("mp", None),
            P(),
            P(),
        ),
        out_specs=(P(("dp", "mp"), None), P(("dp", "mp"), None)),
        check_vma=False,
    )
```
